32 devices in a mesh: groups: 2 (over x), slab: 16 (over z, y, core).
Axes of the slice: x: 2, y: 2, z: 4, core: 2. Of those that a mesh axis runs over, the one named last changes fastest.
Arguments:
- mean_volume: bfloat16 [131072, 256], P(('groups', 'slab')), parts along dimension 0, may hold values from -12 to 12
- components: bfloat16 [6, 131072, 256], P(None, ('groups', 'slab')), parts along dimension 1, may hold values from -12 to 12
- images: bfloat16 [128, 256, 256], P(('groups', 'slab')), parts along dimension 0, may hold values from -24 to 24
- tilt: int32 [128], P(('groups', 'slab')), parts along dimension 0, may hold values from -127 to 127, as said below
- shift: int32 [128], P(('groups', 'slab')), parts along dimension 0, may hold values from 0 to 127
- frac: int32 [128], P(('groups', 'slab')), parts along dimension 0, may hold values from 0 to 15
- noise_var: float32 [128], P(('groups', 'slab')), parts along dimension 0, may hold values from 0.1 to 1
Outputs:
- new_components: bfloat16 [6, 131072, 256], P(None, ('groups', 'slab')), parts along dimension 1
- latents: float32 [128, 6], P(('groups', 'slab')), parts along dimension 0
The draws below stay inside these ranges and needn't reach their ends.
There are 2 independent parts, one for each index of `groups`. The reference program is written for one: setup_inputs(seed, part) draws one part's arguments, and reference() takes and returns one part's arrays. A program takes and returns all parts, laid end to end along the dimension named above; each array names one. Nothing has to cross between parts.
Inputs may be any that keep to these rules, and one draw needn't show every extreme that they name: The magnitude of tilt is 64 or more, and exactly 64 for every image whose index is a multiple of 4; hence at most 32 pixel rows of one image have their plane among one slab device's planes, and some image reaches that.
All inputs are finite; a program needn't handle non-finite values.
Results may differ from the reference program's by a relative error of at most 0.0076.
Values may be sent and summed in bfloat16 or wider, within the bound.
No kernel may reach another device: no remote copies, remote signals or barrier semaphores. Data moves between devices by JAX's collectives and lax.ppermute only.
A program may use at most 192 MiB of HBM per device.

```python
import math
import jax
import jax.numpy as jnp
from jax import lax

GRID = 256
COMPS = 6
TILE = 128
IMAGES = 64


def tilt_values(key):
    size_key, sign_key = jax.random.split(jax.random.fold_in(key, 71))
    magnitude = jax.random.randint(size_key, (IMAGES,), GRID // 4, GRID // 2, dtype=jnp.int32)
    image_index = jnp.arange(IMAGES, dtype=jnp.int32)
    magnitude = jnp.where(image_index % 4 == 0, GRID // 4, magnitude)
    sign_value = jax.random.randint(sign_key, (IMAGES,), 0, 2, dtype=jnp.int32) * 2 - 1
    return magnitude * sign_value


def shift_values(key):
    return jax.random.randint(jax.random.fold_in(key, 72), (IMAGES,), 0, TILE, dtype=jnp.int32)


def frac_values(key):
    return jax.random.randint(jax.random.fold_in(key, 73), (IMAGES,), 0, 16, dtype=jnp.int32)


def volume_values(key, shape, constant, spread):
    noise_key, scale_key = jax.random.split(jax.random.fold_in(key, constant))
    values = jax.random.normal(noise_key, shape, jnp.float32)
    scales = jnp.exp(jax.random.uniform(scale_key, shape[:-1] + (1,), jnp.float32, -1.0, 1.0) * jnp.log(spread))
    return jnp.clip(values * scales, -12.0, 12.0)


def tile_index_drawn(offset):
    cells = jnp.arange(GRID, dtype=jnp.int32)
    inside = cells % TILE
    return cells - inside + (inside + offset) % TILE


def draw_mean_volume(key, part):
    spread = 1.0
    return volume_values(key, (GRID * GRID, GRID), 74, spread).astype(jnp.bfloat16)


def draw_components(key, part):
    spread = 1.0
    return volume_values(key, (COMPS, GRID * GRID, GRID), 75, spread).astype(jnp.bfloat16)


def draw_tilt(key, part):
    return tilt_values(key)


def draw_shift(key, part):
    return shift_values(key)


def draw_frac(key, part):
    return frac_values(key)


def draw_images(key, part):
    spread = 1.0
    mean_part = volume_values(key, (GRID * GRID, GRID), 74, spread)
    comp_part = volume_values(key, (COMPS, GRID * GRID, GRID), 75, spread)
    volume = jnp.concatenate([mean_part[None], comp_part], axis=0).astype(jnp.bfloat16).astype(jnp.float32)
    volume = jnp.concatenate([volume, jnp.zeros((COMPS + 1, GRID, GRID), jnp.float32)], axis=1)
    tilt = tilt_values(key)
    shift = shift_values(key)
    frac = frac_values(key)
    own_key = jax.random.fold_in(key, 76)
    latent_key, noise_key = jax.random.split(own_key)
    truth = jax.random.normal(latent_key, (IMAGES, COMPS), jnp.float32)
    noise = jnp.clip(jax.random.normal(noise_key, (IMAGES, GRID, GRID), jnp.float32), -6.0, 6.0)
    half = GRID // 2
    position = jnp.arange(GRID, dtype=jnp.int32)

    def one_image(pieces):
        tilt_value, shift_value, frac_value, truth_row = pieces
        numerator = (position - half) * tilt_value
        whole_part = jnp.floor_divide(numerator, half)
        plane = half + whole_part
        depth = (numerator - whole_part * half).astype(jnp.float32) / half
        lower = plane * GRID + position
        blended = (1.0 - depth)[None, :, None] * jnp.take(volume, lower, axis=1) + depth[None, :, None] * jnp.take(volume, lower + GRID, axis=1)
        weight = frac_value.astype(jnp.float32) / 16.0
        slices = (1.0 - weight) * jnp.take(blended, tile_index_drawn(shift_value), axis=-1) + weight * jnp.take(blended, tile_index_drawn(shift_value + 1), axis=-1)
        mixture = slices[0]
        for comp_at in range(COMPS):
            mixture = mixture + truth_row[comp_at] * slices[comp_at + 1]
        return mixture
    clean = lax.map(one_image, (tilt, shift, frac, truth))
    return jnp.clip(clean + noise, -24.0, 24.0).astype(jnp.bfloat16)


def levels(key, shape, cuts, smallest, top_value):
    gain, own = 1.0, jax.random.fold_in(key, 6)
    for axis_at, shards_of in cuts:
        draws = jnp.exp(jax.random.uniform(jax.random.fold_in(own, axis_at), (shards_of,), jnp.float32, smallest / len(cuts), top_value / len(cuts)))
        gain = gain * jnp.repeat(draws, shape[axis_at] // shards_of).reshape([-1 if axis == axis_at else 1 for axis in range(len(shape))])
    return gain


def setup_inputs(seed: int = 0, part: int = 0) -> dict:
    splits = jax.random.split(jax.random.key(seed), 8)
    part_splits = jax.random.split(jax.random.fold_in(splits[7], part), 8)
    mean_volume = draw_mean_volume(jax.random.fold_in(jax.random.fold_in(splits[7], part), 71), part)
    components = draw_components(jax.random.fold_in(jax.random.fold_in(splits[7], part), 71), part)
    images = draw_images(jax.random.fold_in(jax.random.fold_in(splits[7], part), 71), part)
    tilt = draw_tilt(jax.random.fold_in(jax.random.fold_in(splits[7], part), 71), part)
    shift = draw_shift(jax.random.fold_in(jax.random.fold_in(splits[7], part), 71), part)
    frac = draw_frac(jax.random.fold_in(jax.random.fold_in(splits[7], part), 71), part)
    noise_var = jnp.clip(jnp.exp(math.log(1.0) - 2.3025851 * jax.random.uniform(part_splits[6], (IMAGES,), jnp.float32) ** levels(part_splits[6], (IMAGES,), ((0, 16),), -0.2, 0.2)), 0.1, 1.0)
    return {"mean_volume": mean_volume, "components": components, "images": images, "tilt": tilt, "shift": shift, "frac": frac, "noise_var": noise_var}


def solve_small(matrix, right_side):
    factor = jnp.linalg.cholesky(matrix)
    order = matrix.shape[-1]
    forward = []
    for row_at in range(order):
        total = right_side[..., row_at]
        for col_at in range(row_at):
            total = total - factor[..., row_at, col_at] * forward[col_at]
        forward.append(total / factor[..., row_at, row_at])
    backward = [None] * order
    for row_at in reversed(range(order)):
        total = forward[row_at]
        for col_at in range(row_at + 1, order):
            total = total - factor[..., col_at, row_at] * backward[col_at]
        backward[row_at] = total / factor[..., row_at, row_at]
    return jnp.stack(backward, axis=-1)

def geometry(tilt_value):
    half = GRID // 2
    position = jnp.arange(GRID, dtype=jnp.int32)
    numerator = (position - half) * tilt_value
    whole_part = jnp.floor_divide(numerator, half)
    return (half + whole_part, (numerator - whole_part * half).astype(jnp.float32) / half)

def tile_index(offset):
    cells = jnp.arange(GRID, dtype=jnp.int32)
    inside = cells % TILE
    return (cells - inside + (inside + offset) % TILE).astype(jnp.int32)

def along_x(rows, shift_value, frac_value):
    weight = frac_value.astype(jnp.float32) / 16.0
    return (1.0 - weight) * jnp.take(rows, tile_index(shift_value), axis=-1) + weight * jnp.take(rows, tile_index(shift_value + 1), axis=-1)

def back_x(rows, shift_value, frac_value):
    weight = frac_value.astype(jnp.float32) / 16.0
    return (1.0 - weight) * jnp.take(rows, tile_index(-shift_value), axis=-1) + weight * jnp.take(rows, tile_index(-shift_value - 1), axis=-1)

def reference(mean_volume, components, images, tilt, shift, frac, noise_var):
    count = GRID * GRID
    position = jnp.arange(GRID, dtype=jnp.int32)
    volume = jnp.concatenate([mean_volume[None], components], axis=0)
    volume = jnp.concatenate([volume, jnp.zeros((COMPS + 1, GRID, GRID), volume.dtype)], axis=1)
    identity = jnp.eye(COMPS, dtype=jnp.float32)

    def one_image(carry, pieces):
        totals, weights = carry
        picture, tilt_value, shift_value, frac_value, noise_value = pieces
        plane, depth = geometry(tilt_value)
        lower = (plane * GRID + position).astype(jnp.int32)
        upper = (lower + GRID).astype(jnp.int32)
        low_rows = jnp.take(volume, lower, axis=1).astype(jnp.float32)
        high_rows = jnp.take(volume, upper, axis=1).astype(jnp.float32)
        blended = ((1.0 - depth)[None, :, None] * low_rows + depth[None, :, None] * high_rows).astype(jnp.bfloat16)
        slices = along_x(blended.astype(jnp.float32), shift_value, frac_value).astype(jnp.bfloat16)
        slices = slices.reshape(COMPS + 1, count)
        flat_picture = picture.reshape(count)
        gram = jnp.dot(slices.astype(jnp.float32), slices.T.astype(jnp.float32), preferred_element_type=jnp.float32)
        project = jnp.dot(slices.astype(jnp.float32), flat_picture.astype(jnp.float32), preferred_element_type=jnp.float32)
        system = gram[1:, 1:] / count + noise_value * identity
        target = (project[1:] - gram[1:, 0]) / count
        latent = solve_small(system, target)
        latent_weight = latent.astype(jnp.bfloat16)
        coefficient = jnp.concatenate([jnp.ones((1,), jnp.bfloat16), latent_weight])
        residual = (flat_picture.astype(jnp.float32) - jnp.dot(coefficient.astype(jnp.float32), slices.astype(jnp.float32), preferred_element_type=jnp.float32)).astype(jnp.bfloat16)
        spread = back_x(residual.reshape(GRID, GRID).astype(jnp.float32), shift_value, frac_value)
        latent_float = latent_weight.astype(jnp.float32)
        low_term = latent_float[:, None, None] * ((1.0 - depth)[:, None] * spread)[None]
        high_term = latent_float[:, None, None] * (depth[:, None] * spread)[None]
        totals = totals.at[:, lower].add(low_term).at[:, upper].add(high_term)
        power = jnp.sum(latent_float * latent_float)
        weights = weights.at[lower].add((1.0 - depth) * power).at[upper].add(depth * power)
        return ((totals, weights), latent)
    start = (jnp.zeros((COMPS, count + GRID, GRID), jnp.float32), jnp.zeros((count + GRID,), jnp.float32))
    (totals, weights), latents = lax.scan(one_image, start, (images, tilt, shift, frac, noise_var))
    new_components = (totals[:, :count] / (1.0 + weights[:count])[None, :, None]).astype(jnp.bfloat16)
    return (new_components, latents)
```

```python
import functools

import jax
import jax.numpy as jnp
from jax import lax
from jax.experimental import pallas as pl
from jax.experimental.pallas import tpu as pltpu
from jax.sharding import PartitionSpec as P

GRID = 256
HALF = GRID // 2
COMPS = 6
CHANS = COMPS + 1
TILE = 128
LANES = 128
PAIRS = [(k, l) for k in range(CHANS) for l in range(k, CHANS)]
PROJECT_AT = len(PAIRS)
VMEM = 56 * 1024 * 1024

f32 = jnp.float32
bf16 = jnp.bfloat16
i32 = jnp.int32


def iota(shape, dim):
    return lax.broadcasted_iota(i32, shape, dim)


def dot(a, b):
    return jnp.dot(a, b, preferred_element_type=f32)


def params():
    return pltpu.CompilerParams(vmem_limit_bytes=VMEM)


def plane_depth(position, tilt):
    numerator = (position - HALF) * tilt
    return jnp.right_shift(numerator, 7) + HALF, jnp.bitwise_and(numerator, HALF - 1)


def pack_kernel(sizes, tilt_ref, image_ref, out_ref):
    planes, slots, peers, count = sizes
    rows = count * slots + 2 * count
    lane = iota((1, count * GRID), 1)
    tilt = jnp.full((1, count * GRID), tilt_ref[0], i32)
    for image in range(1, count):
        tilt = jnp.where(lane >= image * GRID, tilt_ref[image], tilt)
    plane, _ = plane_depth(jnp.bitwise_and(lane, GRID - 1), tilt)
    main_shape = (count * slots, count * GRID)
    row, col = iota(main_shape, 0), iota(main_shape, 1)
    main_hit = (row // slots == col // GRID) & (row % slots == col % slots)
    extra_shape = (2 * count, count * GRID)
    row, col = iota(extra_shape, 0), iota(extra_shape, 1)
    extra_hit = (row // 2 == col // GRID) & (row % 2 == col % 2)
    main_plane = jnp.where(main_hit, plane, -1000)
    extra_plane = jnp.where(extra_hit, plane, -1000)
    picture = image_ref[...]
    for peer in range(peers):
        first = peer * planes
        main = jnp.where((main_plane >= first) & (main_plane < first + planes), 1.0, 0.0)
        extra = jnp.where(extra_plane == first - 1, 1.0, 0.0)
        hit = jnp.concatenate([main, extra], axis=0).astype(bf16)
        out_ref[peer] = dot(hit, picture).astype(bf16)


def slot_order(slots, blocks):
    row, col = iota((GRID, GRID), 0), iota((GRID, GRID), 1)
    return (col == (row % blocks) * slots + row // blocks).astype(f32).astype(bf16)


def table_kernel(sizes, mean_ref, comp_ref, out_ref, order_ref):
    planes, slots, blocks, chunk = sizes

    @pl.when(pl.program_id(0) == 0)
    def _():
        order_ref[...] = slot_order(slots, blocks)

    order = order_ref[...]
    for chan in range(CHANS):
        pieces = []
        for at in range(chunk):
            span = slice(at * GRID, (at + 1) * GRID)
            plane = mean_ref[span, :] if chan == 0 else comp_ref[chan - 1, span, :]
            pieces.append(dot(order, plane).reshape(slots, blocks, GRID))
        both = jnp.concatenate(pieces, axis=1).astype(bf16)
        out_ref[:, :, chan * GRID : (chan + 1) * GRID] = both


def interpolate(rows, index, weight):
    parts = []
    for at in range(GRID // TILE):
        part = rows[:, at * TILE : (at + 1) * TILE]
        mixed = (1.0 - weight) * part + weight * pltpu.roll(part, TILE - 1, 1)
        parts.append(jnp.take_along_axis(mixed, index, axis=1, mode="promise_in_bounds"))
    return parts


def extract_kernel(
    sizes, first_ref, tilt_ref, shift_ref, frac_ref, table_ref, up_ref, low_ref, mean_ref, comp_ref,
    out_ref, extra_ref, gram_ref, upper_ref, sums_ref,
):
    planes, slots, blocks, chunk, images = sizes
    step, first = pl.program_id(0), first_ref[0]
    tilt = tilt_ref[...]
    weight = frac_ref[...].astype(f32) / 16.0
    index = jnp.bitwise_and(iota((images, TILE), 1) + shift_ref[...], TILE - 1)
    upper_rows = upper_ref.shape[1]

    @pl.when(step == 0)
    def _():
        order = slot_order(slots, blocks)
        lane = iota((images, GRID), 1)
        plane, depth = plane_depth(lane, tilt)
        depth = depth.astype(f32) / HALF
        below = plane == first - 1
        parts = []
        for odd in range(2):
            hit = below & (jnp.bitwise_and(lane, 1) == odd)
            low, high = jnp.where(hit, 1.0 - depth, 0.0), jnp.where(hit, depth, 0.0)
            parts.append(jnp.concatenate([low, high], axis=1))
        mixing = jnp.concatenate(parts, axis=0).astype(bf16)
        index2 = jnp.concatenate([index, index], axis=0)
        weight2 = jnp.concatenate([weight, weight], axis=0)
        for chan in range(CHANS):
            at = slice(chan * GRID, (chan + 1) * GRID)
            upper = dot(order, up_ref[chan]).reshape(slots, blocks, GRID)
            if upper_rows > blocks:
                fill = jnp.zeros((slots, upper_rows - blocks, GRID), f32)
                upper = jnp.concatenate([upper, fill], axis=1)
            upper_ref[:, :, at] = upper.astype(bf16)
            own = mean_ref[...] if chan == 0 else comp_ref[chan - 1]
            blended = dot(mixing[:, :GRID], low_ref[chan]) + dot(mixing[:, GRID:], own)
            parts = interpolate(blended.astype(bf16).astype(f32), index2, weight2)
            extra_ref[:, at] = jnp.concatenate(parts, axis=1).astype(bf16)
        sums_ref[...] = jnp.zeros_like(sums_ref)

    lane = iota((images, planes * blocks), 1)
    block_at, plane_at = lane % blocks, lane // blocks
    lane_up = iota((images, upper_rows), 1)
    for at in range(chunk):
        slot = step * chunk + at
        plane, depth = plane_depth(block_at * slots + slot, tilt)
        plane = plane - first
        low = jnp.where(plane == plane_at, HALF - depth, 0)
        high = jnp.where((plane + 1 == plane_at) & (plane_at > 0), depth, 0)
        mixing = ((low + high).astype(f32) / HALF).astype(bf16)
        plane, depth = plane_depth(lane_up * slots + slot, tilt)
        hit = (plane - first == planes - 1) & (lane_up < blocks)
        mixing_up = (jnp.where(hit, depth, 0).astype(f32) / HALF).astype(bf16)
        for chan in range(CHANS):
            span = slice(chan * GRID, (chan + 1) * GRID)
            blended = dot(mixing, table_ref[at, :, span]) + dot(mixing_up, upper_ref[slot, :, span])
            parts = interpolate(blended.astype(bf16).astype(f32), index, weight)
            out_ref[at, :, span] = jnp.concatenate(parts, axis=1).astype(bf16)

    def accumulate(group, carry):
        rows = pl.ds(pl.multiple_of(group * 16, 16), 16)
        sums = [sums_ref[n, rows, :] for n in range(len(PAIRS))]
        for at in range(chunk):
            for tile in range(GRID // LANES):
                values = [
                    out_ref[at, rows, pl.ds(chan * GRID + tile * LANES, LANES)].astype(f32)
                    for chan in range(CHANS)
                ]
                for n, (k, l) in enumerate(PAIRS):
                    sums[n] = sums[n] + values[k] * values[l]
        for n in range(len(PAIRS)):
            sums_ref[n, rows, :] = sums[n]
        return carry

    lax.fori_loop(0, images // 16, accumulate, 0)

    @pl.when(step == pl.num_programs(0) - 1)
    def _():
        lane = iota((images, LANES), 1)
        total = jnp.zeros((images, LANES), f32)
        for n in range(len(PAIRS)):
            total = jnp.where(lane == n, jnp.sum(sums_ref[n], axis=1, keepdims=True), total)
        gram_ref[...] = total


def project_kernel(
    sizes, got_ref, slice_ref, gram_ref, rows_ref, extra_ref, total_ref, wide_ref, sums_ref
):
    slots, chunk, images, peers, count = sizes
    stride = count * slots + 2 * count
    step = pl.program_id(0)

    @pl.when(step == 0)
    def _():
        for tile in range(GRID // LANES):
            wide_ref[tile] = got_ref[:, tile * LANES : (tile + 1) * LANES].astype(f32)
        sums_ref[...] = jnp.zeros_like(sums_ref)
        for odd in range(2):
            for image in range(count):
                start = count * slots + image * 2 + odd
                at = (odd * count + image) * peers
                for tile in range(GRID // LANES):
                    part = wide_ref[tile, pl.ds(start, peers, stride=stride), :]
                    extra_ref[at : at + peers, tile * LANES : (tile + 1) * LANES] = part.astype(bf16)

    for image in range(count):
        span = slice(image * peers, (image + 1) * peers)
        sums = [sums_ref[chan, span, :] for chan in range(CHANS)]
        for at in range(chunk):
            slot = step * chunk + at
            for tile in range(GRID // LANES):
                part = wide_ref[tile, pl.ds(image * slots + slot, peers, stride=stride), :]
                rows_ref[at, span, tile * LANES : (tile + 1) * LANES] = part.astype(bf16)
                for chan in range(CHANS):
                    lanes = slice(chan * GRID + tile * LANES, chan * GRID + (tile + 1) * LANES)
                    sums[chan] = sums[chan] + part * slice_ref[at, span, lanes].astype(f32)
        for chan in range(CHANS):
            sums_ref[chan, span, :] = sums[chan]

    @pl.when(step == pl.num_programs(0) - 1)
    def _():
        lane = iota((images, LANES), 1)
        total = gram_ref[...]
        for chan in range(CHANS):
            value = jnp.sum(sums_ref[chan], axis=1, keepdims=True)
            total = jnp.where(lane == PROJECT_AT + chan, value, total)
        total_ref[...] = total


def solve_rows(table, noise):
    count = float(GRID * GRID)

    def gram(k, l):
        at = PAIRS.index((min(k, l), max(k, l)))
        return table[at : at + 1, :]

    factor = [[None] * COMPS for _ in range(COMPS)]
    inverse = [None] * COMPS
    for col in range(COMPS):
        for row in range(col, COMPS):
            total = gram(row + 1, col + 1) / count
            if row == col:
                total = total + noise
            for at in range(col):
                total = total - factor[row][at] * factor[col][at]
            if row == col:
                inverse[col] = 1.0 / jnp.sqrt(total)
            else:
                factor[row][col] = total * inverse[col]
    forward = []
    for row in range(COMPS):
        at = PROJECT_AT + row + 1
        total = (table[at : at + 1, :] - gram(row + 1, 0)) / count
        for col in range(row):
            total = total - factor[row][col] * forward[col]
        forward.append(total * inverse[row])
    latent = [None] * COMPS
    for row in reversed(range(COMPS)):
        total = forward[row]
        for col in range(row + 1, COMPS):
            total = total - factor[col][row] * latent[col]
        latent[row] = total * inverse[row]
    return latent


def back_kernel(
    sizes, first_ref, total_ref, noise_ref, tilt_row_ref, tilt_ref, shift_ref, frac_ref,
    slice_ref, rows_ref, slice_extra_ref, rows_extra_ref,
    out_ref, latent_ref, stack_ref, row_ref, col_ref, spill_ref, order_ref,
):
    planes, slots, blocks, chunk, images, steps, out_planes = sizes
    step, first = pl.program_id(0), first_ref[0]

    @pl.when(step == 0)
    def _():
        table = jnp.transpose(total_ref[...])
        latent = solve_rows(table, noise_ref[...])
        fill = [jnp.zeros((1, images), f32)] * (8 - COMPS)
        latent_ref[...] = jnp.concatenate(latent + fill, axis=0)
        rounded = [value.astype(bf16).astype(f32) for value in latent]
        power = rounded[0] * rounded[0]
        for value in rounded[1:]:
            power = power + value * value
        rows = jnp.concatenate(rounded + [power, fill[0]], axis=0)
        row_ref[...] = jnp.concatenate([rows, rows, rows], axis=1)
        wide = jnp.concatenate([rows, jnp.zeros((LANES - 8, images), f32)], axis=0)
        col_ref[...] = jnp.transpose(wide)
        row, col = iota((GRID, GRID), 0), iota((GRID, GRID), 1)
        order_ref[...] = (row == (col % blocks) * slots + col // blocks).astype(f32).astype(bf16)

    def spread(slices, rows, copies):
        weight = frac_ref[...].astype(f32) / 16.0
        index = jnp.bitwise_and(iota((images, TILE), 1) - shift_ref[...], TILE - 1)
        latent = col_ref[...]
        if copies > 1:
            weight = jnp.concatenate([weight] * copies, axis=0)
            index = jnp.concatenate([index] * copies, axis=0)
            latent = jnp.concatenate([latent] * copies, axis=0)
        residual = rows[...].astype(f32) - slices[:, :GRID].astype(f32)
        for k in range(COMPS):
            span = slice((k + 1) * GRID, (k + 2) * GRID)
            residual = residual - latent[:, k : k + 1] * slices[:, span].astype(f32)
        residual = residual.astype(bf16).astype(f32)
        parts = []
        for at in range(GRID // TILE):
            part = residual[:, at * TILE : (at + 1) * TILE]
            mixed = (1.0 - weight) * part + weight * pltpu.roll(part, 1, 1)
            parts.append(jnp.take_along_axis(mixed, index, axis=1, mode="promise_in_bounds"))
        return jnp.concatenate(parts, axis=1)

    @pl.when(step == 0)
    def _():
        value = spread(slice_extra_ref, rows_extra_ref, 2)
        plane, depth = plane_depth(iota((images, GRID), 1), tilt_ref[...])
        odd = jnp.bitwise_and(iota((images, GRID), 1), 1)
        parts = []
        for at in range(2):
            hit = (plane == first - 1) & (odd == at)
            parts.append(jnp.sum(jnp.where(hit, depth, 0).astype(f32), axis=1, keepdims=True) / HALF)
        spill_ref[...] = (jnp.concatenate(parts, axis=0) * value).astype(bf16)

    @pl.when(step < steps)
    def _():
        tilt = tilt_row_ref[...]
        shape = (planes * blocks, 3 * images)
        row, lane = iota(shape, 0), iota(shape, 1)
        plane_at, block_at = row // blocks, row % blocks
        own = lane < 2 * images
        low = lane < images
        wanted = jnp.where(low, plane_at, plane_at - 1)
        wanted = jnp.where(own & (wanted < 0), -1000, wanted)
        wanted = jnp.where(own | (wanted < 0), wanted, -1000)
        power = row_ref[COMPS : COMPS + 1, :]
        lane_slot = iota((images, LANES), 1)
        group = 2 if blocks % 16 else 1
        for start in range(0, chunk, group):
            pieces = [[] for _ in range(COMPS)]
            for at in range(start, start + group):
                slot = step * chunk + at
                value = spread(slice_ref.at[at], rows_ref.at[at], 1)
                plane, depth = plane_depth(lane_slot * slots + slot, tilt_ref[...])
                plane = plane - first
                live = (plane >= 0) & (plane < planes) & (lane_slot < blocks)
                depth = jnp.sum(jnp.where(live, depth, 0).astype(f32), axis=1, keepdims=True) / HALF
                odd = (slot % 2) * images
                spill = spill_ref[pl.ds(pl.multiple_of(odd, 16), images), :]
                right = jnp.concatenate(
                    [((1.0 - depth) * value).astype(bf16), (depth * value).astype(bf16), spill], axis=0
                )
                plane, depth = plane_depth(block_at * slots + slot, tilt)
                hit = plane - first == wanted
                part = jnp.where(low, HALF - depth, depth).astype(f32) / HALF
                weight = jnp.sum(jnp.where(hit, part * power, 0.0), axis=1, keepdims=True)
                scale = 1.0 / (1.0 + weight)
                for k in range(COMPS):
                    left = jnp.where(hit, row_ref[k : k + 1, :], 0.0).astype(bf16)
                    total = dot(left, right) * scale
                    pieces[k].append(total.reshape(planes, blocks, GRID))
            rows = pl.ds(pl.multiple_of((step * chunk + start) * blocks, 16), group * blocks)
            for k in range(COMPS):
                stack_ref[k, :, rows, :] = jnp.concatenate(pieces[k], axis=1).astype(bf16)

    @pl.when(step >= steps)
    def _():
        order = order_ref[...]
        for k in range(COMPS):
            for at in range(out_planes):
                plane = (step - steps) * out_planes + at
                out_ref[k, at * GRID : (at + 1) * GRID, :] = dot(order, stack_ref[k, plane]).astype(bf16)


def whole(shape):
    return pl.BlockSpec(shape, lambda *_: (0,) * len(shape))


def smem():
    return pl.BlockSpec(memory_space=pltpu.SMEM)


def local(mean_volume, components, images, tilt, shift, frac, noise_var):
    peers = lax.axis_size("slab")
    me = lax.axis_index("slab")
    planes = mean_volume.shape[0] // GRID
    slots = 2 * planes
    blocks = GRID // slots
    count = images.shape[0]
    total = peers * count
    width = CHANS * GRID
    chunk = max(1, 256 // total)
    steps = slots // chunk
    pack_rows = count * slots + 2 * count
    upper_rows = -(-blocks // 16) * 16
    first = (me * planes).astype(i32).reshape(1)

    packed = pl.pallas_call(
        functools.partial(pack_kernel, (planes, slots, peers, count)),
        out_shape=jax.ShapeDtypeStruct((peers, pack_rows, GRID), bf16),
        in_specs=[smem(), whole((count * GRID, GRID))],
        out_specs=whole((peers, pack_rows, GRID)),
        grid=(1,),
        compiler_params=params(),
        name="pack",
    )(tilt, images.reshape(count * GRID, GRID))
    got = lax.all_to_all(packed, "slab", split_axis=0, concat_axis=0, tiled=True)

    mine = jnp.stack([tilt.astype(f32), shift.astype(f32), frac.astype(f32), noise_var])
    slot_hit = (jnp.arange(peers) == me).astype(f32)
    every = mine[:, :, None] * slot_hit
    every = butterfly(every, peers).reshape(4, total)
    tilts, shifts, fracs = (every[n].astype(i32) for n in range(3))
    noises = every[3]
    tilt_col, shift_col, frac_col = (value[:, None] for value in (tilts, shifts, fracs))

    edge = GRID * (planes - 1)
    bottom = jnp.concatenate([mean_volume[None, :GRID], components[:, :GRID]], axis=0)
    top = jnp.concatenate([mean_volume[None, edge:], components[:, edge:]], axis=0)
    upper = lax.ppermute(bottom, "slab", [(n, n - 1) for n in range(1, peers)])
    lower = lax.ppermute(top, "slab", [(n, n + 1) for n in range(peers - 1)])

    pair = 2 if blocks % 16 else 1
    table = pl.pallas_call(
        functools.partial(table_kernel, (planes, slots, blocks, pair)),
        out_shape=jax.ShapeDtypeStruct((slots, planes * blocks, width), bf16),
        grid=(planes // pair,),
        in_specs=[
            pl.BlockSpec((pair * GRID, GRID), lambda n: (n, 0)),
            pl.BlockSpec((COMPS, pair * GRID, GRID), lambda n: (0, n, 0)),
        ],
        out_specs=pl.BlockSpec((slots, pair * blocks, width), lambda n: (0, n, 0)),
        scratch_shapes=[pltpu.VMEM((GRID, GRID), bf16)],
        compiler_params=params(),
        name="table",
    )(mean_volume, components)

    slices, slices_extra, gram = pl.pallas_call(
        functools.partial(extract_kernel, (planes, slots, blocks, chunk, total)),
        out_shape=[
            jax.ShapeDtypeStruct((slots, total, width), bf16),
            jax.ShapeDtypeStruct((2 * total, width), bf16),
            jax.ShapeDtypeStruct((total, LANES), f32),
        ],
        grid=(steps,),
        in_specs=[
            smem(),
            whole((total, 1)),
            whole((total, 1)),
            whole((total, 1)),
            pl.BlockSpec((chunk, planes * blocks, width), lambda n: (n, 0, 0)),
            whole((CHANS, GRID, GRID)),
            whole((CHANS, GRID, GRID)),
            whole((GRID, GRID)),
            whole((COMPS, GRID, GRID)),
        ],
        out_specs=[
            pl.BlockSpec((chunk, total, width), lambda n: (n, 0, 0)),
            whole((2 * total, width)),
            whole((total, LANES)),
        ],
        scratch_shapes=[
            pltpu.VMEM((slots, upper_rows, width), bf16),
            pltpu.VMEM((len(PAIRS), total, LANES), f32),
        ],
        compiler_params=params(),
        name="extract",
    )(first, tilt_col, shift_col, frac_col, table, upper, lower, mean_volume, components)

    rows, rows_extra, partial = pl.pallas_call(
        functools.partial(project_kernel, (slots, chunk, total, peers, count)),
        out_shape=[
            jax.ShapeDtypeStruct((slots, total, GRID), bf16),
            jax.ShapeDtypeStruct((2 * total, GRID), bf16),
            jax.ShapeDtypeStruct((total, LANES), f32),
        ],
        grid=(steps,),
        in_specs=[
            whole((peers * pack_rows, GRID)),
            pl.BlockSpec((chunk, total, width), lambda n: (n, 0, 0)),
            whole((total, LANES)),
        ],
        out_specs=[
            pl.BlockSpec((chunk, total, GRID), lambda n: (n, 0, 0)),
            whole((2 * total, GRID)),
            whole((total, LANES)),
        ],
        scratch_shapes=[
            pltpu.VMEM((GRID // LANES, peers * pack_rows, LANES), f32),
            pltpu.VMEM((CHANS, total, LANES), f32),
        ],
        compiler_params=params(),
        name="project",
    )(got.reshape(peers * pack_rows, GRID), slices, gram)

    sums = butterfly(partial, peers)

    out_planes = pair
    last = steps - 1
    new_components, latents = pl.pallas_call(
        functools.partial(back_kernel, (planes, slots, blocks, chunk, total, steps, out_planes)),
        out_shape=[
            jax.ShapeDtypeStruct((COMPS, planes * GRID, GRID), bf16),
            jax.ShapeDtypeStruct((8, total), f32),
        ],
        grid=(steps + planes // out_planes,),
        in_specs=[
            smem(),
            whole((total, LANES)),
            whole((1, total)),
            whole((1, 3 * total)),
            whole((total, 1)),
            whole((total, 1)),
            whole((total, 1)),
            pl.BlockSpec((chunk, total, width), lambda n: (jnp.minimum(n, last), 0, 0)),
            pl.BlockSpec((chunk, total, GRID), lambda n: (jnp.minimum(n, last), 0, 0)),
            whole((2 * total, width)),
            whole((2 * total, GRID)),
        ],
        out_specs=[
            pl.BlockSpec((COMPS, out_planes * GRID, GRID), lambda n: (0, jnp.maximum(n - steps, 0), 0)),
            whole((8, total)),
        ],
        scratch_shapes=[
            pltpu.VMEM((COMPS, planes, GRID, GRID), bf16),
            pltpu.VMEM((8, 3 * total), f32),
            pltpu.VMEM((total, LANES), f32),
            pltpu.VMEM((2 * total, GRID), bf16),
            pltpu.VMEM((GRID, GRID), bf16),
        ],
        compiler_params=params(),
        name="back",
    )(
        first, sums, noises[None], jnp.tile(tilts, 3)[None], tilt_col, shift_col, frac_col,
        slices, rows, slices_extra, rows_extra,
    )
    mine = lax.dynamic_index_in_dim(latents.reshape(8, count, peers), me, 2, keepdims=False)
    return new_components, jnp.transpose(mine[:COMPS])


def butterfly(value, peers):
    step = 1
    while step < peers:
        value = value + lax.ppermute(value, "slab", [(n, n ^ step) for n in range(peers)])
        step *= 2
    return value


def solution(mesh):
    placed = (
        P(("groups", "slab"), None),
        P(None, ("groups", "slab"), None),
        P(("groups", "slab"), None, None),
        P(("groups", "slab")),
        P(("groups", "slab")),
        P(("groups", "slab")),
        P(("groups", "slab")),
    )
    return jax.shard_map(
        local,
        mesh=mesh,
        in_specs=placed,
        out_specs=(P(None, ("groups", "slab"), None), P(("groups", "slab"), None)),
        check_vma=False,
    )
```

```python
import functools

import jax
import jax.numpy as jnp
from jax import lax
from jax.experimental import pallas as pl
from jax.experimental.pallas import tpu as pltpu
from jax.sharding import PartitionSpec as P

GRID = 256
HALF = GRID // 2
COMPS = 6
CHANS = COMPS + 1
TILE = 128
LANES = 128
PAIRS = [(k, l) for k in range(CHANS) for l in range(k, CHANS)]
PROJECT_AT = len(PAIRS)

f32 = jnp.float32
bf16 = jnp.bfloat16
i32 = jnp.int32


def iota(shape, dim):
    return lax.broadcasted_iota(i32, shape, dim)


def dot(a, b):
    return jnp.dot(a, b, preferred_element_type=f32)


def params(mebibytes):
    return pltpu.CompilerParams(vmem_limit_bytes=mebibytes * 1024 * 1024)


def plane_depth(position, tilt):
    numerator = (position - HALF) * tilt
    return jnp.right_shift(numerator, 7) + HALF, jnp.bitwise_and(numerator, HALF - 1)


def pack_kernel(sizes, tilt_ref, shift_ref, mine_ref, image_ref, out_ref, turned_ref):
    planes, slots, peers, count = sizes
    main_rows = count * slots
    shape = (peers * slots, GRID)
    row, col = iota(shape, 0), iota(shape, 1)
    slot_hit = row % slots == col % slots
    first = row // slots * planes
    for image in range(count):
        rows = slice(image * GRID, (image + 1) * GRID)
        for at in range(GRID // TILE):
            span = slice(at * TILE, (at + 1) * TILE)
            part = image_ref[rows, span].astype(f32)
            turned_ref[rows, span] = pltpu.roll(part, shift_ref[image], 1).astype(bf16)
        plane, _ = plane_depth(iota((1, GRID), 1), tilt_ref[image])
        ahead = plane - first
        hit = slot_hit & (ahead >= 0) & (ahead < planes)
        found = dot(jnp.where(hit, 1.0, 0.0).astype(bf16), turned_ref[rows, :])
        found = found.reshape(peers, slots, GRID).astype(bf16)
        out_ref[:, image * slots : (image + 1) * slots, :] = found
    lane = iota((1, count * GRID), 1)
    tilt = jnp.full((1, count * GRID), tilt_ref[0], i32)
    for image in range(1, count):
        tilt = jnp.where(lane >= image * GRID, tilt_ref[image], tilt)
    plane, _ = plane_depth(jnp.bitwise_and(lane, GRID - 1), tilt)
    shape = (peers * 2 * count, count * GRID)
    row, col = iota(shape, 0), iota(shape, 1)
    hit = (row // 2 % count == col // GRID) & (row % 2 == col % 2)
    hit = hit & (plane == row // (2 * count) * planes - 1)
    found = dot(jnp.where(hit, 1.0, 0.0).astype(bf16), turned_ref[...])
    out_ref[:, main_rows:, :] = found.reshape(peers, 2 * count, GRID).astype(bf16)


def slot_order(slots, blocks):
    row, col = iota((GRID, GRID), 0), iota((GRID, GRID), 1)
    return (col == (row % blocks) * slots + row // blocks).astype(f32).astype(bf16)


WINDOW = 80
MIDDLE = 32


def window_starts(boundary):
    away = jnp.abs(boundary)
    nearest = jnp.where(boundary > 0, away - 1, away)
    furthest = jnp.minimum(jnp.where(boundary > 0, 2 * away - 1, 2 * away + 2), HALF)
    low = (HALF - furthest) // 16 * 16
    high = jnp.minimum((HALF + nearest) // 16 * 16, GRID - WINDOW)
    return low, high


def window_rows(boundary):
    low, high = window_starts(boundary)
    lane = iota((1, 2 * WINDOW + MIDDLE), 1)
    far = boundary != 0
    below = jnp.where(far & (low + lane < HALF), low + lane, -1)
    above = high + lane - WINDOW
    above = jnp.where(far & (above >= HALF), above, -1)
    middle = jnp.where(far, -1, HALF - MIDDLE // 2 + lane - 2 * WINDOW)
    return jnp.where(lane < WINDOW, below, jnp.where(lane < 2 * WINDOW, above, middle))


def edges_kernel(
    planes, place_ref, tilt_ref, frac_ref, noise_ref, mean_ref, comp_ref, mean_top_ref, comp_top_ref,
    down_ref, up_ref, middle_ref, mine_ref,
):
    first = place_ref[0]
    here = iota((1, mine_ref.shape[1]), 1) == place_ref[1]
    count = mine_ref.shape[0] // 3
    for image in range(count):
        values = (tilt_ref[image].astype(f32), frac_ref[image].astype(f32), noise_ref[image])
        for n, value in enumerate(values):
            mine_ref[pl.ds(n * count + image, 1), :] = jnp.where(here, value, 0.0)
    bottom = first - HALF
    middle = pl.ds(HALF - MIDDLE // 2, MIDDLE)
    sides = (
        (bottom, mean_ref, comp_ref, down_ref),
        (bottom + planes, mean_top_ref, comp_top_ref, up_ref),
    )
    for chan in range(CHANS):
        middles = []
        for boundary, mean, comp, out in sides:
            plane = mean if chan == 0 else comp.at[chan - 1]
            low, high = window_starts(boundary)
            out[chan, :WINDOW, :] = plane[pl.ds(pl.multiple_of(low, 16), WINDOW), :]
            out[chan, WINDOW:, :] = plane[pl.ds(pl.multiple_of(high, 16), WINDOW), :]
            middles.append(plane[middle, :])
        middle_ref[chan] = jnp.where(bottom == 0, middles[0], middles[1])


def stream(step, parts, copies):
    @pl.when(step == 0)
    def _():
        for part in range(parts):
            for copy in copies(part):
                copy.start()

    @pl.when(step < parts)
    def _():
        for copy in copies(step):
            copy.wait()


def parameter_rows(every_ref):
    count = every_ref.shape[0] // 3
    rows = []
    for n in range(3):
        parts = [every_ref[n * count + at : n * count + at + 1, :] for at in range(count)]
        rows.append(jnp.concatenate(parts, axis=1))
    return rows


def columns(rows):
    fill = jnp.zeros((LANES - len(rows), rows[0].shape[1]), f32)
    return jnp.transpose(jnp.concatenate(rows + [fill], axis=0))


def interpolate(rows, weight, turn):
    parts = []
    for at in range(GRID // TILE):
        part = rows[:, at * TILE : (at + 1) * TILE]
        parts.append((1.0 - weight) * part + weight * pltpu.roll(part, turn, 1))
    return jnp.concatenate(parts, axis=1)


def extract_kernel(
    sizes, place_ref, every_ref, mean_hbm, comp_hbm, up_ref, low_ref, middle_ref,
    out_ref, extra_ref, gram_ref,
    mean_ref, comp_ref, mean_sem, comp_sem, table_ref, order_ref, sums_ref, column_ref,
):
    planes, slots, blocks, chunk, images, pair = sizes
    step, first = pl.program_id(0), place_ref[0]
    tables = planes // pair

    def copies(part):
        rows = pl.ds(pl.multiple_of(part * pair * GRID, GRID), pair * GRID)
        return (
            pltpu.make_async_copy(mean_hbm.at[rows], mean_ref.at[rows], mean_sem.at[part]),
            pltpu.make_async_copy(comp_hbm.at[:, rows], comp_ref.at[:, rows], comp_sem.at[part]),
        )

    stream(step, tables, copies)

    @pl.when(step == 0)
    def _():
        column_ref[...] = columns(parameter_rows(every_ref))

    tilt = column_ref[:, 0:1].astype(i32)
    weight = column_ref[:, 1:2] / 16.0
    own_rows = planes * blocks

    @pl.when(step == 0)
    def _():
        order_ref[...] = slot_order(slots, blocks)
        at_up, at_low = window_rows(first + planes - HALF), window_rows(first - HALF)
        row = iota((GRID, at_up.shape[1]), 0)
        order = (at_up == (row % blocks) * slots + row // blocks).astype(f32).astype(bf16)
        parts = []
        for odd in range(2):
            pieces = []
            for lane, part in ((at_low, 0), (iota((1, GRID), 1), 1)):
                plane, depth = plane_depth(lane, tilt)
                hit = (plane == first - 1) & (lane >= 0) & (jnp.bitwise_and(lane, 1) == odd)
                depth = depth if part else HALF - depth
                pieces.append(jnp.where(hit, depth, 0).astype(f32) / HALF)
            parts.append(pieces)
        mixing_low = jnp.concatenate([parts[0][0], parts[1][0]], axis=0).astype(bf16)
        mixing_own = jnp.concatenate([parts[0][1], parts[1][1]], axis=0).astype(bf16)
        weight2 = jnp.concatenate([weight, weight], axis=0)
        fill = table_ref.shape[1] - own_rows - blocks
        for chan in range(CHANS):
            at = slice(chan * GRID, (chan + 1) * GRID)
            upper = jnp.concatenate([up_ref[chan], middle_ref[chan]], axis=0)
            upper = dot(order, upper).reshape(slots, blocks, GRID)
            if fill:
                upper = jnp.concatenate([upper, jnp.zeros((slots, fill, GRID), f32)], axis=1)
            table_ref[:, own_rows:, at] = upper.astype(bf16)
            lower = jnp.concatenate([low_ref[chan], middle_ref[chan]], axis=0)
            own = mean_ref[:GRID, :] if chan == 0 else comp_ref[chan - 1, :GRID, :]
            blended = dot(mixing_low, lower) + dot(mixing_own, own)
            blended = blended.astype(bf16).astype(f32)
            extra_ref[:, at] = interpolate(blended, weight2, TILE - 1).astype(bf16)
        sums_ref[...] = jnp.zeros_like(sums_ref)

    @pl.when(step < tables)
    def _():
        order = order_ref[...]
        rows = pl.ds(pl.multiple_of(step * pair * blocks, 16), pair * blocks)
        for chan in range(CHANS):
            pieces = []
            for at in range(pair):
                span = pl.ds(pl.multiple_of((step * pair + at) * GRID, GRID), GRID)
                plane = mean_ref[span, :] if chan == 0 else comp_ref[chan - 1, span, :]
                pieces.append(dot(order, plane).reshape(slots, blocks, GRID))
            both = jnp.concatenate(pieces, axis=1).astype(bf16)
            table_ref[:, rows, chan * GRID : (chan + 1) * GRID] = both

    @pl.when(step >= tables)
    def _():
        lane = iota((images, table_ref.shape[1]), 1)
        block_at, plane_at = lane % blocks, lane // blocks
        plane_at = jnp.where(plane_at > planes, -1000, plane_at) + first
        low_at = jnp.where(plane_at < first + planes, plane_at, -1000)
        high_at = jnp.where(plane_at > first, plane_at - 1, -1000)
        base = (block_at * slots - HALF) * tilt
        for at in range(chunk):
            slot = (step - tables) * chunk + at
            numerator = base + slot * tilt
            plane, depth = jnp.right_shift(numerator, 7) + HALF, jnp.bitwise_and(numerator, HALF - 1)
            mixing = jnp.where(plane == low_at, HALF - depth, jnp.where(plane == high_at, depth, 0))
            mixing = (mixing.astype(f32) * (1.0 / HALF)).astype(bf16)
            blended = dot(mixing, table_ref[slot])
            for chan in range(CHANS):
                span = slice(chan * GRID, (chan + 1) * GRID)
                part = blended[:, span].astype(bf16).astype(f32)
                out_ref[at, :, span] = interpolate(part, weight, TILE - 1).astype(bf16)
        gram_sums(chunk, images, out_ref, sums_ref)

    @pl.when(step == pl.num_programs(0) - 1)
    def _():
        lane = iota((images, LANES), 1)
        total = jnp.zeros((images, LANES), f32)
        for n in range(len(PAIRS)):
            total = jnp.where(lane == n, jnp.sum(sums_ref[n], axis=1, keepdims=True), total)
        gram_ref[...] = total


def gram_sums(chunk, images, out_ref, sums_ref):
    def accumulate(group, carry):
        rows = pl.ds(pl.multiple_of(group * 16, 16), 16)
        sums = [sums_ref[n, rows, :] for n in range(len(PAIRS))]
        for at in range(chunk):
            for tile in range(GRID // LANES):
                values = [
                    out_ref[at, rows, pl.ds(chan * GRID + tile * LANES, LANES)].astype(f32)
                    for chan in range(CHANS)
                ]
                for n, (k, l) in enumerate(PAIRS):
                    sums[n] = sums[n] + values[k] * values[l]
        for n in range(len(PAIRS)):
            sums_ref[n, rows, :] = sums[n]
        return carry

    lax.fori_loop(0, images // 16, accumulate, 0)


def project_kernel(
    sizes, got_ref, slice_hbm, gram_ref, rows_ref, extra_ref, total_ref,
    slice_ref, slice_sem, wide_ref, sums_ref,
):
    slots, chunk, images, peers, count = sizes
    stride = count * slots + 2 * count
    step = pl.program_id(0)

    def copies(part):
        at = pl.ds(part * chunk, chunk)
        return (pltpu.make_async_copy(slice_hbm.at[at], slice_ref.at[at], slice_sem.at[part]),)

    stream(step, slots // chunk, copies)

    @pl.when(step == 0)
    def _():
        for tile in range(GRID // LANES):
            wide_ref[tile] = got_ref[:, tile * LANES : (tile + 1) * LANES].astype(f32)
        sums_ref[...] = jnp.zeros_like(sums_ref)
        for odd in range(2):
            for image in range(count):
                start = count * slots + image * 2 + odd
                at = (odd * count + image) * peers
                for tile in range(GRID // LANES):
                    part = wide_ref[tile, pl.ds(start, peers, stride=stride), :]
                    extra_ref[at : at + peers, tile * LANES : (tile + 1) * LANES] = part.astype(bf16)

    for image in range(count):
        span = slice(image * peers, (image + 1) * peers)
        sums = [sums_ref[chan, span, :] for chan in range(CHANS)]
        for at in range(chunk):
            slot = step * chunk + at
            for tile in range(GRID // LANES):
                part = wide_ref[tile, pl.ds(image * slots + slot, peers, stride=stride), :]
                rows_ref[at, span, tile * LANES : (tile + 1) * LANES] = part.astype(bf16)
                for chan in range(CHANS):
                    lanes = slice(chan * GRID + tile * LANES, chan * GRID + (tile + 1) * LANES)
                    sums[chan] = sums[chan] + part * slice_ref[slot, span, lanes].astype(f32)
        for chan in range(CHANS):
            sums_ref[chan, span, :] = sums[chan]

    @pl.when(step == pl.num_programs(0) - 1)
    def _():
        lane = iota((images, LANES), 1)
        total = gram_ref[...]
        for chan in range(CHANS):
            value = jnp.sum(sums_ref[chan], axis=1, keepdims=True)
            total = jnp.where(lane == PROJECT_AT + chan, value, total)
        total_ref[...] = total


def solve_rows(table, noise):
    count = float(GRID * GRID)

    def gram(k, l):
        at = PAIRS.index((min(k, l), max(k, l)))
        return table[at : at + 1, :]

    factor = [[None] * COMPS for _ in range(COMPS)]
    inverse = [None] * COMPS
    for col in range(COMPS):
        for row in range(col, COMPS):
            total = gram(row + 1, col + 1) / count
            if row == col:
                total = total + noise
            for at in range(col):
                total = total - factor[row][at] * factor[col][at]
            if row == col:
                inverse[col] = 1.0 / jnp.sqrt(total)
            else:
                factor[row][col] = total * inverse[col]
    forward = []
    for row in range(COMPS):
        at = PROJECT_AT + row + 1
        total = (table[at : at + 1, :] - gram(row + 1, 0)) / count
        for col in range(row):
            total = total - factor[row][col] * forward[col]
        forward.append(total * inverse[row])
    latent = [None] * COMPS
    for row in reversed(range(COMPS)):
        total = forward[row]
        for col in range(row + 1, COMPS):
            total = total - factor[col][row] * latent[col]
        latent[row] = total * inverse[row]
    return latent


def back_kernel(
    sizes, place_ref, total_ref, every_ref,
    slice_hbm, rows_ref, slice_extra_ref, rows_extra_ref,
    out_ref, latent_ref, slice_ref, slice_sem, stack_ref, row_ref, tilt_ref, col_ref, free_ref, spill_ref, spill_power_ref, order_ref,
):
    planes, slots, blocks, chunk, images, steps, out_planes = sizes
    step, first = pl.program_id(0), place_ref[0]
    group = 2 if blocks % 16 else 1

    def copies(part):
        at = pl.ds(part * chunk, chunk)
        return (pltpu.make_async_copy(slice_hbm.at[at], slice_ref.at[at], slice_sem.at[part]),)

    stream(step, steps, copies)

    @pl.when(step == 0)
    def _():
        table = jnp.transpose(total_ref[...])
        tilt, frac, noise = parameter_rows(every_ref)
        latent = solve_rows(table, noise)
        free_ref[...] = columns(latent)
        count = latent_ref.shape[0]
        for image in range(count):
            at = image * (images // count) + place_ref[1]
            latent_ref[image : image + 1, :] = free_ref[pl.ds(at, 1), :COMPS]
        rounded = [value.astype(bf16).astype(f32) for value in latent]
        power = rounded[0] * rounded[0]
        for value in rounded[1:]:
            power = power + value * value
        rows = jnp.concatenate(rounded + [power, power], axis=0)
        row_ref[...] = jnp.concatenate([rows, rows, rows], axis=1).astype(bf16)
        tilt_ref[...] = jnp.concatenate([tilt, tilt, tilt], axis=1).astype(i32)
        col_ref[...] = columns(rounded + [power, tilt, frac])
        row, col = iota((GRID, GRID), 0), iota((GRID, GRID), 1)
        order_ref[...] = (row == (col % blocks) * slots + col // blocks).astype(f32).astype(bf16)

    def spread(slices, rows, copies):
        weight = col_ref[:, COMPS + 2 : COMPS + 3] / 16.0
        latent = col_ref[...]
        if copies > 1:
            weight = jnp.concatenate([weight] * copies, axis=0)
            latent = jnp.concatenate([latent] * copies, axis=0)
        residual = rows[...].astype(f32) - slices[:, :GRID].astype(f32)
        for k in range(COMPS):
            span = slice((k + 1) * GRID, (k + 2) * GRID)
            residual = residual - latent[:, k : k + 1] * slices[:, span].astype(f32)
        return interpolate(residual.astype(bf16).astype(f32), weight, 1)

    def factors(parts):
        high = [part.astype(bf16) for part in parts]
        low = [(part - top.astype(f32)).astype(bf16) for part, top in zip(parts, high)]
        shape = (images, LANES)
        high = jnp.concatenate([jnp.broadcast_to(part, shape) for part in high], axis=0)
        low = jnp.concatenate([jnp.broadcast_to(part, shape) for part in low], axis=0)
        return jnp.concatenate([high, low], axis=1)

    @pl.when(step == 0)
    def _():
        value = spread(slice_extra_ref, rows_extra_ref, 2)
        power = col_ref[:, COMPS : COMPS + 1]
        plane, depth = plane_depth(iota((images, GRID), 1), col_ref[:, COMPS + 1 : COMPS + 2].astype(i32))
        odd = jnp.bitwise_and(iota((images, GRID), 1), 1)
        for at in range(2):
            hit = (plane == first - 1) & (odd == at)
            part = jnp.sum(jnp.where(hit, depth, 0).astype(f32), axis=1, keepdims=True) / HALF
            span = slice(at * images, (at + 1) * images)
            spill_ref[span, :] = (part * value[span]).astype(bf16)
            spill_power_ref[span, :] = factors([part * power])

    @pl.when(step < steps)
    def _():
        power = col_ref[:, COMPS : COMPS + 1]
        lane_slot = iota((images, LANES), 1)
        tilt = tilt_ref[...]
        tilt_col = col_ref[:, COMPS + 1 : COMPS + 2].astype(i32)
        row = iota((blocks, 3 * images), 0)
        base = (row * slots - HALF) * tilt
        shape = (planes, blocks, 3 * images)
        plane_at, lane = iota(shape, 0), iota(shape, 2)
        wanted = jnp.where(lane < images, plane_at, plane_at - 1)
        wanted = jnp.where((lane < 2 * images) == (wanted < 0), -1000, wanted) + (first - HALF)
        for start in range(0, chunk, group):
            pieces = [[] for _ in range(COMPS)]
            for at in range(start, start + group):
                slot = step * chunk + at
                value = spread(slice_ref.at[slot], rows_ref.at[at], 1)
                plane, depth = plane_depth(lane_slot * slots + slot, tilt_col)
                plane = plane - first
                live = (plane >= 0) & (plane < planes) & (lane_slot < blocks)
                depth = jnp.sum(jnp.where(live, depth, 0).astype(f32), axis=1, keepdims=True) / HALF
                odd = pl.ds(pl.multiple_of((slot % 2) * images, 16), images)
                right = jnp.concatenate(
                    [
                        ((1.0 - depth) * value).astype(bf16),
                        (depth * value).astype(bf16),
                        spill_ref[odd, :],
                    ],
                    axis=0,
                )
                powers = jnp.concatenate(
                    [factors([(1.0 - depth) * power, depth * power]), spill_power_ref[odd, :]], axis=0
                )
                plane = jnp.right_shift(base + slot * tilt, 7)
                hit = jnp.where(plane[None] == wanted, 1.0, 0.0)
                hit = hit.reshape(planes * blocks, 3 * images).astype(bf16)
                weight = dot(hit, powers)
                scale = 1.0 / (1.0 + (weight[:, :LANES] + weight[:, LANES:]))
                scale = jnp.concatenate([scale, scale], axis=1)
                left = jnp.concatenate([hit * row_ref[k : k + 1, :] for k in range(COMPS)], axis=0)
                totals = dot(left, right)
                for k in range(COMPS):
                    total = totals[k * planes * blocks : (k + 1) * planes * blocks] * scale
                    pieces[k].append(total.reshape(planes, blocks, GRID))
            rows = pl.ds(pl.multiple_of((step * chunk + start) * blocks, 16), group * blocks)
            for k in range(COMPS):
                stack_ref[k, :, rows, :] = jnp.concatenate(pieces[k], axis=1).astype(bf16)

    @pl.when(step >= steps)
    def _():
        order = order_ref[...]
        for k in range(COMPS):
            for at in range(out_planes):
                plane = (step - steps) * out_planes + at
                out_ref[k, at * GRID : (at + 1) * GRID, :] = dot(order, stack_ref[k, plane]).astype(bf16)


def whole(shape):
    return pl.BlockSpec(shape, lambda *_: (0,) * len(shape))


def smem():
    return pl.BlockSpec(memory_space=pltpu.SMEM)


def local(mean_volume, components, images, tilt, shift, frac, noise_var):
    peers = lax.axis_size("slab")
    me = lax.axis_index("slab")
    planes = mean_volume.shape[0] // GRID
    slots = 2 * planes
    blocks = GRID // slots
    count = images.shape[0]
    total = peers * count
    width = CHANS * GRID
    chunk = max(1, 256 // total)
    steps = slots // chunk
    pack_rows = count * slots + 2 * count
    upper_rows = -(-blocks // 16) * 16
    place = jnp.stack([me * planes, me]).astype(i32)

    top = planes - 1
    wide = 2 * WINDOW
    down_rows, up_rows, middle_rows, mine = pl.pallas_call(
        functools.partial(edges_kernel, planes),
        out_shape=[
            jax.ShapeDtypeStruct((CHANS, rows, GRID), bf16) for rows in (wide, wide, MIDDLE)
        ] + [jax.ShapeDtypeStruct((3 * count, peers), f32)],
        grid=(1,),
        in_specs=[
            smem(),
            smem(),
            smem(),
            smem(),
            pl.BlockSpec((GRID, GRID), lambda n: (0, 0)),
            pl.BlockSpec((COMPS, GRID, GRID), lambda n: (0, 0, 0)),
            pl.BlockSpec((GRID, GRID), lambda n: (top, 0)),
            pl.BlockSpec((COMPS, GRID, GRID), lambda n: (0, top, 0)),
        ],
        out_specs=[whole((CHANS, rows, GRID)) for rows in (wide, wide, MIDDLE)]
        + [whole((3 * count, peers))],
        compiler_params=params(56),
        name="edges",
    )(place, tilt, frac, noise_var, mean_volume, components, mean_volume, components)
    half = peers // 2
    upper = lax.ppermute(down_rows, "slab", [(n, n - 1) for n in range(1, peers) if n != half])
    lower = lax.ppermute(up_rows, "slab", [(n, n + 1) for n in range(peers - 1) if n + 1 != half])
    middle = lax.ppermute(middle_rows, "slab", [(half, half - 1), (half - 1, half)])

    every = gather_places(mine, peers)

    packed = pl.pallas_call(
        functools.partial(pack_kernel, (planes, slots, peers, count)),
        out_shape=jax.ShapeDtypeStruct((peers, pack_rows, GRID), bf16),
        in_specs=[smem(), smem(), pl.BlockSpec(memory_space=pl.ANY), whole((count * GRID, GRID))],
        out_specs=whole((peers, pack_rows, GRID)),
        scratch_shapes=[pltpu.VMEM((count * GRID, GRID), bf16)],
        grid=(1,),
        compiler_params=params(56),
        name="pack",
    )(tilt, shift, mine, images.reshape(count * GRID, GRID))
    got = lax.all_to_all(packed, "slab", split_axis=0, concat_axis=0, tiled=True)

    pair = 2 if blocks % 16 else 1
    tables = planes // pair
    table_rows = -(-(planes + 1) * blocks // 16) * 16
    slices, slices_extra, gram = pl.pallas_call(
        functools.partial(extract_kernel, (planes, slots, blocks, chunk, total, pair)),
        out_shape=[
            jax.ShapeDtypeStruct((slots, total, width), bf16),
            jax.ShapeDtypeStruct((2 * total, width), bf16),
            jax.ShapeDtypeStruct((total, LANES), f32),
        ],
        grid=(tables + steps,),
        in_specs=[
            smem(),
            whole((3 * count, peers)),
            pl.BlockSpec(memory_space=pl.ANY),
            pl.BlockSpec(memory_space=pl.ANY),
            whole((CHANS, wide, GRID)),
            whole((CHANS, wide, GRID)),
            whole((CHANS, MIDDLE, GRID)),
        ],
        out_specs=[
            pl.BlockSpec((chunk, total, width), lambda n: (jnp.maximum(n - tables, 0), 0, 0)),
            whole((2 * total, width)),
            whole((total, LANES)),
        ],
        scratch_shapes=[
            pltpu.VMEM((planes * GRID, GRID), bf16),
            pltpu.VMEM((COMPS, planes * GRID, GRID), bf16),
            pltpu.SemaphoreType.DMA((tables,)),
            pltpu.SemaphoreType.DMA((tables,)),
            pltpu.VMEM((slots, table_rows, width), bf16),
            pltpu.VMEM((GRID, GRID), bf16),
            pltpu.VMEM((len(PAIRS), total, LANES), f32),
            pltpu.VMEM((total, LANES), f32),
        ],
        compiler_params=params(56),
        name="extract",
    )(place, every, mean_volume, components, upper, lower, middle)

    rows, rows_extra, partial = pl.pallas_call(
        functools.partial(project_kernel, (slots, chunk, total, peers, count)),
        out_shape=[
            jax.ShapeDtypeStruct((slots, total, GRID), bf16),
            jax.ShapeDtypeStruct((2 * total, GRID), bf16),
            jax.ShapeDtypeStruct((total, LANES), f32),
        ],
        grid=(steps,),
        in_specs=[
            whole((peers * pack_rows, GRID)),
            pl.BlockSpec(memory_space=pl.ANY),
            whole((total, LANES)),
        ],
        out_specs=[
            pl.BlockSpec((chunk, total, GRID), lambda n: (n, 0, 0)),
            whole((2 * total, GRID)),
            whole((total, LANES)),
        ],
        scratch_shapes=[
            pltpu.VMEM((slots, total, width), bf16),
            pltpu.SemaphoreType.DMA((steps,)),
            pltpu.VMEM((GRID // LANES, peers * pack_rows, LANES), f32),
            pltpu.VMEM((CHANS, total, LANES), f32),
        ],
        compiler_params=params(56),
        name="project",
    )(got.reshape(peers * pack_rows, GRID), slices, gram)

    sums = butterfly(partial, peers)

    out_planes = 2
    last = steps - 1
    new_components, latents = pl.pallas_call(
        functools.partial(back_kernel, (planes, slots, blocks, chunk, total, steps, out_planes)),
        out_shape=[
            jax.ShapeDtypeStruct((COMPS, planes * GRID, GRID), bf16),
            jax.ShapeDtypeStruct((count, COMPS), f32),
        ],
        grid=(steps + planes // out_planes,),
        in_specs=[
            smem(),
            whole((total, LANES)),
            whole((3 * count, peers)),
            pl.BlockSpec(memory_space=pl.ANY),
            pl.BlockSpec((chunk, total, GRID), lambda n: (jnp.minimum(n, last), 0, 0)),
            whole((2 * total, width)),
            whole((2 * total, GRID)),
        ],
        out_specs=[
            pl.BlockSpec((COMPS, out_planes * GRID, GRID), lambda n: (0, jnp.maximum(n - steps, 0), 0)),
            whole((count, COMPS)),
        ],
        scratch_shapes=[
            pltpu.VMEM((slots, total, width), bf16),
            pltpu.SemaphoreType.DMA((steps,)),
            pltpu.VMEM((COMPS, planes, GRID, GRID), bf16),
            pltpu.VMEM((8, 3 * total), bf16),
            pltpu.VMEM((1, 3 * total), i32),
            pltpu.VMEM((total, LANES), f32),
            pltpu.VMEM((total, LANES), f32),
            pltpu.VMEM((2 * total, GRID), bf16),
            pltpu.VMEM((2 * total, 2 * LANES), bf16),
            pltpu.VMEM((GRID, GRID), bf16),
        ],
        compiler_params=params(56),
        name="back",
    )(place, sums, every, slices, rows, slices_extra, rows_extra)
    return new_components, latents


def exchange(value, step):
    peers = lax.axis_size("slab")
    return value + lax.ppermute(value, "slab", [(n, n ^ step) for n in range(peers)])


def gather_places(value, peers):
    fours = [value] + [
        lax.ppermute(value, "slab", [(n, n ^ (part * peers // 4)) for n in range(peers)])
        for part in (2, 3, 1)
    ]
    value = (fours[0] + fours[1]) + (fours[2] + fours[3])
    step = peers // 8
    while step:
        value = exchange(value, step)
        step //= 2
    return value


def butterfly(value, peers):
    step = 1
    while step < peers:
        value = exchange(value, step)
        step *= 2
    return value


def solution(mesh):
    placed = (
        P(("groups", "slab"), None),
        P(None, ("groups", "slab"), None),
        P(("groups", "slab"), None, None),
        P(("groups", "slab")),
        P(("groups", "slab")),
        P(("groups", "slab")),
        P(("groups", "slab")),
    )
    return jax.shard_map(
        local,
        mesh=mesh,
        in_specs=placed,
        out_specs=(P(None, ("groups", "slab"), None), P(("groups", "slab"), None)),
        check_vma=False,
    )
```

```python
import functools

import jax
import jax.numpy as jnp
from jax import lax
from jax.experimental import pallas as pl
from jax.experimental.pallas import tpu as pltpu
from jax.sharding import PartitionSpec as P

GRID = 256
HALF = GRID // 2
COMPS = 6
CHANS = COMPS + 1
TILE = 128
LANES = 128
PAIRS = [(k, l) for k in range(CHANS) for l in range(k, CHANS)]
PROJECT_AT = len(PAIRS)

f32 = jnp.float32
bf16 = jnp.bfloat16
i32 = jnp.int32


def iota(shape, dim):
    return lax.broadcasted_iota(i32, shape, dim)


def dot(a, b):
    return jnp.dot(a, b, preferred_element_type=f32)


def params(mebibytes):
    return pltpu.CompilerParams(vmem_limit_bytes=mebibytes * 1024 * 1024)


def plane_depth(position, tilt):
    numerator = (position - HALF) * tilt
    return jnp.right_shift(numerator, 7) + HALF, jnp.bitwise_and(numerator, HALF - 1)


def pack_kernel(sizes, tilt_ref, shift_ref, image_ref, out_ref, turned_ref):
    planes, slots, peers, count = sizes
    main_rows = count * slots
    shape = (peers * slots, GRID)
    row, col = iota(shape, 0), iota(shape, 1)
    slot_hit = jnp.bitwise_and(row - col, slots - 1) == 0
    first_hit = jnp.where(slot_hit, row // slots * planes, -1)
    for image in range(count):
        rows = slice(image * GRID, (image + 1) * GRID)
        for at in range(GRID // TILE):
            span = slice(at * TILE, (at + 1) * TILE)
            part = image_ref[rows, span].astype(f32)
            turned_ref[rows, span] = pltpu.roll(part, shift_ref[image], 1).astype(bf16)
        plane, _ = plane_depth(iota((1, GRID), 1), tilt_ref[image])
        hit = jnp.bitwise_and(plane, -planes) == first_hit
        found = dot(jnp.where(hit, 1.0, 0.0).astype(bf16), turned_ref[rows, :])
        found = found.reshape(peers, slots, GRID).astype(bf16)
        out_ref[:, image * slots : (image + 1) * slots, :] = found
    lane = iota((1, count * GRID), 1)
    tilt = jnp.full((1, count * GRID), tilt_ref[0], i32)
    for image in range(1, count):
        tilt = jnp.where(lane >= image * GRID, tilt_ref[image], tilt)
    plane, _ = plane_depth(jnp.bitwise_and(lane, GRID - 1), tilt)
    shape = (peers * 2 * count, count * GRID)
    row, col = iota(shape, 0), iota(shape, 1)
    hit = (row // 2 % count == col // GRID) & (row % 2 == col % 2)
    hit = hit & (plane == row // (2 * count) * planes - 1)
    found = dot(jnp.where(hit, 1.0, 0.0).astype(bf16), turned_ref[...])
    out_ref[:, main_rows:, :] = found.reshape(peers, 2 * count, GRID).astype(bf16)


def after_kernel(*refs):
    pass


def slot_order(slots, blocks):
    row, col = iota((GRID, GRID), 0), iota((GRID, GRID), 1)
    return (col == (row % blocks) * slots + row // blocks).astype(f32).astype(bf16)


WINDOW = 80


def window_starts(boundary):
    away = jnp.abs(boundary)
    nearest = jnp.where(boundary > 0, away - 1, away)
    furthest = jnp.minimum(jnp.where(boundary > 0, 2 * away - 1, 2 * away + 2), HALF)
    low = (HALF - furthest) // 16 * 16
    high = jnp.minimum((HALF + nearest) // 16 * 16, GRID - WINDOW)
    return low, high


def window_rows(boundary):
    low, high = window_starts(boundary)
    lane = iota((1, 2 * WINDOW), 1)
    below = jnp.where(low + lane < HALF, low + lane, -1)
    above = high + lane - WINDOW
    above = jnp.where(above >= HALF, above, -1)
    return jnp.where(lane < WINDOW, below, above)


def reached_starts(distance):
    away = jnp.abs(distance)
    nearest = jnp.where(away > 1, away, 0)
    furthest = jnp.minimum(2 * away + 2, HALF)
    low = jnp.minimum((HALF - furthest) // 16 * 16, HALF - 32)
    high = jnp.minimum(jnp.maximum((HALF + nearest) // 16 * 16, low + WINDOW), GRID - WINDOW)
    return low, high


def edges_kernel(planes, place_ref, mean_ref, comp_ref, mean_top_ref, comp_top_ref, near_ref, far_ref):
    bottom = place_ref[0] - HALF
    even = place_ref[1] % 2 == 0

    def fill(boundary, mean, comp, out):
        for chan in range(CHANS):
            plane = mean if chan == 0 else comp.at[chan - 1]
            for n, start in enumerate(window_starts(boundary)):
                rows = pl.ds(pl.multiple_of(start, 16), WINDOW)
                out[chan, n * WINDOW : (n + 1) * WINDOW, :] = plane[rows, :]

    @pl.when(even)
    def _():
        fill(bottom + planes, mean_top_ref, comp_top_ref, near_ref)
        fill(bottom, mean_ref, comp_ref, far_ref)

    @pl.when(jnp.logical_not(even))
    def _():
        fill(bottom, mean_ref, comp_ref, near_ref)
        fill(bottom + planes, mean_top_ref, comp_top_ref, far_ref)


def stream(step, parts, copies):
    @pl.when(step == 0)
    def _():
        for part in range(parts):
            for copy in copies(part):
                copy.start()

    @pl.when(step < parts)
    def _():
        for copy in copies(step):
            copy.wait()


def parameter_rows(every_ref, images):
    table = jnp.transpose(every_ref[:, 0, :])
    count = images // every_ref.shape[0]
    rows = []
    for n in range(3):
        parts = [table[n * count + at : n * count + at + 1, :] for at in range(count)]
        rows.append(jnp.concatenate(parts, axis=1))
    return rows


def columns(rows):
    fill = jnp.zeros((LANES - len(rows), rows[0].shape[1]), f32)
    return jnp.transpose(jnp.concatenate(rows + [fill], axis=0))


def interpolate(rows, weight, turn):
    parts = []
    for at in range(GRID // TILE):
        part = rows[:, at * TILE : (at + 1) * TILE]
        parts.append((1.0 - weight) * part + weight * pltpu.roll(part, turn, 1))
    return jnp.concatenate(parts, axis=1)


def extract_kernel(
    sizes, place_ref, every_ref, mean_hbm, comp_hbm, near_hbm, far_hbm,
    out_ref, extra_ref, gram_ref, blank_ref,
    near_ref, far_ref, edge_sem, zero_ref, zero_sem, mean_ref, comp_ref, mean_sem, comp_sem, table_ref, order_ref, sums_ref, column_ref,
):
    planes, slots, blocks, chunk, images, pair = sizes
    step, first = pl.program_id(0), place_ref[0]
    tables = planes // pair

    def copies(part):
        rows = pl.ds(pl.multiple_of(part * pair * GRID, GRID), pair * GRID)
        return (
            pltpu.make_async_copy(mean_hbm.at[rows], mean_ref.at[rows], mean_sem.at[part]),
            pltpu.make_async_copy(comp_hbm.at[:, rows], comp_ref.at[:, rows], comp_sem.at[part]),
        )

    stream(step, tables, copies)

    def blanks(part):
        rows = pl.ds(pl.multiple_of(part * GRID, GRID), GRID)
        return pltpu.make_async_copy(zero_ref, blank_ref.at[:, rows], zero_sem.at[part])

    @pl.when(step == 0)
    def _():
        zero_ref[...] = jnp.zeros_like(zero_ref)

    @pl.when(step == tables)
    def _():
        for part in range(planes):
            blanks(part).start()

    @pl.when(step == pl.num_programs(0) - 1)
    def _():
        for part in range(planes):
            blanks(part).wait()

    @pl.when(step == 0)
    def _():
        column_ref[...] = columns(parameter_rows(every_ref, images))

    tilt = column_ref[:, 0:1].astype(i32)
    weight = column_ref[:, 1:2] / 16.0
    own_rows = planes * blocks

    edges = (
        pltpu.make_async_copy(near_hbm, near_ref, edge_sem.at[0]),
        pltpu.make_async_copy(far_hbm, far_ref, edge_sem.at[1]),
    )

    @pl.when(step == 0)
    def _():
        for copy in edges:
            copy.start()
        order_ref[...] = slot_order(slots, blocks)
        sums_ref[...] = jnp.zeros_like(sums_ref)

    @pl.when(step == tables - 1)
    def _():
        for copy in edges:
            copy.wait()
        at_up, at_low = window_rows(first + planes - HALF), window_rows(first - HALF)
        row = iota((GRID, at_up.shape[1]), 0)
        order = (at_up == (row % blocks) * slots + row // blocks).astype(f32).astype(bf16)
        parts = []
        for odd in range(2):
            pieces = []
            for lane, part in ((at_low, 0), (iota((1, GRID), 1), 1)):
                plane, depth = plane_depth(lane, tilt)
                hit = (plane == first - 1) & (lane >= 0) & (jnp.bitwise_and(lane, 1) == odd)
                depth = depth if part else HALF - depth
                pieces.append(jnp.where(hit, depth, 0).astype(f32) / HALF)
            parts.append(pieces)
        mixing_low = jnp.concatenate([parts[0][0], parts[1][0]], axis=0).astype(bf16)
        mixing_own = jnp.concatenate([parts[0][1], parts[1][1]], axis=0).astype(bf16)
        weight2 = jnp.concatenate([weight, weight], axis=0)
        fill = table_ref.shape[1] - own_rows - blocks
        even = place_ref[1] % 2 == 0
        for chan in range(CHANS):
            at = slice(chan * GRID, (chan + 1) * GRID)
            near, far = near_ref[chan], far_ref[chan]
            upper = dot(order, jnp.where(even, near, far)).reshape(slots, blocks, GRID)
            if fill:
                upper = jnp.concatenate([upper, jnp.zeros((slots, fill, GRID), f32)], axis=1)
            table_ref[:, own_rows:, at] = upper.astype(bf16)
            own = mean_ref[:GRID, :] if chan == 0 else comp_ref[chan - 1, :GRID, :]
            blended = dot(mixing_low, jnp.where(even, far, near)) + dot(mixing_own, own)
            blended = blended.astype(bf16).astype(f32)
            extra_ref[:, at] = interpolate(blended, weight2, TILE - 1).astype(bf16)

    @pl.when(step < tables)
    def _():
        order = order_ref[...]
        rows = pl.ds(pl.multiple_of(step * pair * blocks, 16), pair * blocks)
        for chan in range(CHANS):
            pieces = []
            for at in range(pair):
                span = pl.ds(pl.multiple_of((step * pair + at) * GRID, GRID), GRID)
                plane = mean_ref[span, :] if chan == 0 else comp_ref[chan - 1, span, :]
                pieces.append(dot(order, plane).reshape(slots, blocks, GRID))
            both = jnp.concatenate(pieces, axis=1).astype(bf16)
            table_ref[:, rows, chan * GRID : (chan + 1) * GRID] = both

    @pl.when(step >= tables)
    def _():
        lane = iota((images, table_ref.shape[1]), 1)
        block_at, plane_at = lane % blocks, lane // blocks
        plane_at = jnp.where(plane_at > planes, -1000, plane_at) + first
        low_at = jnp.where(plane_at < first + planes, plane_at, -1000)
        high_at = jnp.where(plane_at > first, plane_at - 1, -1000)
        base = (block_at * slots - HALF) * tilt
        for at in range(chunk):
            slot = (step - tables) * chunk + at
            numerator = base + slot * tilt
            plane, depth = jnp.right_shift(numerator, 7) + HALF, jnp.bitwise_and(numerator, HALF - 1)
            mixing = jnp.where(plane == low_at, HALF - depth, jnp.where(plane == high_at, depth, 0))
            mixing = (mixing.astype(f32) * (1.0 / HALF)).astype(bf16)
            blended = dot(mixing, table_ref[slot])
            for chan in range(CHANS):
                span = slice(chan * GRID, (chan + 1) * GRID)
                part = blended[:, span].astype(bf16).astype(f32)
                part = interpolate(part, weight, TILE - 1).astype(bf16)
                out_ref[at, chan * images : (chan + 1) * images, :] = part
        gram_sums(chunk, images, out_ref, sums_ref)

    @pl.when(step == pl.num_programs(0) - 1)
    def _():
        lane = iota((images, LANES), 1)
        total = jnp.zeros((images, LANES), f32)
        for n in range(len(PAIRS)):
            total = jnp.where(lane == n, jnp.sum(sums_ref[n], axis=1, keepdims=True), total)
        gram_ref[...] = total


def gram_sums(chunk, images, out_ref, sums_ref):
    def accumulate(group, carry):
        start = pl.multiple_of(group * 16, 16)
        rows = pl.ds(start, 16)
        sums = [sums_ref[n, rows, :] for n in range(len(PAIRS))]
        for at in range(chunk):
            for tile in range(GRID // LANES):
                values = [
                    out_ref[at, pl.ds(chan * images + start, 16), pl.ds(tile * LANES, LANES)].astype(f32)
                    for chan in range(CHANS)
                ]
                for n, (k, l) in enumerate(PAIRS):
                    sums[n] = sums[n] + values[k] * values[l]
        for n in range(len(PAIRS)):
            sums_ref[n, rows, :] = sums[n]
        return carry

    lax.fori_loop(0, images // 16, accumulate, 0)


def project_kernel(
    sizes, got_ref, slice_ref, gram_ref, rows_ref, extra_ref, total_ref, wide_ref, sums_ref
):
    slots, chunk, images, peers, count = sizes
    stride = count * slots + 2 * count
    step = pl.program_id(0)

    @pl.when(step == 0)
    def _():
        for tile in range(GRID // LANES):
            wide_ref[tile] = got_ref[:, tile * LANES : (tile + 1) * LANES].astype(f32)
        sums_ref[...] = jnp.zeros_like(sums_ref)
        for odd in range(2):
            for image in range(count):
                start = count * slots + image * 2 + odd
                at = (odd * count + image) * peers
                for tile in range(GRID // LANES):
                    part = wide_ref[tile, pl.ds(start, peers, stride=stride), :]
                    extra_ref[at : at + peers, tile * LANES : (tile + 1) * LANES] = part.astype(bf16)

    for image in range(count):
        span = slice(image * peers, (image + 1) * peers)
        sums = [sums_ref[chan, span, :] for chan in range(CHANS)]
        for at in range(chunk):
            slot = step * chunk + at
            for tile in range(GRID // LANES):
                part = wide_ref[tile, pl.ds(image * slots + slot, peers, stride=stride), :]
                rows_ref[at, span, tile * LANES : (tile + 1) * LANES] = part.astype(bf16)
                for chan in range(CHANS):
                    at_rows = slice(chan * images + image * peers, chan * images + (image + 1) * peers)
                    lanes = slice(tile * LANES, (tile + 1) * LANES)
                    sums[chan] = sums[chan] + part * slice_ref[slot, at_rows, lanes].astype(f32)
        for chan in range(CHANS):
            sums_ref[chan, span, :] = sums[chan]

    @pl.when(step == pl.num_programs(0) - 1)
    def _():
        lane = iota((images, LANES), 1)
        total = gram_ref[...]
        for chan in range(CHANS):
            value = jnp.sum(sums_ref[chan], axis=1, keepdims=True)
            total = jnp.where(lane == PROJECT_AT + chan, value, total)
        total_ref[...] = total


def solve_rows(table, noise):
    count = float(GRID * GRID)

    def gram(k, l):
        at = PAIRS.index((min(k, l), max(k, l)))
        return table[at : at + 1, :]

    factor = [[None] * COMPS for _ in range(COMPS)]
    inverse = [None] * COMPS
    for col in range(COMPS):
        for row in range(col, COMPS):
            total = gram(row + 1, col + 1) / count
            if row == col:
                total = total + noise
            for at in range(col):
                total = total - factor[row][at] * factor[col][at]
            if row == col:
                inverse[col] = 1.0 / jnp.sqrt(total)
            else:
                factor[row][col] = total * inverse[col]
    forward = []
    for row in range(COMPS):
        at = PROJECT_AT + row + 1
        total = (table[at : at + 1, :] - gram(row + 1, 0)) / count
        for col in range(row):
            total = total - factor[row][col] * forward[col]
        forward.append(total * inverse[row])
    latent = [None] * COMPS
    for row in reversed(range(COMPS)):
        total = forward[row]
        for col in range(row + 1, COMPS):
            total = total - factor[col][row] * latent[col]
        latent[row] = total * inverse[row]
    return latent


def back_kernel(
    sizes, place_ref, part_ref, other_ref, every_ref,
    slice_ref, rows_ref, slice_extra_ref, rows_extra_ref, _,
    out_ref, latent_ref, reached_ref, reached_sem, stack_ref, row_ref, power_ref, tilt_ref, col_ref, free_ref, spill_ref, order_ref,
    depth_ref, share_at_ref, share_ref, combine_ref,
):
    planes, slots, blocks, chunk, images, steps, out_planes = sizes
    step, first = pl.program_id(0), place_ref[0]
    group = 2 if blocks % 16 else 1

    @pl.when(step == 0)
    def _():
        table = jnp.transpose(part_ref[...] + other_ref[...])
        tilt, frac, noise = parameter_rows(every_ref, images)
        latent = solve_rows(table, noise)
        free_ref[...] = columns(latent)
        count = latent_ref.shape[0]
        for image in range(count):
            at = image * (images // count) + place_ref[1]
            latent_ref[image : image + 1, :] = free_ref[pl.ds(at, 1), :COMPS]
        rounded = [value.astype(bf16).astype(f32) for value in latent]
        power = rounded[0] * rounded[0]
        for value in rounded[1:]:
            power = power + value * value
        rows = jnp.concatenate(rounded + [power, power], axis=0)
        row_ref[...] = jnp.concatenate([rows, rows, rows], axis=1).astype(bf16)
        power_ref[...] = jnp.concatenate([power, power], axis=1)
        tilt_ref[...] = jnp.concatenate([tilt, tilt, tilt], axis=1).astype(i32)
        col_ref[...] = columns(rounded + [power, tilt, frac])
        one = jnp.ones((1, images), f32)
        same = iota((images, images), 0) == iota((images, images), 1)
        parts = [jnp.where(same, value, 0.0) for value in [one] + rounded]
        combine_ref[...] = jnp.concatenate(parts, axis=1).astype(bf16)
        col = iota((WINDOW, GRID), 1)
        order_ref[...] = (col % blocks) * slots + col // blocks - iota((WINDOW, GRID), 0)

    def spread(total, rows, weight):
        residual = rows.astype(f32) - total
        return interpolate(residual.astype(bf16).astype(f32), weight, 1)

    weight = col_ref[:, COMPS + 2 : COMPS + 3] / 16.0

    @pl.when(step == 0)
    def _():
        latent = jnp.concatenate([col_ref[...]] * 2, axis=0)
        total = slice_extra_ref[:, :GRID].astype(f32)
        for k in range(COMPS):
            span = slice((k + 1) * GRID, (k + 2) * GRID)
            total = total + latent[:, k : k + 1] * slice_extra_ref[:, span].astype(f32)
        value = spread(total, rows_extra_ref[...], jnp.concatenate([weight, weight], axis=0))
        tilt = col_ref[:, COMPS + 1 : COMPS + 2].astype(i32)
        plane, depth = plane_depth(iota((images, GRID), 1), tilt)
        odd = jnp.bitwise_and(iota((images, GRID), 1), 1)
        for at in range(2):
            hit = (plane == first - 1) & (odd == at)
            part = jnp.sum(jnp.where(hit, depth, 0).astype(f32), axis=1, keepdims=True) / HALF
            span = slice(at * images, (at + 1) * images)
            spill_ref[span, :] = (part * value[span]).astype(bf16)
        slot_at = iota((images, LANES), 1)
        depths = jnp.zeros((images, LANES), f32)
        for block in range(blocks):
            plane, depth = plane_depth(block * slots + slot_at, tilt)
            live = (plane >= first) & (plane < first + planes)
            depths = depths + jnp.where(live, depth, 0).astype(f32)
        depth_ref[...] = depths / HALF
        shape = (GRID, 2 * images)
        low = iota(shape, 1) < images
        plane, depth = plane_depth(iota(shape, 0), tilt_ref[:, : 2 * images])
        share_at_ref[...] = jnp.where(low, plane, plane + 1)
        share_ref[...] = jnp.where(low, HALF - depth, depth).astype(f32) / HALF * power_ref[:, : 2 * images]

    @pl.when(step < steps)
    def _():
        tilt = tilt_ref[...]
        row = iota((blocks, 3 * images), 0)
        base = (row * slots - HALF) * tilt
        shape = (planes, blocks, 3 * images)
        plane_at, lane = iota(shape, 0), iota(shape, 2)
        wanted = jnp.where(lane < images, plane_at, plane_at - 1)
        wanted = jnp.where((lane < 2 * images) == (wanted < 0), -1000, wanted) + (first - HALF)
        depths = pltpu.roll(depth_ref[...], (LANES - step * chunk) % LANES, 1)
        rights, hits = [], []
        for at in range(chunk):
            slot = step * chunk + at
            value = spread(dot(combine_ref[...], slice_ref[slot]), rows_ref[at], weight)
            depth = depths[:, at : at + 1]
            odd = pl.ds(pl.multiple_of((slot % 2) * images, 16), images)
            low, high = ((1.0 - depth) * value).astype(bf16), (depth * value).astype(bf16)
            rights.append(jnp.concatenate([low, high, spill_ref[odd, :]], axis=0))
            plane = jnp.right_shift(base + slot * tilt, 7)
            hit = jnp.where(plane[None] == wanted, 1.0, 0.0)
            hits.append(hit.reshape(planes * blocks, 3 * images).astype(bf16))
        for start in range(0, chunk, group):
            pieces = [[] for _ in range(COMPS)]
            for at in range(start, start + group):
                left = jnp.concatenate([hits[at] * row_ref[k : k + 1, :] for k in range(COMPS)], axis=0)
                totals = dot(left, rights[at])
                for k in range(COMPS):
                    total = totals[k * planes * blocks : (k + 1) * planes * blocks]
                    pieces[k].append(total.reshape(planes, blocks, GRID))
            rows = pl.ds(pl.multiple_of((step * chunk + start) * blocks, 16), group * blocks)
            for k in range(COMPS):
                stack_ref[k, :, rows, :] = jnp.concatenate(pieces[k], axis=1).astype(bf16)

    def stores(plane):
        copies = []
        for n, start in enumerate(reached_starts(first + plane - HALF)):
            rows = pl.ds(pl.multiple_of(plane * GRID + start, 16), WINDOW)
            part = reached_ref.at[plane, :, pl.ds(n * WINDOW, WINDOW)]
            copies.append(pltpu.make_async_copy(part, out_ref.at[:, rows], reached_sem.at[2 * plane + n]))
        return copies

    @pl.when(step >= steps)
    def _():
        for at in range(out_planes):
            plane = (step - steps) * out_planes + at
            orders, shares = [], []
            for start in reached_starts(first + plane - HALF):
                rows = pl.ds(pl.multiple_of(start, 16), WINDOW)
                orders.append(jnp.where(order_ref[...] == start, 1.0, 0.0))
                shares.append(jnp.where(share_at_ref[rows, :] == first + plane, share_ref[rows, :], 0.0))
            order = jnp.concatenate(orders, axis=0).astype(bf16)
            share = jnp.concatenate(shares, axis=0)
            scale = 1.0 / (1.0 + jnp.sum(share, axis=1, keepdims=True))
            for k in range(COMPS):
                reached_ref[plane, k] = (dot(order, stack_ref[k, plane]) * scale).astype(bf16)
            for copy in stores(plane):
                copy.start()

    @pl.when(step == pl.num_programs(0) - 1)
    def _():
        for plane in range(planes):
            for copy in stores(plane):
                copy.wait()


def whole(shape):
    return pl.BlockSpec(shape, lambda *_: (0,) * len(shape))


def anywhere():
    return pl.BlockSpec(memory_space=pl.ANY)


def in_hbm(value):
    return pltpu.with_memory_space_constraint(value, pltpu.HBM)


def hbm():
    return pl.BlockSpec(memory_space=pltpu.HBM)


def smem():
    return pl.BlockSpec(memory_space=pltpu.SMEM)


def local(mean_volume, components, images, tilt, shift, frac, noise_var):
    peers = lax.axis_size("slab")
    me = lax.axis_index("slab")
    planes = mean_volume.shape[0] // GRID
    slots = 2 * planes
    blocks = GRID // slots
    count = images.shape[0]
    total = peers * count
    width = CHANS * GRID
    chunk = max(1, 256 // total)
    steps = slots // chunk
    pack_rows = count * slots + 2 * count
    upper_rows = -(-blocks // 16) * 16
    place = jnp.stack([me * planes, me]).astype(i32)

    mine = jnp.concatenate([tilt.astype(f32), frac.astype(f32), noise_var])
    mine = jnp.broadcast_to(jnp.pad(mine, (0, LANES - 3 * count)), (peers, 8, LANES))
    every = lax.all_to_all(mine, "slab", split_axis=0, concat_axis=0, tiled=True)

    wide = 2 * WINDOW
    top = planes - 1
    near, far = pl.pallas_call(
        functools.partial(edges_kernel, planes),
        out_shape=[jax.ShapeDtypeStruct((CHANS, wide, GRID), bf16)] * 2,
        grid=(1,),
        in_specs=[
            smem(),
            pl.BlockSpec((GRID, GRID), lambda n: (0, 0)),
            pl.BlockSpec((COMPS, GRID, GRID), lambda n: (0, 0, 0)),
            pl.BlockSpec((GRID, GRID), lambda n: (top, 0)),
            pl.BlockSpec((COMPS, GRID, GRID), lambda n: (0, top, 0)),
        ],
        out_specs=[whole((CHANS, wide, GRID))] * 2,
        compiler_params=params(56),
        cost_estimate=pl.CostEstimate(flops=0, bytes_accessed=6 * CHANS * wide * GRID, transcendentals=0),
        name="edges",
    )(place, mean_volume, components, mean_volume, components)
    near = lax.ppermute(near, "slab", [(n, n ^ 1) for n in range(peers)])
    far = lax.ppermute(far, "slab", [(n, n + 1 if n % 2 else n - 1) for n in range(1, peers - 1)])

    packed = pl.pallas_call(
        functools.partial(pack_kernel, (planes, slots, peers, count)),
        out_shape=jax.ShapeDtypeStruct((peers, pack_rows, GRID), bf16),
        in_specs=[smem(), smem(), whole((count * GRID, GRID))],
        out_specs=whole((peers, pack_rows, GRID)),
        scratch_shapes=[pltpu.VMEM((count * GRID, GRID), bf16)],
        grid=(1,),
        compiler_params=params(56),
        cost_estimate=pl.CostEstimate(
            flops=0, bytes_accessed=2 * (count * GRID + peers * pack_rows) * GRID, transcendentals=0
        ),
        name="pack",
    )(tilt, shift, images.reshape(count * GRID, GRID))
    packed = pl.pallas_call(
        after_kernel,
        out_shape=pltpu.HBM(packed.shape, bf16),
        in_specs=[hbm()] + [pl.BlockSpec(memory_space=pltpu.VMEM)] * 3,
        out_specs=hbm(),
        input_output_aliases={0: 0},
        compiler_params=params(4),
        name="after",
    )(in_hbm(packed), *(pltpu.with_memory_space_constraint(value, pltpu.VMEM) for value in (every, near, far)))
    got = lax.all_to_all(packed, "slab", split_axis=0, concat_axis=0, tiled=True)

    pair = 2 if blocks % 16 else 1
    tables = planes // pair
    table_rows = -(-(planes + 1) * blocks // 16) * 16
    slices, slices_extra, gram, blank = pl.pallas_call(
        functools.partial(extract_kernel, (planes, slots, blocks, chunk, total, pair)),
        out_shape=[
            pltpu.HBM((slots, CHANS * total, GRID), bf16),
            jax.ShapeDtypeStruct((2 * total, width), bf16),
            jax.ShapeDtypeStruct((total, LANES), f32),
            jax.ShapeDtypeStruct((COMPS, planes * GRID, GRID), bf16),
        ],
        grid=(tables + steps,),
        in_specs=[
            smem(),
            whole((peers, 8, LANES)),
            anywhere(),
            anywhere(),
            hbm(),
            hbm(),
        ],
        out_specs=[
            pl.BlockSpec((chunk, CHANS * total, GRID), lambda n: (jnp.maximum(n - tables, 0), 0, 0)),
            whole((2 * total, width)),
            whole((total, LANES)),
            anywhere(),
        ],
        scratch_shapes=[
            pltpu.VMEM((CHANS, wide, GRID), bf16),
            pltpu.VMEM((CHANS, wide, GRID), bf16),
            pltpu.SemaphoreType.DMA((2,)),
            pltpu.VMEM((COMPS, GRID, GRID), bf16),
            pltpu.SemaphoreType.DMA((planes,)),
            pltpu.VMEM((planes * GRID, GRID), bf16),
            pltpu.VMEM((COMPS, planes * GRID, GRID), bf16),
            pltpu.SemaphoreType.DMA((tables,)),
            pltpu.SemaphoreType.DMA((tables,)),
            pltpu.VMEM((slots, table_rows, width), bf16),
            pltpu.VMEM((GRID, GRID), bf16),
            pltpu.VMEM((len(PAIRS), total, LANES), f32),
            pltpu.VMEM((total, LANES), f32),
        ],
        compiler_params=params(44),
        name="extract",
    )(place, every, mean_volume, components, in_hbm(near), in_hbm(far))

    rows, rows_extra, partial = pl.pallas_call(
        functools.partial(project_kernel, (slots, chunk, total, peers, count)),
        out_shape=[
            jax.ShapeDtypeStruct((slots, total, GRID), bf16),
            jax.ShapeDtypeStruct((2 * total, GRID), bf16),
            jax.ShapeDtypeStruct((total, LANES), f32),
        ],
        grid=(steps,),
        in_specs=[
            whole((peers * pack_rows, GRID)),
            pl.BlockSpec(memory_space=pltpu.VMEM),
            whole((total, LANES)),
        ],
        out_specs=[
            pl.BlockSpec((chunk, total, GRID), lambda n: (n, 0, 0)),
            whole((2 * total, GRID)),
            whole((total, LANES)),
        ],
        scratch_shapes=[
            pltpu.VMEM((GRID // LANES, peers * pack_rows, LANES), f32),
            pltpu.VMEM((CHANS, total, LANES), f32),
        ],
        compiler_params=params(24),
        name="project",
    )(
        got.reshape(peers * pack_rows, GRID),
        pltpu.with_memory_space_constraint(slices, pltpu.VMEM),
        gram,
    )

    step = 1
    while step < peers // 2:
        partial = partial + lax.ppermute(partial, "slab", [(n, n ^ step) for n in range(peers)])
        step *= 2
    halves = partial, lax.ppermute(partial, "slab", [(n, n ^ step) for n in range(peers)])

    out_planes = 2
    last = steps - 1
    new_components, latents = pl.pallas_call(
        functools.partial(back_kernel, (planes, slots, blocks, chunk, total, steps, out_planes)),
        out_shape=[
            jax.ShapeDtypeStruct((COMPS, planes * GRID, GRID), bf16),
            jax.ShapeDtypeStruct((count, COMPS), f32),
        ],
        grid=(steps + planes // out_planes,),
        in_specs=[
            smem(),
            whole((total, LANES)),
            whole((total, LANES)),
            whole((peers, 8, LANES)),
            pl.BlockSpec(memory_space=pltpu.VMEM),
            pl.BlockSpec((chunk, total, GRID), lambda n: (jnp.minimum(n, last), 0, 0)),
            whole((2 * total, width)),
            whole((2 * total, GRID)),
            anywhere(),
        ],
        out_specs=[
            anywhere(),
            whole((count, COMPS)),
        ],
        scratch_shapes=[
            pltpu.VMEM((planes, COMPS, 2 * WINDOW, GRID), bf16),
            pltpu.SemaphoreType.DMA((2 * planes,)),
            pltpu.VMEM((COMPS, planes, GRID, GRID), bf16),
            pltpu.VMEM((8, 3 * total), bf16),
            pltpu.VMEM((1, 2 * total), f32),
            pltpu.VMEM((1, 3 * total), i32),
            pltpu.VMEM((total, LANES), f32),
            pltpu.VMEM((total, LANES), f32),
            pltpu.VMEM((2 * total, GRID), bf16),
            pltpu.VMEM((WINDOW, GRID), i32),
            pltpu.VMEM((total, LANES), f32),
            pltpu.VMEM((GRID, 2 * total), i32),
            pltpu.VMEM((GRID, 2 * total), f32),
            pltpu.VMEM((total, CHANS * total), bf16),
        ],
        input_output_aliases={8: 0},
        compiler_params=params(29),
        name="back",
    )(place, *halves, every, pltpu.with_memory_space_constraint(slices, pltpu.VMEM), rows, slices_extra, rows_extra, blank)
    return new_components, latents


def solution(mesh):
    placed = (
        P(("groups", "slab"), None),
        P(None, ("groups", "slab"), None),
        P(("groups", "slab"), None, None),
        P(("groups", "slab")),
        P(("groups", "slab")),
        P(("groups", "slab")),
        P(("groups", "slab")),
    )
    return jax.shard_map(
        local,
        mesh=mesh,
        in_specs=placed,
        out_specs=(P(None, ("groups", "slab"), None), P(("groups", "slab"), None)),
        check_vma=False,
    )
```

```python
import functools

import jax
import jax.numpy as jnp
from jax import lax
from jax.experimental import pallas as pl
from jax.experimental.pallas import tpu as pltpu
from jax.sharding import PartitionSpec as P

GRID = 256
HALF = GRID // 2
COMPS = 6
CHANS = COMPS + 1
TILE = 128
LANES = 128
PAIRS = [(k, l) for k in range(CHANS) for l in range(k, CHANS + 1)]
NOISE_AT = len(PAIRS)

f32 = jnp.float32
bf16 = jnp.bfloat16
i32 = jnp.int32


def iota(shape, dim):
    return lax.broadcasted_iota(i32, shape, dim)


def dot(a, b):
    return jnp.dot(a, b, preferred_element_type=f32)


def params(mebibytes):
    return pltpu.CompilerParams(vmem_limit_bytes=mebibytes * 1024 * 1024)


def plane_depth(position, tilt):
    numerator = (position - HALF) * tilt
    return jnp.right_shift(numerator, 7) + HALF, jnp.bitwise_and(numerator, HALF - 1)


PARAMETERS = 8


def pack_kernel(sizes, tilt_ref, shift_ref, frac_ref, image_ref, out_ref, turned_ref):
    planes, slots, peers, count = sizes
    main_rows = count * slots
    shape = (peers * slots, GRID)
    row, col = iota(shape, 0), iota(shape, 1)
    slot_hit = jnp.bitwise_and(row - col, slots - 1) == 0
    first_hit = jnp.where(slot_hit, row // slots * planes, -1)
    for image in range(count):
        rows = slice(image * GRID, (image + 1) * GRID)
        for at in range(GRID // TILE):
            span = slice(at * TILE, (at + 1) * TILE)
            part = image_ref[rows, span].astype(f32)
            turned_ref[rows, span] = pltpu.roll(part, shift_ref[image], 1).astype(bf16)
        plane, _ = plane_depth(iota((1, GRID), 1), tilt_ref[image])
        hit = jnp.bitwise_and(plane, -planes) == first_hit
        found = dot(jnp.where(hit, 1.0, 0.0).astype(bf16), turned_ref[rows, :])
        found = found.reshape(peers, slots, GRID).astype(bf16)
        out_ref[:, image * slots : (image + 1) * slots, :] = found
    lane = iota((1, count * GRID), 1)
    tilt = jnp.full((1, count * GRID), tilt_ref[0], i32)
    for image in range(1, count):
        tilt = jnp.where(lane >= image * GRID, tilt_ref[image], tilt)
    plane, _ = plane_depth(jnp.bitwise_and(lane, GRID - 1), tilt)
    shape = (peers * 2 * count, count * GRID)
    row, col = iota(shape, 0), iota(shape, 1)
    hit = (row // 2 % count == col // GRID) & (row % 2 == col % 2)
    hit = hit & (plane == row // (2 * count) * planes - 1)
    found = dot(jnp.where(hit, 1.0, 0.0).astype(bf16), turned_ref[...])
    found = found.reshape(peers, 2 * count, GRID)
    row, lane = iota((PARAMETERS, GRID), 0), iota((PARAMETERS, GRID), 1)
    values = jnp.zeros((PARAMETERS, GRID), f32)
    for image in range(count):
        value = jnp.where(lane == 0, tilt_ref[image], jnp.where(lane == 1, frac_ref[image], 0))
        values = jnp.where(row == image, value.astype(f32), values)
    values = jnp.broadcast_to(values[None], (peers, PARAMETERS, GRID))
    out_ref[:, main_rows:, :] = jnp.concatenate([found, values], axis=1).astype(bf16)


def slot_order(slots, blocks):
    row, col = iota((GRID, GRID), 0), iota((GRID, GRID), 1)
    return (col == (row % blocks) * slots + row // blocks).astype(f32).astype(bf16)


WINDOW = 80
MIDDLE = 32


def window_starts(boundary):
    away = jnp.abs(boundary)
    nearest = jnp.where(boundary > 0, away - 1, away)
    furthest = jnp.minimum(jnp.where(boundary > 0, 2 * away - 1, 2 * away + 2), HALF)
    low = (HALF - furthest) // 16 * 16
    high = jnp.minimum((HALF + nearest) // 16 * 16, GRID - WINDOW)
    return low, high


def window_rows(boundary):
    low, high = window_starts(boundary)
    lane = iota((1, 2 * WINDOW + MIDDLE), 1)
    off_middle = boundary != 0
    below = jnp.where(off_middle & (low + lane < HALF), low + lane, -1)
    above = high + lane - WINDOW
    above = jnp.where(off_middle & (above >= HALF), above, -1)
    middle = jnp.where(off_middle, -1, HALF - MIDDLE // 2 + lane - 2 * WINDOW)
    return jnp.where(lane < WINDOW, below, jnp.where(lane < 2 * WINDOW, above, middle))


def reached_starts(distance):
    away = jnp.abs(distance)
    nearest = jnp.where(away > 1, away, 0)
    furthest = jnp.minimum(2 * away + 2, HALF)
    low = jnp.minimum((HALF - furthest) // 16 * 16, HALF - 32)
    high = jnp.minimum(jnp.maximum((HALF + nearest) // 16 * 16, low + WINDOW), GRID - WINDOW)
    return low, high


def edges_kernel(
    planes, place_ref, mean_ref, comp_ref, mean_top_ref, comp_top_ref, near_ref, far_ref, middle_ref
):
    bottom = place_ref[0] - HALF
    even = place_ref[1] % 2 == 0

    def fill(boundary, mean, comp, out):
        for chan in range(CHANS):
            plane = mean if chan == 0 else comp.at[chan - 1]
            for n, start in enumerate(window_starts(boundary)):
                rows = pl.ds(pl.multiple_of(start, 16), WINDOW)
                out[chan, n * WINDOW : (n + 1) * WINDOW, :] = plane[rows, :]
            if out is far_ref:
                middle_ref[chan] = plane[HALF - MIDDLE // 2 : HALF + MIDDLE // 2, :]

    @pl.when(even)
    def _():
        fill(bottom + planes, mean_top_ref, comp_top_ref, near_ref)
        fill(bottom, mean_ref, comp_ref, far_ref)

    @pl.when(jnp.logical_not(even))
    def _():
        fill(bottom, mean_ref, comp_ref, near_ref)
        fill(bottom + planes, mean_top_ref, comp_top_ref, far_ref)


def stream(step, parts, copies):
    @pl.when(step == 0)
    def _():
        for part in range(parts):
            for copy in copies(part):
                copy.start()

    @pl.when(step < parts)
    def _():
        for copy in copies(step):
            copy.wait()


def columns(rows):
    fill = jnp.zeros((LANES - len(rows), rows[0].shape[1]), f32)
    return jnp.transpose(jnp.concatenate(rows + [fill], axis=0))


def interpolate(rows, weight, turn):
    parts = []
    for at in range(GRID // TILE):
        part = rows[:, at * TILE : (at + 1) * TILE]
        parts.append((1.0 - weight) * part + weight * pltpu.roll(part, turn, 1))
    return jnp.concatenate(parts, axis=1)


def table_kernel(
    sizes, place_ref, mean_hbm, comp_hbm, out_ref, blank_ref,
    mean_ref, comp_ref, mean_sem, comp_sem, order_ref, zero_ref, zero_sem,
):
    planes, slots, blocks, pair = sizes
    step, first = pl.program_id(0), place_ref[0]
    tables = planes // pair

    def copies(part):
        rows = pl.ds(pl.multiple_of(part * pair * GRID, GRID), pair * GRID)
        return (
            pltpu.make_async_copy(mean_hbm.at[rows], mean_ref.at[rows], mean_sem.at[part]),
            pltpu.make_async_copy(comp_hbm.at[:, rows], comp_ref.at[:, rows], comp_sem.at[part]),
        )

    def blanks(plane):
        low, high = reached_starts(first + plane - HALF)
        parts = []
        for n in range((GRID - 2 * WINDOW) // 16):
            start = jnp.where(n * 16 >= low, n * 16 + WINDOW, n * 16)
            start = jnp.where(start >= high, start + WINDOW, start)
            rows = pl.ds(pl.multiple_of(plane * GRID + start, 16), 16)
            parts.append(pltpu.make_async_copy(zero_ref, blank_ref.at[:, rows], zero_sem.at[plane, n]))
        return parts

    @pl.when(step == 0)
    def _():
        zero_ref[...] = jnp.zeros_like(zero_ref)
        order_ref[...] = slot_order(slots, blocks)

    stream(step, tables, copies)
    for at in range(pair):
        for copy in blanks(step * pair + at):
            copy.start()
    order = order_ref[...]
    for chan in range(CHANS):
        pieces = []
        for at in range(pair):
            span = pl.ds(pl.multiple_of((step * pair + at) * GRID, GRID), GRID)
            plane = mean_ref[span, :] if chan == 0 else comp_ref[chan - 1, span, :]
            pieces.append(dot(order, plane).reshape(slots, blocks, GRID))
        out_ref[:, :, chan * GRID : (chan + 1) * GRID] = jnp.concatenate(pieces, axis=1).astype(bf16)

    @pl.when(step == tables - 1)
    def _():
        for plane in range(planes):
            for copy in blanks(plane):
                copy.wait()


def extract_kernel(
    sizes, place_ref, noise_ref, got_hbm, near_hbm, far_hbm, middle_hbm, mean_hbm, comp_hbm, table_hbm,
    out_ref, rows_ref, extra_ref, rows_extra_ref, total_ref, column_ref,
    got_ref, near_ref, far_ref, middle_ref, own_ref, table_ref, edge_sem, table_sem,
    wide_ref, upper_ref, sums_ref,
):
    planes, slots, blocks, chunk, images, peers = sizes
    step, first = pl.program_id(0), place_ref[0]
    count = images // peers
    stride = count * slots + 2 * count + PARAMETERS
    one_plane = pl.ds(0, GRID)
    edges = (
        pltpu.make_async_copy(got_hbm, got_ref, edge_sem.at[0]),
        pltpu.make_async_copy(near_hbm, near_ref, edge_sem.at[1]),
        pltpu.make_async_copy(far_hbm, far_ref, edge_sem.at[2]),
        pltpu.make_async_copy(middle_hbm, middle_ref, edge_sem.at[3]),
        pltpu.make_async_copy(mean_hbm.at[one_plane], own_ref.at[0], edge_sem.at[4]),
        pltpu.make_async_copy(comp_hbm.at[:, one_plane], own_ref.at[pl.ds(1, COMPS)], edge_sem.at[5]),
    )

    def copies(part):
        at = pl.ds(part * chunk, chunk)
        return (pltpu.make_async_copy(table_hbm.at[at], table_ref.at[at], table_sem.at[part]),)

    @pl.when(step == 0)
    def _():
        for copy in edges:
            copy.start()

    @pl.when(step == 0)
    def _():
        for part in range(slots // chunk):
            copies(part)[0].start()
        edges[0].wait()
        for tile in range(GRID // LANES):
            wide_ref[tile] = got_ref[:, tile * LANES : (tile + 1) * LANES].astype(f32)
        for image in range(count):
            span = slice(image * peers, (image + 1) * peers)
            start = stride - PARAMETERS + image
            column_ref[span, :] = wide_ref[0, pl.ds(start, peers, stride=stride), :]
            for odd in range(2):
                start = count * slots + image * 2 + odd
                at = (odd * count + image) * peers
                for tile in range(GRID // LANES):
                    part = wide_ref[tile, pl.ds(start, peers, stride=stride), :]
                    rows_extra_ref[at : at + peers, tile * LANES : (tile + 1) * LANES] = part.astype(bf16)
        sums_ref[...] = jnp.zeros_like(sums_ref)
        for copy in edges[1:]:
            copy.wait()

    @pl.when(step < slots // chunk)
    def _():
        copies(step)[0].wait()

    tilt = column_ref[:, 0:1].astype(i32)
    weight = column_ref[:, 1:2] / 16.0

    @pl.when(step == 0)
    def _():
        at_up, at_low = window_rows(first + planes - HALF), window_rows(first - HALF)
        row = iota((GRID, at_up.shape[1]), 0)
        order = (at_up == (row % blocks) * slots + row // blocks).astype(f32).astype(bf16)
        parts = []
        for odd in range(2):
            pieces = []
            for lane, part in ((at_low, 0), (iota((1, GRID), 1), 1)):
                plane, depth = plane_depth(lane, tilt)
                hit = (plane == first - 1) & (lane >= 0) & (jnp.bitwise_and(lane, 1) == odd)
                depth = depth if part else HALF - depth
                pieces.append(jnp.where(hit, depth, 0).astype(f32) / HALF)
            parts.append(pieces)
        mixing_low = jnp.concatenate([parts[0][0], parts[1][0]], axis=0).astype(bf16)
        mixing_own = jnp.concatenate([parts[0][1], parts[1][1]], axis=0).astype(bf16)
        weight2 = jnp.concatenate([weight, weight], axis=0)
        fill = upper_ref.shape[1] - blocks
        even = place_ref[1] % 2 == 0
        for chan in range(CHANS):
            at = slice(chan * GRID, (chan + 1) * GRID)
            near, far, middle = near_ref[chan], far_ref[chan], middle_ref[chan]
            upper = jnp.concatenate([jnp.where(even, near, far), middle], axis=0)
            upper = dot(order, upper).reshape(slots, blocks, GRID)
            if fill:
                upper = jnp.concatenate([upper, jnp.zeros((slots, fill, GRID), f32)], axis=1)
            upper_ref[:, :, at] = upper.astype(bf16)
            lower = jnp.concatenate([jnp.where(even, far, near), middle], axis=0)
            blended = dot(mixing_low, lower) + dot(mixing_own, own_ref[chan])
            blended = blended.astype(bf16).astype(f32)
            extra_ref[:, at] = interpolate(blended, weight2, TILE - 1).astype(bf16)

    lane = iota((images, planes * blocks + upper_ref.shape[1]), 1)
    block_at, plane_at = lane % blocks, lane // blocks
    plane_at = jnp.where(plane_at > planes, -1000, plane_at) + first
    low_at = jnp.where(plane_at < first + planes, plane_at, -1000)
    high_at = jnp.where(plane_at > first, plane_at - 1, -1000)
    base = (block_at * slots - HALF) * tilt
    for at in range(chunk):
        slot = step * chunk + at
        for image in range(count):
            span = slice(image * peers, (image + 1) * peers)
            for tile in range(GRID // LANES):
                part = wide_ref[tile, pl.ds(image * slots + slot, peers, stride=stride), :]
                rows_ref[at, span, tile * LANES : (tile + 1) * LANES] = part.astype(bf16)
        numerator = base + slot * tilt
        plane, depth = jnp.right_shift(numerator, 7) + HALF, jnp.bitwise_and(numerator, HALF - 1)
        mixing = jnp.where(plane == low_at, HALF - depth, jnp.where(plane == high_at, depth, 0))
        mixing = (mixing.astype(f32) * (1.0 / HALF)).astype(bf16)
        for chan in range(CHANS):
            span = slice(chan * GRID, (chan + 1) * GRID)
            right = jnp.concatenate([table_ref[slot, :, span], upper_ref[slot, :, span]], axis=0)
            part = dot(mixing, right).astype(bf16).astype(f32)
            part = interpolate(part, weight, TILE - 1).astype(bf16)
            out_ref[at, chan * images : (chan + 1) * images, :] = part
    gram_sums(chunk, images, out_ref, rows_ref, sums_ref)

    @pl.when(step == pl.num_programs(0) - 1)
    def _():
        row, lane = iota((images, LANES), 0), iota((images, LANES), 1)
        total = own_products(images, sums_ref)
        for image in range(count):
            mine = (lane == NOISE_AT) & (row == image * peers + place_ref[1])
            total = jnp.where(mine, noise_ref[image], total)
        total_ref[...] = total


def gram_sums(chunk, images, out_ref, rows_ref, sums_ref):
    for group in range(images // 16):
        start = group * 16
        slots = []
        for at in range(chunk):
            rows = [out_ref[at, chan * images + start : chan * images + start + 16, :] for chan in range(CHANS)]
            rows.append(rows_ref[at, start : start + 16, :])
            slots.append(jnp.concatenate(rows, axis=0))
        block = jnp.concatenate(slots, axis=1)
        product = lax.dot_general(block, block, (((1,), (1,)), ((), ())), preferred_element_type=f32)
        sums_ref[group] = sums_ref[group] + product


def own_products(images, sums_ref):
    parts = []
    for group in range(images // 16):
        row, lane = iota((16, LANES), 0), iota((16, LANES), 1)
        total = jnp.zeros((16, LANES), f32)
        for n, (k, l) in enumerate(PAIRS):
            block = sums_ref[group, k * 16 : (k + 1) * 16, :]
            value = jnp.sum(jnp.where(lane == row + l * 16, block, 0.0), axis=1, keepdims=True)
            total = jnp.where(lane == n, value, total)
        parts.append(total)
    return jnp.concatenate(parts, axis=0)


def solve_rows(table, noise):
    count = float(GRID * GRID)

    def gram(k, l):
        at = PAIRS.index((min(k, l), max(k, l)))
        return table[at : at + 1, :]

    factor = [[None] * COMPS for _ in range(COMPS)]
    inverse = [None] * COMPS
    for col in range(COMPS):
        for row in range(col, COMPS):
            total = gram(row + 1, col + 1) / count
            if row == col:
                total = total + noise
            for at in range(col):
                total = total - factor[row][at] * factor[col][at]
            if row == col:
                inverse[col] = 1.0 / jnp.sqrt(total)
            else:
                factor[row][col] = total * inverse[col]
    forward = []
    for row in range(COMPS):
        total = (gram(row + 1, CHANS) - gram(row + 1, 0)) / count
        for col in range(row):
            total = total - factor[row][col] * forward[col]
        forward.append(total * inverse[row])
    latent = [None] * COMPS
    for row in reversed(range(COMPS)):
        total = forward[row]
        for col in range(row + 1, COMPS):
            total = total - factor[col][row] * latent[col]
        latent[row] = total * inverse[row]
    return latent


def back_kernel(
    sizes, place_ref, part_ref, other_ref, column_ref,
    slice_ref, rows_ref, slice_extra_ref, rows_extra_ref, _,
    out_ref, latent_ref, reached_ref, reached_sem, stack_ref, row_ref, power_ref, tilt_ref, col_ref, free_ref, spill_ref, order_ref,
    depth_ref, share_at_ref, share_ref, combine_ref,
):
    planes, slots, blocks, chunk, images, steps, out_planes = sizes
    step, first = pl.program_id(0), place_ref[0]
    group = 2 if blocks % 16 else 1

    @pl.when(step == 0)
    def _():
        table = jnp.transpose(part_ref[...] + other_ref[...])
        values = jnp.transpose(column_ref[...])
        tilt, frac = values[0:1, :], values[1:2, :]
        latent = solve_rows(table, table[NOISE_AT : NOISE_AT + 1, :])
        free_ref[...] = columns(latent)
        count = latent_ref.shape[0]
        for image in range(count):
            at = image * (images // count) + place_ref[1]
            latent_ref[image : image + 1, :] = free_ref[pl.ds(at, 1), :COMPS]
        rounded = [value.astype(bf16).astype(f32) for value in latent]
        power = rounded[0] * rounded[0]
        for value in rounded[1:]:
            power = power + value * value
        rows = jnp.concatenate(rounded + [power, power], axis=0)
        row_ref[...] = jnp.concatenate([rows, rows, rows], axis=1).astype(bf16)
        power_ref[...] = jnp.concatenate([power, power], axis=1)
        tilt_ref[...] = jnp.concatenate([tilt, tilt, tilt], axis=1).astype(i32)
        col_ref[...] = columns(rounded + [power, tilt, frac])
        one = jnp.ones((1, images), f32)
        same = iota((images, images), 0) == iota((images, images), 1)
        parts = [jnp.where(same, value, 0.0) for value in [one] + rounded]
        combine_ref[...] = jnp.concatenate(parts, axis=1).astype(bf16)
        col = iota((WINDOW, GRID), 1)
        order_ref[...] = (col % blocks) * slots + col // blocks - iota((WINDOW, GRID), 0)

    def spread(total, rows, weight):
        residual = rows.astype(f32) - total
        return interpolate(residual.astype(bf16).astype(f32), weight, 1)

    weight = col_ref[:, COMPS + 2 : COMPS + 3] / 16.0

    @pl.when(step == 0)
    def _():
        latent = jnp.concatenate([col_ref[...]] * 2, axis=0)
        total = slice_extra_ref[:, :GRID].astype(f32)
        for k in range(COMPS):
            span = slice((k + 1) * GRID, (k + 2) * GRID)
            total = total + latent[:, k : k + 1] * slice_extra_ref[:, span].astype(f32)
        value = spread(total, rows_extra_ref[...], jnp.concatenate([weight, weight], axis=0))
        tilt = col_ref[:, COMPS + 1 : COMPS + 2].astype(i32)
        plane, depth = plane_depth(iota((images, GRID), 1), tilt)
        odd = jnp.bitwise_and(iota((images, GRID), 1), 1)
        for at in range(2):
            hit = (plane == first - 1) & (odd == at)
            part = jnp.sum(jnp.where(hit, depth, 0).astype(f32), axis=1, keepdims=True) / HALF
            span = slice(at * images, (at + 1) * images)
            spill_ref[span, :] = (part * value[span]).astype(bf16)
        slot_at = iota((images, LANES), 1)
        depths = jnp.zeros((images, LANES), f32)
        for block in range(blocks):
            plane, depth = plane_depth(block * slots + slot_at, tilt)
            live = (plane >= first) & (plane < first + planes)
            depths = depths + jnp.where(live, depth, 0).astype(f32)
        depth_ref[...] = depths / HALF
        shape = (GRID, 2 * images)
        low = iota(shape, 1) < images
        plane, depth = plane_depth(iota(shape, 0), tilt_ref[:, : 2 * images])
        share_at_ref[...] = jnp.where(low, plane, plane + 1)
        share_ref[...] = jnp.where(low, HALF - depth, depth).astype(f32) / HALF * power_ref[:, : 2 * images]

    @pl.when(step < steps)
    def _():
        tilt = tilt_ref[...]
        row = iota((blocks, 3 * images), 0)
        base = (row * slots - HALF) * tilt
        shape = (planes, blocks, 3 * images)
        plane_at, lane = iota(shape, 0), iota(shape, 2)
        wanted = jnp.where(lane < images, plane_at, plane_at - 1)
        wanted = jnp.where((lane < 2 * images) == (wanted < 0), -1000, wanted) + (first - HALF)
        depths = pltpu.roll(depth_ref[...], (LANES - step * chunk) % LANES, 1)
        rights, hits = [], []
        for at in range(chunk):
            slot = step * chunk + at
            value = spread(dot(combine_ref[...], slice_ref[slot]), rows_ref[at], weight)
            depth = depths[:, at : at + 1]
            odd = pl.ds(pl.multiple_of((slot % 2) * images, 16), images)
            low, high = ((1.0 - depth) * value).astype(bf16), (depth * value).astype(bf16)
            rights.append(jnp.concatenate([low, high, spill_ref[odd, :]], axis=0))
            plane = jnp.right_shift(base + slot * tilt, 7)
            hit = jnp.where(plane[None] == wanted, 1.0, 0.0)
            hits.append(hit.reshape(planes * blocks, 3 * images).astype(bf16))
        for start in range(0, chunk, group):
            pieces = [[] for _ in range(COMPS)]
            for at in range(start, start + group):
                left = jnp.concatenate([hits[at] * row_ref[k : k + 1, :] for k in range(COMPS)], axis=0)
                totals = dot(left, rights[at])
                for k in range(COMPS):
                    total = totals[k * planes * blocks : (k + 1) * planes * blocks]
                    pieces[k].append(total.reshape(planes, blocks, GRID))
            rows = pl.ds(pl.multiple_of((step * chunk + start) * blocks, 16), group * blocks)
            for k in range(COMPS):
                stack_ref[k, :, rows, :] = jnp.concatenate(pieces[k], axis=1).astype(bf16)

    def stores(plane):
        copies = []
        for n, start in enumerate(reached_starts(first + plane - HALF)):
            rows = pl.ds(pl.multiple_of(plane * GRID + start, 16), WINDOW)
            part = reached_ref.at[plane, :, pl.ds(n * WINDOW, WINDOW)]
            copies.append(pltpu.make_async_copy(part, out_ref.at[:, rows], reached_sem.at[2 * plane + n]))
        return copies

    @pl.when(step >= steps)
    def _():
        for at in range(out_planes):
            plane = (step - steps) * out_planes + at
            orders, shares = [], []
            for start in reached_starts(first + plane - HALF):
                rows = pl.ds(pl.multiple_of(start, 16), WINDOW)
                orders.append(jnp.where(order_ref[...] == start, 1.0, 0.0))
                shares.append(jnp.where(share_at_ref[rows, :] == first + plane, share_ref[rows, :], 0.0))
            order = jnp.concatenate(orders, axis=0).astype(bf16)
            share = jnp.concatenate(shares, axis=0)
            scale = 1.0 / (1.0 + jnp.sum(share, axis=1, keepdims=True))
            for k in range(COMPS):
                reached_ref[plane, k] = (dot(order, stack_ref[k, plane]) * scale).astype(bf16)
            for copy in stores(plane):
                copy.start()

    @pl.when(step == pl.num_programs(0) - 1)
    def _():
        for plane in range(planes):
            for copy in stores(plane):
                copy.wait()


def whole(shape):
    return pl.BlockSpec(shape, lambda *_: (0,) * len(shape))


def anywhere():
    return pl.BlockSpec(memory_space=pl.ANY)


def in_hbm(value):
    return pltpu.with_memory_space_constraint(value, pltpu.HBM)


def hbm():
    return pl.BlockSpec(memory_space=pltpu.HBM)


def smem():
    return pl.BlockSpec(memory_space=pltpu.SMEM)


def local(mean_volume, components, images, tilt, shift, frac, noise_var):
    peers = lax.axis_size("slab")
    me = lax.axis_index("slab")
    planes = mean_volume.shape[0] // GRID
    slots = 2 * planes
    blocks = GRID // slots
    count = images.shape[0]
    total = peers * count
    width = CHANS * GRID
    chunk = max(1, 1024 // total)
    steps = slots // chunk
    pack_rows = count * slots + 2 * count + PARAMETERS
    place = jnp.stack([me * planes, me]).astype(i32)

    packed = pl.pallas_call(
        functools.partial(pack_kernel, (planes, slots, peers, count)),
        out_shape=jax.ShapeDtypeStruct((peers, pack_rows, GRID), bf16),
        in_specs=[smem(), smem(), smem(), whole((count * GRID, GRID))],
        out_specs=whole((peers, pack_rows, GRID)),
        scratch_shapes=[pltpu.VMEM((count * GRID, GRID), bf16)],
        grid=(1,),
        compiler_params=params(56),
        name="pack",
    )(tilt, shift, frac, images.reshape(count * GRID, GRID))
    got = lax.all_to_all(packed, "slab", split_axis=0, concat_axis=0, tiled=True)

    wide = 2 * WINDOW
    top = planes - 1
    edge_rows = (wide, wide, MIDDLE)
    near, far, middle = pl.pallas_call(
        functools.partial(edges_kernel, planes),
        out_shape=[jax.ShapeDtypeStruct((CHANS, rows, GRID), bf16) for rows in edge_rows],
        grid=(1,),
        in_specs=[
            smem(),
            pl.BlockSpec((GRID, GRID), lambda n: (0, 0)),
            pl.BlockSpec((COMPS, GRID, GRID), lambda n: (0, 0, 0)),
            pl.BlockSpec((GRID, GRID), lambda n: (top, 0)),
            pl.BlockSpec((COMPS, GRID, GRID), lambda n: (0, top, 0)),
        ],
        out_specs=[whole((CHANS, rows, GRID)) for rows in edge_rows],
        compiler_params=params(56),
        name="edges",
    )(place, mean_volume, components, mean_volume, components)
    half = peers // 2
    pairs = [(n, n + 1 if n % 2 else n - 1) for n in range(1, peers - 1) if n not in (half - 1, half)]
    middle = lax.ppermute(middle, "slab", [(half - 1, half), (half, half - 1)])
    near = lax.ppermute(near, "slab", [(n, n ^ 1) for n in range(peers)])
    far = lax.ppermute(far, "slab", pairs)

    pair = 2 if blocks % 16 else 1
    tables = planes // pair
    table, blank = pl.pallas_call(
        functools.partial(table_kernel, (planes, slots, blocks, pair)),
        out_shape=[
            pltpu.HBM((slots, planes * blocks, width), bf16),
            jax.ShapeDtypeStruct((COMPS, planes * GRID, GRID), bf16),
        ],
        grid=(tables,),
        in_specs=[smem(), anywhere(), anywhere()],
        out_specs=[
            pl.BlockSpec((slots, pair * blocks, width), lambda n: (0, n, 0)),
            anywhere(),
        ],
        scratch_shapes=[
            pltpu.VMEM((planes * GRID, GRID), bf16),
            pltpu.VMEM((COMPS, planes * GRID, GRID), bf16),
            pltpu.SemaphoreType.DMA((tables,)),
            pltpu.SemaphoreType.DMA((tables,)),
            pltpu.VMEM((GRID, GRID), bf16),
            pltpu.VMEM((COMPS, 16, GRID), bf16),
            pltpu.SemaphoreType.DMA((planes, (GRID - wide) // 16)),
        ],
        compiler_params=params(30),
        name="table",
    )(place, mean_volume, components)

    slices, rows, slices_extra, rows_extra, partial, columns_all = pl.pallas_call(
        functools.partial(extract_kernel, (planes, slots, blocks, chunk, total, peers)),
        out_shape=[
            jax.ShapeDtypeStruct((slots, CHANS * total, GRID), bf16),
            jax.ShapeDtypeStruct((slots, total, GRID), bf16),
            jax.ShapeDtypeStruct((2 * total, width), bf16),
            jax.ShapeDtypeStruct((2 * total, GRID), bf16),
            jax.ShapeDtypeStruct((total, LANES), f32),
            jax.ShapeDtypeStruct((total, LANES), f32),
        ],
        grid=(steps,),
        in_specs=[smem(), smem()] + [hbm()] * 7,
        out_specs=[
            pl.BlockSpec((chunk, CHANS * total, GRID), lambda n: (n, 0, 0)),
            pl.BlockSpec((chunk, total, GRID), lambda n: (n, 0, 0)),
            whole((2 * total, width)),
            whole((2 * total, GRID)),
            whole((total, LANES)),
            whole((total, LANES)),
        ],
        scratch_shapes=[
            pltpu.VMEM((peers * pack_rows, GRID), bf16),
            pltpu.VMEM((CHANS, wide, GRID), bf16),
            pltpu.VMEM((CHANS, wide, GRID), bf16),
            pltpu.VMEM((CHANS, MIDDLE, GRID), bf16),
            pltpu.VMEM((CHANS, GRID, GRID), bf16),
            pltpu.VMEM((slots, planes * blocks, width), bf16),
            pltpu.SemaphoreType.DMA((6,)),
            pltpu.SemaphoreType.DMA((steps,)),
            pltpu.VMEM((GRID // LANES, peers * pack_rows, LANES), f32),
            pltpu.VMEM((slots, -(-blocks // 16) * 16, width), bf16),
            pltpu.VMEM((total // 16, LANES, LANES), f32),
        ],
        compiler_params=params(40),
        name="extract",
    )(
        place,
        noise_var,
        in_hbm(got.reshape(peers * pack_rows, GRID)),
        in_hbm(near),
        in_hbm(far),
        in_hbm(middle),
        in_hbm(mean_volume),
        in_hbm(components),
        in_hbm(table),
    )

    step = 1
    while step < peers // 2:
        partial = partial + lax.ppermute(partial, "slab", [(n, n ^ step) for n in range(peers)])
        step *= 2
    halves = partial, lax.ppermute(partial, "slab", [(n, n ^ step) for n in range(peers)])

    out_planes = 2
    last = steps - 1
    new_components, latents = pl.pallas_call(
        functools.partial(back_kernel, (planes, slots, blocks, chunk, total, steps, out_planes)),
        out_shape=[
            jax.ShapeDtypeStruct((COMPS, planes * GRID, GRID), bf16),
            jax.ShapeDtypeStruct((count, COMPS), f32),
        ],
        grid=(steps + planes // out_planes,),
        in_specs=[
            smem(),
            whole((total, LANES)),
            whole((total, LANES)),
            whole((total, LANES)),
            pl.BlockSpec(memory_space=pltpu.VMEM),
            pl.BlockSpec((chunk, total, GRID), lambda n: (jnp.minimum(n, last), 0, 0)),
            whole((2 * total, width)),
            whole((2 * total, GRID)),
            anywhere(),
        ],
        out_specs=[
            anywhere(),
            whole((count, COMPS)),
        ],
        scratch_shapes=[
            pltpu.VMEM((planes, COMPS, 2 * WINDOW, GRID), bf16),
            pltpu.SemaphoreType.DMA((2 * planes,)),
            pltpu.VMEM((COMPS, planes, GRID, GRID), bf16),
            pltpu.VMEM((8, 3 * total), bf16),
            pltpu.VMEM((1, 2 * total), f32),
            pltpu.VMEM((1, 3 * total), i32),
            pltpu.VMEM((total, LANES), f32),
            pltpu.VMEM((total, LANES), f32),
            pltpu.VMEM((2 * total, GRID), bf16),
            pltpu.VMEM((WINDOW, GRID), i32),
            pltpu.VMEM((total, LANES), f32),
            pltpu.VMEM((GRID, 2 * total), i32),
            pltpu.VMEM((GRID, 2 * total), f32),
            pltpu.VMEM((total, CHANS * total), bf16),
        ],
        input_output_aliases={8: 0},
        compiler_params=params(29),
        name="back",
    )(place, *halves, columns_all, pltpu.with_memory_space_constraint(slices, pltpu.VMEM), rows, slices_extra, rows_extra, blank)
    return new_components, latents


def solution(mesh):
    placed = (
        P(("groups", "slab"), None),
        P(None, ("groups", "slab"), None),
        P(("groups", "slab"), None, None),
        P(("groups", "slab")),
        P(("groups", "slab")),
        P(("groups", "slab")),
        P(("groups", "slab")),
    )
    return jax.shard_map(
        local,
        mesh=mesh,
        in_specs=placed,
        out_specs=(P(None, ("groups", "slab"), None), P(("groups", "slab"), None)),
        check_vma=False,
    )
```

```python
import functools

import jax
import jax.numpy as jnp
from jax import lax
from jax.experimental import pallas as pl
from jax.experimental.pallas import tpu as pltpu
from jax.sharding import PartitionSpec as P

GRID = 256
HALF = GRID // 2
COMPS = 6
CHANS = COMPS + 1
TILE = 128
LANES = 128
PAIRS = [(k, l) for k in range(CHANS) for l in range(k, CHANS + 1)]
NOISE_AT = len(PAIRS)

f32 = jnp.float32
bf16 = jnp.bfloat16
i32 = jnp.int32


def iota(shape, dim):
    return lax.broadcasted_iota(i32, shape, dim)


def dot(a, b):
    return jnp.dot(a, b, preferred_element_type=f32)


def params(mebibytes):
    return pltpu.CompilerParams(vmem_limit_bytes=mebibytes * 1024 * 1024)


def plane_depth(position, tilt):
    numerator = (position - HALF) * tilt
    return jnp.right_shift(numerator, 7) + HALF, jnp.bitwise_and(numerator, HALF - 1)


PARAMETERS = 8


def pack_kernel(sizes, tilt_ref, shift_ref, frac_ref, image_ref, out_ref, turned_ref):
    planes, slots, peers, count = sizes
    main_rows = count * slots
    shape = (peers * slots, GRID)
    row, col = iota(shape, 0), iota(shape, 1)
    slot_hit = jnp.bitwise_and(row - col, slots - 1) == 0
    first_hit = jnp.where(slot_hit, row // slots * planes, -1)
    for image in range(count):
        rows = slice(image * GRID, (image + 1) * GRID)
        for at in range(GRID // TILE):
            span = slice(at * TILE, (at + 1) * TILE)
            part = image_ref[rows, span].astype(f32)
            turned_ref[rows, span] = pltpu.roll(part, shift_ref[image], 1).astype(bf16)
        plane, _ = plane_depth(iota((1, GRID), 1), tilt_ref[image])
        hit = jnp.bitwise_and(plane, -planes) == first_hit
        found = dot(jnp.where(hit, 1.0, 0.0).astype(bf16), turned_ref[rows, :])
        found = found.reshape(peers, slots, GRID).astype(bf16)
        out_ref[:, image * slots : (image + 1) * slots, :] = found
    lane = iota((1, count * GRID), 1)
    tilt = jnp.full((1, count * GRID), tilt_ref[0], i32)
    for image in range(1, count):
        tilt = jnp.where(lane >= image * GRID, tilt_ref[image], tilt)
    plane, _ = plane_depth(jnp.bitwise_and(lane, GRID - 1), tilt)
    shape = (peers * 2 * count, count * GRID)
    row, col = iota(shape, 0), iota(shape, 1)
    hit = (row // 2 % count == col // GRID) & (row % 2 == col % 2)
    hit = hit & (plane == row // (2 * count) * planes - 1)
    found = dot(jnp.where(hit, 1.0, 0.0).astype(bf16), turned_ref[...])
    found = found.reshape(peers, 2 * count, GRID)
    row, lane = iota((PARAMETERS, GRID), 0), iota((PARAMETERS, GRID), 1)
    values = jnp.zeros((PARAMETERS, GRID), f32)
    for image in range(count):
        value = jnp.where(lane == 0, tilt_ref[image], jnp.where(lane == 1, frac_ref[image], 0))
        values = jnp.where(row == image, value.astype(f32), values)
    values = jnp.broadcast_to(values[None], (peers, PARAMETERS, GRID))
    out_ref[:, main_rows:, :] = jnp.concatenate([found, values], axis=1).astype(bf16)


def slot_order(slots, blocks):
    row, col = iota((GRID, GRID), 0), iota((GRID, GRID), 1)
    return (col == (row % blocks) * slots + row // blocks).astype(f32).astype(bf16)


WINDOW = 80
MIDDLE = 32


def window_starts(boundary):
    away = jnp.abs(boundary)
    nearest = jnp.where(boundary > 0, away - 1, away)
    furthest = jnp.minimum(jnp.where(boundary > 0, 2 * away - 1, 2 * away + 2), HALF)
    low = (HALF - furthest) // 16 * 16
    high = jnp.minimum((HALF + nearest) // 16 * 16, GRID - WINDOW)
    return low, high


def window_rows(boundary):
    low, high = window_starts(boundary)
    lane = iota((1, 2 * WINDOW + MIDDLE), 1)
    off_middle = boundary != 0
    below = jnp.where(off_middle & (low + lane < HALF), low + lane, -1)
    above = high + lane - WINDOW
    above = jnp.where(off_middle & (above >= HALF), above, -1)
    middle = jnp.where(off_middle, -1, HALF - MIDDLE // 2 + lane - 2 * WINDOW)
    return jnp.where(lane < WINDOW, below, jnp.where(lane < 2 * WINDOW, above, middle))


def reached_starts(distance):
    away = jnp.abs(distance)
    nearest = jnp.where(away > 1, away, 0)
    furthest = jnp.minimum(2 * away + 2, HALF)
    low = jnp.minimum((HALF - furthest) // 16 * 16, HALF - 32)
    high = jnp.minimum(jnp.maximum((HALF + nearest) // 16 * 16, low + WINDOW), GRID - WINDOW)
    return low, high


def edges_kernel(
    planes, place_ref, mean_ref, comp_ref, mean_top_ref, comp_top_ref, near_ref, far_ref, middle_ref
):
    bottom = place_ref[0] - HALF
    even = place_ref[1] % 2 == 0

    def fill(boundary, mean, comp, out):
        for chan in range(CHANS):
            plane = mean if chan == 0 else comp.at[chan - 1]
            for n, start in enumerate(window_starts(boundary)):
                rows = pl.ds(pl.multiple_of(start, 16), WINDOW)
                out[chan, n * WINDOW : (n + 1) * WINDOW, :] = plane[rows, :]
            if out is far_ref:
                middle_ref[chan] = plane[HALF - MIDDLE // 2 : HALF + MIDDLE // 2, :]

    @pl.when(even)
    def _():
        fill(bottom + planes, mean_top_ref, comp_top_ref, near_ref)
        fill(bottom, mean_ref, comp_ref, far_ref)

    @pl.when(jnp.logical_not(even))
    def _():
        fill(bottom, mean_ref, comp_ref, near_ref)
        fill(bottom + planes, mean_top_ref, comp_top_ref, far_ref)


def stream(step, parts, copies):
    @pl.when(step == 0)
    def _():
        for part in range(parts):
            for copy in copies(part):
                copy.start()

    @pl.when(step < parts)
    def _():
        for copy in copies(step):
            copy.wait()


def columns(rows):
    fill = jnp.zeros((LANES - len(rows), rows[0].shape[1]), f32)
    return jnp.transpose(jnp.concatenate(rows + [fill], axis=0))


def interpolate(rows, weight, turn):
    parts = []
    for at in range(GRID // TILE):
        part = rows[:, at * TILE : (at + 1) * TILE]
        parts.append((1.0 - weight) * part + weight * pltpu.roll(part, turn, 1))
    return jnp.concatenate(parts, axis=1)


def table_kernel(
    sizes, place_ref, mean_hbm, comp_hbm, out_ref, blank_ref,
    mean_ref, comp_ref, mean_sem, comp_sem, order_ref, zero_ref, zero_sem,
):
    planes, slots, blocks, pair = sizes
    step, first = pl.program_id(0), place_ref[0]
    tables = planes // pair

    def copies(part):
        rows = pl.ds(pl.multiple_of(part * pair * GRID, GRID), pair * GRID)
        return (
            pltpu.make_async_copy(mean_hbm.at[rows], mean_ref.at[rows], mean_sem.at[part]),
            pltpu.make_async_copy(comp_hbm.at[:, rows], comp_ref.at[:, rows], comp_sem.at[part]),
        )

    def blanks(plane):
        low, high = reached_starts(first + plane - HALF)
        parts = []
        for n in range((GRID - 2 * WINDOW) // 16):
            start = jnp.where(n * 16 >= low, n * 16 + WINDOW, n * 16)
            start = jnp.where(start >= high, start + WINDOW, start)
            rows = pl.ds(pl.multiple_of(plane * GRID + start, 16), 16)
            parts.append(pltpu.make_async_copy(zero_ref, blank_ref.at[:, rows], zero_sem.at[plane, n]))
        return parts

    @pl.when(step == 0)
    def _():
        zero_ref[...] = jnp.zeros_like(zero_ref)
        order_ref[...] = slot_order(slots, blocks)

    stream(step, tables, copies)
    for at in range(pair):
        for copy in blanks(step * pair + at):
            copy.start()
    order = order_ref[...]
    for chan in range(CHANS):
        pieces = []
        for at in range(pair):
            span = pl.ds(pl.multiple_of((step * pair + at) * GRID, GRID), GRID)
            plane = mean_ref[span, :] if chan == 0 else comp_ref[chan - 1, span, :]
            pieces.append(dot(order, plane).reshape(slots, blocks, GRID))
        out_ref[:, :, chan * GRID : (chan + 1) * GRID] = jnp.concatenate(pieces, axis=1).astype(bf16)

    @pl.when(step == tables - 1)
    def _():
        for plane in range(planes):
            for copy in blanks(plane):
                copy.wait()


def extract_kernel(
    sizes, place_ref, noise_ref, got_hbm, near_hbm, far_hbm, middle_hbm, mean_hbm, comp_hbm, table_hbm,
    out_ref, rows_ref, extra_ref, rows_extra_ref, total_ref, column_ref,
    got_ref, near_ref, far_ref, middle_ref, own_ref, table_ref, edge_sem, table_sem,
    wide_ref, upper_ref, sums_ref,
):
    planes, slots, blocks, chunk, images, peers = sizes
    step, first = pl.program_id(0), place_ref[0]
    count = images // peers
    stride = count * slots + 2 * count + PARAMETERS
    one_plane = pl.ds(0, GRID)
    edges = (
        pltpu.make_async_copy(got_hbm, got_ref, edge_sem.at[0]),
        pltpu.make_async_copy(near_hbm, near_ref, edge_sem.at[1]),
        pltpu.make_async_copy(far_hbm, far_ref, edge_sem.at[2]),
        pltpu.make_async_copy(middle_hbm, middle_ref, edge_sem.at[3]),
        pltpu.make_async_copy(mean_hbm.at[one_plane], own_ref.at[0], edge_sem.at[4]),
        pltpu.make_async_copy(comp_hbm.at[:, one_plane], own_ref.at[pl.ds(1, COMPS)], edge_sem.at[5]),
    )

    def copies(part):
        at = pl.ds(part * chunk, chunk)
        return (pltpu.make_async_copy(table_hbm.at[at], table_ref.at[at], table_sem.at[part]),)

    @pl.when(step == 0)
    def _():
        for copy in edges:
            copy.start()

    @pl.when(step == 0)
    def _():
        for part in range(slots // chunk):
            copies(part)[0].start()
        edges[0].wait()
        for tile in range(GRID // LANES):
            wide_ref[tile] = got_ref[:, tile * LANES : (tile + 1) * LANES].astype(f32)
        for image in range(count):
            span = slice(image * peers, (image + 1) * peers)
            start = stride - PARAMETERS + image
            column_ref[span, :] = wide_ref[0, pl.ds(start, peers, stride=stride), :]
            for odd in range(2):
                start = count * slots + image * 2 + odd
                at = (odd * count + image) * peers
                for tile in range(GRID // LANES):
                    part = wide_ref[tile, pl.ds(start, peers, stride=stride), :]
                    rows_extra_ref[at : at + peers, tile * LANES : (tile + 1) * LANES] = part.astype(bf16)
        sums_ref[...] = jnp.zeros_like(sums_ref)
        for copy in edges[1:]:
            copy.wait()

    @pl.when(step < slots // chunk)
    def _():
        copies(step)[0].wait()

    tilt = column_ref[:, 0:1].astype(i32)
    weight = column_ref[:, 1:2] / 16.0

    @pl.when(step == 0)
    def _():
        at_up, at_low = window_rows(first + planes - HALF), window_rows(first - HALF)
        row = iota((GRID, at_up.shape[1]), 0)
        order = (at_up == (row % blocks) * slots + row // blocks).astype(f32).astype(bf16)
        parts = []
        for odd in range(2):
            pieces = []
            for lane, part in ((at_low, 0), (iota((1, GRID), 1), 1)):
                plane, depth = plane_depth(lane, tilt)
                hit = (plane == first - 1) & (lane >= 0) & (jnp.bitwise_and(lane, 1) == odd)
                depth = depth if part else HALF - depth
                pieces.append(jnp.where(hit, depth, 0).astype(f32) / HALF)
            parts.append(pieces)
        mixing_low = jnp.concatenate([parts[0][0], parts[1][0]], axis=0).astype(bf16)
        mixing_own = jnp.concatenate([parts[0][1], parts[1][1]], axis=0).astype(bf16)
        weight2 = jnp.concatenate([weight, weight], axis=0)
        fill = upper_ref.shape[1] - blocks
        even = place_ref[1] % 2 == 0
        for chan in range(CHANS):
            at = slice(chan * GRID, (chan + 1) * GRID)
            near, far, middle = near_ref[chan], far_ref[chan], middle_ref[chan]
            upper = jnp.concatenate([jnp.where(even, near, far), middle], axis=0)
            upper = dot(order, upper).reshape(slots, blocks, GRID)
            if fill:
                upper = jnp.concatenate([upper, jnp.zeros((slots, fill, GRID), f32)], axis=1)
            upper_ref[:, :, at] = upper.astype(bf16)
            lower = jnp.concatenate([jnp.where(even, far, near), middle], axis=0)
            blended = dot(mixing_low, lower) + dot(mixing_own, own_ref[chan])
            blended = blended.astype(bf16).astype(f32)
            extra_ref[:, at] = interpolate(blended, weight2, TILE - 1).astype(bf16)

    lane = iota((images, planes * blocks + upper_ref.shape[1]), 1)
    block_at, plane_at = lane % blocks, lane // blocks
    plane_at = jnp.where(plane_at > planes, -1000, plane_at) + first
    low_at = jnp.where(plane_at < first + planes, plane_at, -1000)
    high_at = jnp.where(plane_at > first, plane_at - 1, -1000)
    base = (block_at * slots - HALF) * tilt
    for at in range(chunk):
        slot = step * chunk + at
        for image in range(count):
            span = slice(image * peers, (image + 1) * peers)
            for tile in range(GRID // LANES):
                part = wide_ref[tile, pl.ds(image * slots + slot, peers, stride=stride), :]
                rows_ref[at, span, tile * LANES : (tile + 1) * LANES] = part.astype(bf16)
        numerator = base + slot * tilt
        plane, depth = jnp.right_shift(numerator, 7) + HALF, jnp.bitwise_and(numerator, HALF - 1)
        mixing = jnp.where(plane == low_at, HALF - depth, jnp.where(plane == high_at, depth, 0))
        mixing = (mixing.astype(f32) * (1.0 / HALF)).astype(bf16)
        for chan in range(CHANS):
            span = slice(chan * GRID, (chan + 1) * GRID)
            right = jnp.concatenate([table_ref[slot, :, span], upper_ref[slot, :, span]], axis=0)
            part = dot(mixing, right).astype(bf16).astype(f32)
            part = interpolate(part, weight, TILE - 1).astype(bf16)
            out_ref[at, chan * images : (chan + 1) * images, :] = part
    gram_sums(chunk, images, out_ref, rows_ref, sums_ref)

    @pl.when(step == pl.num_programs(0) - 1)
    def _():
        row, lane = iota((images, LANES), 0), iota((images, LANES), 1)
        total = own_products(images, sums_ref)
        for image in range(count):
            mine = (lane == NOISE_AT) & (row == image * peers + place_ref[1])
            total = jnp.where(mine, noise_ref[image], total)
        total_ref[...] = total


def gram_sums(chunk, images, out_ref, rows_ref, sums_ref):
    for group in range(images // 16):
        start = group * 16
        slots = []
        for at in range(chunk):
            rows = [out_ref[at, chan * images + start : chan * images + start + 16, :] for chan in range(CHANS)]
            rows.append(rows_ref[at, start : start + 16, :])
            slots.append(jnp.concatenate(rows, axis=0))
        block = jnp.concatenate(slots, axis=1)
        product = lax.dot_general(block, block, (((1,), (1,)), ((), ())), preferred_element_type=f32)
        sums_ref[group] = sums_ref[group] + product


def own_products(images, sums_ref):
    parts = []
    for group in range(images // 16):
        row, lane = iota((16, LANES), 0), iota((16, LANES), 1)
        total = jnp.zeros((16, LANES), f32)
        for n, (k, l) in enumerate(PAIRS):
            block = sums_ref[group, k * 16 : (k + 1) * 16, :]
            value = jnp.sum(jnp.where(lane == row + l * 16, block, 0.0), axis=1, keepdims=True)
            total = jnp.where(lane == n, value, total)
        parts.append(total)
    return jnp.concatenate(parts, axis=0)


def solve_rows(table, noise):
    count = float(GRID * GRID)

    def gram(k, l):
        at = PAIRS.index((min(k, l), max(k, l)))
        return table[at : at + 1, :]

    factor = [[None] * COMPS for _ in range(COMPS)]
    inverse = [None] * COMPS
    for col in range(COMPS):
        for row in range(col, COMPS):
            total = gram(row + 1, col + 1) / count
            if row == col:
                total = total + noise
            for at in range(col):
                total = total - factor[row][at] * factor[col][at]
            if row == col:
                inverse[col] = 1.0 / jnp.sqrt(total)
            else:
                factor[row][col] = total * inverse[col]
    forward = []
    for row in range(COMPS):
        total = (gram(row + 1, CHANS) - gram(row + 1, 0)) / count
        for col in range(row):
            total = total - factor[row][col] * forward[col]
        forward.append(total * inverse[row])
    latent = [None] * COMPS
    for row in reversed(range(COMPS)):
        total = forward[row]
        for col in range(row + 1, COMPS):
            total = total - factor[col][row] * latent[col]
        latent[row] = total * inverse[row]
    return latent


def back_kernel(
    sizes, place_ref, part_ref, other_ref, column_ref,
    slice_ref, rows_ref, slice_extra_ref, rows_extra_ref, _,
    out_ref, latent_ref, reached_ref, reached_sem, stack_ref, row_ref, power_ref, tilt_ref, col_ref, free_ref, spill_ref, order_ref,
    depth_ref, share_at_ref, share_ref, combine_ref,
):
    planes, slots, blocks, chunk, images, steps, out_planes = sizes
    step, first = pl.program_id(0), place_ref[0]
    group = 2 if blocks % 16 else 1

    @pl.when(step == 0)
    def _():
        table = jnp.transpose(part_ref[...] + other_ref[...])
        values = jnp.transpose(column_ref[...])
        tilt, frac = values[0:1, :], values[1:2, :]
        latent = solve_rows(table, table[NOISE_AT : NOISE_AT + 1, :])
        free_ref[...] = columns(latent)
        count = latent_ref.shape[0]
        for image in range(count):
            at = image * (images // count) + place_ref[1]
            latent_ref[image : image + 1, :] = free_ref[pl.ds(at, 1), :COMPS]
        rounded = [value.astype(bf16).astype(f32) for value in latent]
        power = rounded[0] * rounded[0]
        for value in rounded[1:]:
            power = power + value * value
        rows = jnp.concatenate(rounded + [power, power], axis=0)
        row_ref[...] = jnp.concatenate([rows, rows, rows], axis=1).astype(bf16)
        power_ref[...] = jnp.concatenate([power, power], axis=1)
        tilt_ref[...] = jnp.concatenate([tilt, tilt, tilt], axis=1).astype(i32)
        col_ref[...] = columns(rounded + [power, tilt, frac])
        one = jnp.ones((1, images), f32)
        same = iota((images, images), 0) == iota((images, images), 1)
        parts = [jnp.where(same, value, 0.0) for value in [one] + rounded]
        combine_ref[...] = jnp.concatenate(parts, axis=1).astype(bf16)
        col = iota((WINDOW, GRID), 1)
        order_ref[...] = (col % blocks) * slots + col // blocks - iota((WINDOW, GRID), 0)

    def spread(total, rows, weight):
        residual = rows.astype(f32) - total
        return interpolate(residual.astype(bf16).astype(f32), weight, 1)

    weight = col_ref[:, COMPS + 2 : COMPS + 3] / 16.0

    @pl.when(step == 0)
    def _():
        latent = jnp.concatenate([col_ref[...]] * 2, axis=0)
        total = slice_extra_ref[:, :GRID].astype(f32)
        for k in range(COMPS):
            span = slice((k + 1) * GRID, (k + 2) * GRID)
            total = total + latent[:, k : k + 1] * slice_extra_ref[:, span].astype(f32)
        value = spread(total, rows_extra_ref[...], jnp.concatenate([weight, weight], axis=0))
        tilt = col_ref[:, COMPS + 1 : COMPS + 2].astype(i32)
        plane, depth = plane_depth(iota((images, GRID), 1), tilt)
        odd = jnp.bitwise_and(iota((images, GRID), 1), 1)
        for at in range(2):
            hit = (plane == first - 1) & (odd == at)
            part = jnp.sum(jnp.where(hit, depth, 0).astype(f32), axis=1, keepdims=True) / HALF
            span = slice(at * images, (at + 1) * images)
            spill_ref[span, :] = (part * value[span]).astype(bf16)
        slot_at = iota((images, LANES), 1)
        depths = jnp.zeros((images, LANES), f32)
        for block in range(blocks):
            plane, depth = plane_depth(block * slots + slot_at, tilt)
            live = (plane >= first) & (plane < first + planes)
            depths = depths + jnp.where(live, depth, 0).astype(f32)
        depth_ref[...] = depths / HALF
        shape = (GRID, 2 * images)
        low = iota(shape, 1) < images
        plane, depth = plane_depth(iota(shape, 0), tilt_ref[:, : 2 * images])
        share_at_ref[...] = jnp.where(low, plane, plane + 1)
        share_ref[...] = jnp.where(low, HALF - depth, depth).astype(f32) / HALF * power_ref[:, : 2 * images]

    @pl.when(step < steps)
    def _():
        tilt = tilt_ref[...]
        row = iota((blocks, 3 * images), 0)
        base = (row * slots - HALF) * tilt
        shape = (planes, blocks, 3 * images)
        plane_at, lane = iota(shape, 0), iota(shape, 2)
        wanted = jnp.where(lane < images, plane_at, plane_at - 1)
        wanted = jnp.where((lane < 2 * images) == (wanted < 0), -1000, wanted) + (first - HALF)
        depths = pltpu.roll(depth_ref[...], (LANES - step * chunk) % LANES, 1)
        rights, hits = [], []
        for at in range(chunk):
            slot = step * chunk + at
            value = spread(dot(combine_ref[...], slice_ref[slot]), rows_ref[at], weight)
            depth = depths[:, at : at + 1]
            odd = pl.ds(pl.multiple_of((slot % 2) * images, 16), images)
            low, high = ((1.0 - depth) * value).astype(bf16), (depth * value).astype(bf16)
            rights.append(jnp.concatenate([low, high, spill_ref[odd, :]], axis=0))
            plane = jnp.right_shift(base + slot * tilt, 7)
            hit = jnp.where(plane[None] == wanted, 1.0, 0.0)
            hits.append(hit.reshape(planes * blocks, 3 * images).astype(bf16))
        for start in range(0, chunk, group):
            pieces = [[] for _ in range(COMPS)]
            for at in range(start, start + group):
                left = jnp.concatenate([hits[at] * row_ref[k : k + 1, :] for k in range(COMPS)], axis=0)
                totals = dot(left, rights[at])
                for k in range(COMPS):
                    total = totals[k * planes * blocks : (k + 1) * planes * blocks]
                    pieces[k].append(total.reshape(planes, blocks, GRID))
            rows = pl.ds(pl.multiple_of((step * chunk + start) * blocks, 16), group * blocks)
            for k in range(COMPS):
                stack_ref[k, :, rows, :] = jnp.concatenate(pieces[k], axis=1).astype(bf16)

    def stores(plane):
        copies = []
        for n, start in enumerate(reached_starts(first + plane - HALF)):
            rows = pl.ds(pl.multiple_of(plane * GRID + start, 16), WINDOW)
            part = reached_ref.at[plane, :, pl.ds(n * WINDOW, WINDOW)]
            copies.append(pltpu.make_async_copy(part, out_ref.at[:, rows], reached_sem.at[2 * plane + n]))
        return copies

    @pl.when(step >= steps)
    def _():
        for at in range(out_planes):
            plane = (step - steps) * out_planes + at
            orders, shares = [], []
            for start in reached_starts(first + plane - HALF):
                rows = pl.ds(pl.multiple_of(start, 16), WINDOW)
                orders.append(jnp.where(order_ref[...] == start, 1.0, 0.0))
                shares.append(jnp.where(share_at_ref[rows, :] == first + plane, share_ref[rows, :], 0.0))
            order = jnp.concatenate(orders, axis=0).astype(bf16)
            share = jnp.concatenate(shares, axis=0)
            scale = 1.0 / (1.0 + jnp.sum(share, axis=1, keepdims=True))
            for k in range(COMPS):
                reached_ref[plane, k] = (dot(order, stack_ref[k, plane]) * scale).astype(bf16)
            for copy in stores(plane):
                copy.start()

    @pl.when(step == pl.num_programs(0) - 1)
    def _():
        for plane in range(planes):
            for copy in stores(plane):
                copy.wait()


def whole(shape):
    return pl.BlockSpec(shape, lambda *_: (0,) * len(shape))


def anywhere():
    return pl.BlockSpec(memory_space=pl.ANY)


def in_hbm(value):
    return pltpu.with_memory_space_constraint(value, pltpu.HBM)


def hbm():
    return pl.BlockSpec(memory_space=pltpu.HBM)


def smem():
    return pl.BlockSpec(memory_space=pltpu.SMEM)


def local(mean_volume, components, images, tilt, shift, frac, noise_var):
    peers = lax.axis_size("slab")
    me = lax.axis_index("slab")
    planes = mean_volume.shape[0] // GRID
    slots = 2 * planes
    blocks = GRID // slots
    count = images.shape[0]
    total = peers * count
    width = CHANS * GRID
    chunk = max(1, 1024 // total)
    steps = slots // chunk
    pack_rows = count * slots + 2 * count + PARAMETERS
    place = jnp.stack([me * planes, me]).astype(i32)

    packed = pl.pallas_call(
        functools.partial(pack_kernel, (planes, slots, peers, count)),
        out_shape=jax.ShapeDtypeStruct((peers, pack_rows, GRID), bf16),
        in_specs=[smem(), smem(), smem(), whole((count * GRID, GRID))],
        out_specs=whole((peers, pack_rows, GRID)),
        scratch_shapes=[pltpu.VMEM((count * GRID, GRID), bf16)],
        grid=(1,),
        compiler_params=params(56),
        name="pack",
    )(tilt, shift, frac, images.reshape(count * GRID, GRID))
    got = lax.all_to_all(packed, "slab", split_axis=0, concat_axis=0, tiled=True)

    wide = 2 * WINDOW
    top = planes - 1
    edge_rows = (wide, wide, MIDDLE)
    near, far, middle = pl.pallas_call(
        functools.partial(edges_kernel, planes),
        out_shape=[jax.ShapeDtypeStruct((CHANS, rows, GRID), bf16) for rows in edge_rows],
        grid=(1,),
        in_specs=[
            smem(),
            pl.BlockSpec((GRID, GRID), lambda n: (0, 0)),
            pl.BlockSpec((COMPS, GRID, GRID), lambda n: (0, 0, 0)),
            pl.BlockSpec((GRID, GRID), lambda n: (top, 0)),
            pl.BlockSpec((COMPS, GRID, GRID), lambda n: (0, top, 0)),
        ],
        out_specs=[whole((CHANS, rows, GRID)) for rows in edge_rows],
        compiler_params=params(56),
        name="edges",
    )(place, mean_volume, components, mean_volume, components)
    half = peers // 2
    pairs = [(n, n + 1 if n % 2 else n - 1) for n in range(1, peers - 1) if n not in (half - 1, half)]
    middle = lax.ppermute(middle, "slab", [(half - 1, half), (half, half - 1)])
    near = lax.ppermute(near, "slab", [(n, n ^ 1) for n in range(peers)])
    far = lax.ppermute(far, "slab", pairs)

    pair = 2 if blocks % 16 else 1
    tables = planes // pair
    table, blank = pl.pallas_call(
        functools.partial(table_kernel, (planes, slots, blocks, pair)),
        out_shape=[
            pltpu.HBM((slots, planes * blocks, width), bf16),
            jax.ShapeDtypeStruct((COMPS, planes * GRID, GRID), bf16),
        ],
        grid=(tables,),
        in_specs=[smem(), anywhere(), anywhere()],
        out_specs=[
            pl.BlockSpec((slots, pair * blocks, width), lambda n: (0, n, 0)),
            anywhere(),
        ],
        scratch_shapes=[
            pltpu.VMEM((planes * GRID, GRID), bf16),
            pltpu.VMEM((COMPS, planes * GRID, GRID), bf16),
            pltpu.SemaphoreType.DMA((tables,)),
            pltpu.SemaphoreType.DMA((tables,)),
            pltpu.VMEM((GRID, GRID), bf16),
            pltpu.VMEM((COMPS, 16, GRID), bf16),
            pltpu.SemaphoreType.DMA((planes, (GRID - wide) // 16)),
        ],
        compiler_params=params(30),
        name="table",
    )(place, mean_volume, components)

    slices, rows, slices_extra, rows_extra, partial, columns_all = pl.pallas_call(
        functools.partial(extract_kernel, (planes, slots, blocks, chunk, total, peers)),
        out_shape=[
            jax.ShapeDtypeStruct((slots, CHANS * total, GRID), bf16),
            jax.ShapeDtypeStruct((slots, total, GRID), bf16),
            jax.ShapeDtypeStruct((2 * total, width), bf16),
            jax.ShapeDtypeStruct((2 * total, GRID), bf16),
            jax.ShapeDtypeStruct((total, LANES), f32),
            jax.ShapeDtypeStruct((total, LANES), f32),
        ],
        grid=(steps,),
        in_specs=[smem(), smem()] + [hbm()] * 7,
        out_specs=[
            pl.BlockSpec((chunk, CHANS * total, GRID), lambda n: (n, 0, 0)),
            pl.BlockSpec((chunk, total, GRID), lambda n: (n, 0, 0)),
            whole((2 * total, width)),
            whole((2 * total, GRID)),
            whole((total, LANES)),
            whole((total, LANES)),
        ],
        scratch_shapes=[
            pltpu.VMEM((peers * pack_rows, GRID), bf16),
            pltpu.VMEM((CHANS, wide, GRID), bf16),
            pltpu.VMEM((CHANS, wide, GRID), bf16),
            pltpu.VMEM((CHANS, MIDDLE, GRID), bf16),
            pltpu.VMEM((CHANS, GRID, GRID), bf16),
            pltpu.VMEM((slots, planes * blocks, width), bf16),
            pltpu.SemaphoreType.DMA((6,)),
            pltpu.SemaphoreType.DMA((steps,)),
            pltpu.VMEM((GRID // LANES, peers * pack_rows, LANES), f32),
            pltpu.VMEM((slots, -(-blocks // 16) * 16, width), bf16),
            pltpu.VMEM((total // 16, LANES, LANES), f32),
        ],
        compiler_params=params(40),
        name="extract",
    )(
        place,
        noise_var,
        in_hbm(got.reshape(peers * pack_rows, GRID)),
        in_hbm(near),
        in_hbm(far),
        in_hbm(middle),
        in_hbm(mean_volume),
        in_hbm(components),
        in_hbm(table),
    )

    step = 1
    while step < peers // 2:
        partial = partial + lax.ppermute(partial, "slab", [(n, n ^ step) for n in range(peers)])
        step *= 2
    halves = partial, lax.ppermute(partial, "slab", [(n, n ^ step) for n in range(peers)])

    out_planes = min(16, planes)
    last = steps - 1
    new_components, latents = pl.pallas_call(
        functools.partial(back_kernel, (planes, slots, blocks, chunk, total, steps, out_planes)),
        out_shape=[
            jax.ShapeDtypeStruct((COMPS, planes * GRID, GRID), bf16),
            jax.ShapeDtypeStruct((count, COMPS), f32),
        ],
        grid=(steps + planes // out_planes,),
        in_specs=[
            smem(),
            whole((total, LANES)),
            whole((total, LANES)),
            whole((total, LANES)),
            pl.BlockSpec(memory_space=pltpu.VMEM),
            pl.BlockSpec((chunk, total, GRID), lambda n: (jnp.minimum(n, last), 0, 0)),
            whole((2 * total, width)),
            whole((2 * total, GRID)),
            anywhere(),
        ],
        out_specs=[
            anywhere(),
            whole((count, COMPS)),
        ],
        scratch_shapes=[
            pltpu.VMEM((planes, COMPS, 2 * WINDOW, GRID), bf16),
            pltpu.SemaphoreType.DMA((2 * planes,)),
            pltpu.VMEM((COMPS, planes, GRID, GRID), bf16),
            pltpu.VMEM((8, 3 * total), bf16),
            pltpu.VMEM((1, 2 * total), f32),
            pltpu.VMEM((1, 3 * total), i32),
            pltpu.VMEM((total, LANES), f32),
            pltpu.VMEM((total, LANES), f32),
            pltpu.VMEM((2 * total, GRID), bf16),
            pltpu.VMEM((WINDOW, GRID), i32),
            pltpu.VMEM((total, LANES), f32),
            pltpu.VMEM((GRID, 2 * total), i32),
            pltpu.VMEM((GRID, 2 * total), f32),
            pltpu.VMEM((total, CHANS * total), bf16),
        ],
        input_output_aliases={8: 0},
        compiler_params=params(29),
        name="back",
    )(place, *halves, columns_all, pltpu.with_memory_space_constraint(slices, pltpu.VMEM), rows, slices_extra, rows_extra, blank)
    return new_components, latents


def solution(mesh):
    placed = (
        P(("groups", "slab"), None),
        P(None, ("groups", "slab"), None),
        P(("groups", "slab"), None, None),
        P(("groups", "slab")),
        P(("groups", "slab")),
        P(("groups", "slab")),
        P(("groups", "slab")),
    )
    return jax.shard_map(
        local,
        mesh=mesh,
        in_specs=placed,
        out_specs=(P(None, ("groups", "slab"), None), P(("groups", "slab"), None)),
        check_vma=False,
    )
```

```python
import functools

import jax
import jax.numpy as jnp
from jax import lax
from jax.experimental import pallas as pl
from jax.experimental.pallas import tpu as pltpu
from jax.sharding import PartitionSpec as P

GRID = 256
HALF = GRID // 2
COMPS = 6
CHANS = COMPS + 1
TILE = 128
LANES = 128
PAIRS = [(k, l) for k in range(CHANS) for l in range(k, CHANS + 1)]
NOISE_AT = len(PAIRS)

f32 = jnp.float32
bf16 = jnp.bfloat16
i32 = jnp.int32


def iota(shape, dim):
    return lax.broadcasted_iota(i32, shape, dim)


def dot(a, b):
    return jnp.dot(a, b, preferred_element_type=f32)


def params(mebibytes):
    return pltpu.CompilerParams(vmem_limit_bytes=mebibytes * 1024 * 1024)


def plane_depth(position, tilt):
    numerator = (position - HALF) * tilt
    return jnp.right_shift(numerator, 7) + HALF, jnp.bitwise_and(numerator, HALF - 1)


PARAMETERS = 8


def pack_kernel(sizes, tilt_ref, shift_ref, frac_ref, image_ref, out_ref, turned_ref):
    planes, slots, peers, count = sizes
    main_rows = count * slots
    shape = (peers * slots, GRID)
    row, col = iota(shape, 0), iota(shape, 1)
    slot_hit = jnp.bitwise_and(row - col, slots - 1) == 0
    first_hit = jnp.where(slot_hit, row // slots * planes, -1)
    for image in range(count):
        rows = slice(image * GRID, (image + 1) * GRID)
        for at in range(GRID // TILE):
            span = slice(at * TILE, (at + 1) * TILE)
            part = image_ref[rows, span].astype(f32)
            turned_ref[rows, span] = pltpu.roll(part, shift_ref[image], 1).astype(bf16)
        plane, _ = plane_depth(iota((1, GRID), 1), tilt_ref[image])
        hit = jnp.bitwise_and(plane, -planes) == first_hit
        found = dot(jnp.where(hit, 1.0, 0.0).astype(bf16), turned_ref[rows, :])
        found = found.reshape(peers, slots, GRID).astype(bf16)
        out_ref[:, image * slots : (image + 1) * slots, :] = found
    lane = iota((1, count * GRID), 1)
    tilt = jnp.full((1, count * GRID), tilt_ref[0], i32)
    for image in range(1, count):
        tilt = jnp.where(lane >= image * GRID, tilt_ref[image], tilt)
    plane, _ = plane_depth(jnp.bitwise_and(lane, GRID - 1), tilt)
    shape = (peers * 2 * count, count * GRID)
    row, col = iota(shape, 0), iota(shape, 1)
    hit = (row // 2 % count == col // GRID) & (row % 2 == col % 2)
    hit = hit & (plane == row // (2 * count) * planes - 1)
    found = dot(jnp.where(hit, 1.0, 0.0).astype(bf16), turned_ref[...])
    found = found.reshape(peers, 2 * count, GRID)
    row, lane = iota((PARAMETERS, GRID), 0), iota((PARAMETERS, GRID), 1)
    values = jnp.zeros((PARAMETERS, GRID), f32)
    for image in range(count):
        value = jnp.where(lane == 0, tilt_ref[image], jnp.where(lane == 1, frac_ref[image], 0))
        values = jnp.where(row == image, value.astype(f32), values)
    values = jnp.broadcast_to(values[None], (peers, PARAMETERS, GRID))
    out_ref[:, main_rows:, :] = jnp.concatenate([found, values], axis=1).astype(bf16)


def slot_order(slots, blocks):
    row, col = iota((GRID, GRID), 0), iota((GRID, GRID), 1)
    return (col == (row % blocks) * slots + row // blocks).astype(f32).astype(bf16)


WINDOW = 80
MIDDLE = 32


def window_starts(boundary):
    away = jnp.abs(boundary)
    nearest = jnp.where(boundary > 0, away - 1, away)
    furthest = jnp.minimum(jnp.where(boundary > 0, 2 * away - 1, 2 * away + 2), HALF)
    low = (HALF - furthest) // 16 * 16
    high = jnp.minimum((HALF + nearest) // 16 * 16, GRID - WINDOW)
    return low, high


def window_rows(boundary):
    low, high = window_starts(boundary)
    lane = iota((1, 2 * WINDOW + MIDDLE), 1)
    off_middle = boundary != 0
    below = jnp.where(off_middle & (low + lane < HALF), low + lane, -1)
    above = high + lane - WINDOW
    above = jnp.where(off_middle & (above >= HALF), above, -1)
    middle = jnp.where(off_middle, -1, HALF - MIDDLE // 2 + lane - 2 * WINDOW)
    return jnp.where(lane < WINDOW, below, jnp.where(lane < 2 * WINDOW, above, middle))


def reached_starts(distance):
    away = jnp.abs(distance)
    nearest = jnp.where(away > 1, away, 0)
    furthest = jnp.minimum(2 * away + 2, HALF)
    low = jnp.minimum((HALF - furthest) // 16 * 16, HALF - 32)
    high = jnp.minimum(jnp.maximum((HALF + nearest) // 16 * 16, low + WINDOW), GRID - WINDOW)
    return low, high


def edges_kernel(
    planes, place_ref, mean_ref, comp_ref, mean_top_ref, comp_top_ref, near_ref, far_ref, middle_ref
):
    bottom = place_ref[0] - HALF
    even = place_ref[1] % 2 == 0

    def fill(boundary, mean, comp, out):
        for chan in range(CHANS):
            plane = mean if chan == 0 else comp.at[chan - 1]
            for n, start in enumerate(window_starts(boundary)):
                rows = pl.ds(pl.multiple_of(start, 16), WINDOW)
                out[chan, n * WINDOW : (n + 1) * WINDOW, :] = plane[rows, :]
            if out is far_ref:
                middle_ref[chan] = plane[HALF - MIDDLE // 2 : HALF + MIDDLE // 2, :]

    @pl.when(even)
    def _():
        fill(bottom + planes, mean_top_ref, comp_top_ref, near_ref)
        fill(bottom, mean_ref, comp_ref, far_ref)

    @pl.when(jnp.logical_not(even))
    def _():
        fill(bottom, mean_ref, comp_ref, near_ref)
        fill(bottom + planes, mean_top_ref, comp_top_ref, far_ref)


def stream(step, parts, copies):
    @pl.when(step == 0)
    def _():
        for part in range(parts):
            for copy in copies(part):
                copy.start()

    @pl.when(step < parts)
    def _():
        for copy in copies(step):
            copy.wait()


def columns(rows):
    fill = jnp.zeros((LANES - len(rows), rows[0].shape[1]), f32)
    return jnp.transpose(jnp.concatenate(rows + [fill], axis=0))


def interpolate(rows, weight, turn):
    parts = []
    for at in range(GRID // TILE):
        part = rows[:, at * TILE : (at + 1) * TILE]
        parts.append((1.0 - weight) * part + weight * pltpu.roll(part, turn, 1))
    return jnp.concatenate(parts, axis=1)


def table_kernel(
    sizes, place_ref, mean_hbm, comp_hbm, out_ref, blank_ref,
    mean_ref, comp_ref, mean_sem, comp_sem, order_ref, zero_ref, zero_sem,
):
    planes, slots, blocks, pair = sizes
    step, first = pl.program_id(0), place_ref[0]
    tables = planes // pair

    def copies(part):
        rows = pl.ds(pl.multiple_of(part * pair * GRID, GRID), pair * GRID)
        return (
            pltpu.make_async_copy(mean_hbm.at[rows], mean_ref.at[rows], mean_sem.at[part]),
            pltpu.make_async_copy(comp_hbm.at[:, rows], comp_ref.at[:, rows], comp_sem.at[part]),
        )

    def blanks(plane):
        low, high = reached_starts(first + plane - HALF)
        parts = []
        for n in range((GRID - 2 * WINDOW) // 16):
            start = jnp.where(n * 16 >= low, n * 16 + WINDOW, n * 16)
            start = jnp.where(start >= high, start + WINDOW, start)
            rows = pl.ds(pl.multiple_of(plane * GRID + start, 16), 16)
            parts.append(pltpu.make_async_copy(zero_ref, blank_ref.at[:, rows], zero_sem.at[plane, n]))
        return parts

    @pl.when(step == 0)
    def _():
        zero_ref[...] = jnp.zeros_like(zero_ref)
        order_ref[...] = slot_order(slots, blocks)

    stream(step, tables, copies)
    for at in range(pair):
        for copy in blanks(step * pair + at):
            copy.start()
    order = order_ref[...]
    for chan in range(CHANS):
        pieces = []
        for at in range(pair):
            span = pl.ds(pl.multiple_of((step * pair + at) * GRID, GRID), GRID)
            plane = mean_ref[span, :] if chan == 0 else comp_ref[chan - 1, span, :]
            pieces.append(dot(order, plane).reshape(slots, blocks, GRID))
        out_ref[:, :, chan * GRID : (chan + 1) * GRID] = jnp.concatenate(pieces, axis=1).astype(bf16)

    @pl.when(step == tables - 1)
    def _():
        for plane in range(planes):
            for copy in blanks(plane):
                copy.wait()


def extract_kernel(
    sizes, place_ref, noise_ref, got_ref, near_hbm, far_hbm, middle_hbm, mean_hbm, comp_hbm, table_hbm,
    out_ref, rows_ref, extra_ref, rows_extra_ref, total_ref, column_ref,
    near_ref, far_ref, middle_ref, own_ref, table_ref, edge_sem, table_sem,
    wide_ref, upper_ref, sums_ref,
):
    planes, slots, blocks, chunk, images, peers = sizes
    step, first = pl.program_id(0), place_ref[0]
    count = images // peers
    stride = count * slots + 2 * count + PARAMETERS
    one_plane = pl.ds(0, GRID)
    edges = (
        pltpu.make_async_copy(near_hbm, near_ref, edge_sem.at[0]),
        pltpu.make_async_copy(far_hbm, far_ref, edge_sem.at[1]),
        pltpu.make_async_copy(middle_hbm, middle_ref, edge_sem.at[2]),
        pltpu.make_async_copy(mean_hbm.at[one_plane], own_ref.at[0], edge_sem.at[3]),
        pltpu.make_async_copy(comp_hbm.at[:, one_plane], own_ref.at[pl.ds(1, COMPS)], edge_sem.at[4]),
    )

    def copies(part):
        at = pl.ds(part * chunk, chunk)
        return (pltpu.make_async_copy(table_hbm.at[at], table_ref.at[at], table_sem.at[part]),)

    @pl.when(step == 0)
    def _():
        for copy in edges:
            copy.start()

    @pl.when(step == 0)
    def _():
        for part in range(slots // chunk):
            copies(part)[0].start()
        for tile in range(GRID // LANES):
            wide_ref[tile] = got_ref[:, tile * LANES : (tile + 1) * LANES].astype(f32)
        for image in range(count):
            span = slice(image * peers, (image + 1) * peers)
            start = stride - PARAMETERS + image
            column_ref[span, :] = wide_ref[0, pl.ds(start, peers, stride=stride), :]
            for odd in range(2):
                start = count * slots + image * 2 + odd
                at = (odd * count + image) * peers
                for tile in range(GRID // LANES):
                    part = wide_ref[tile, pl.ds(start, peers, stride=stride), :]
                    rows_extra_ref[at : at + peers, tile * LANES : (tile + 1) * LANES] = part.astype(bf16)
        sums_ref[...] = jnp.zeros_like(sums_ref)
        for copy in edges:
            copy.wait()

    @pl.when(step < slots // chunk)
    def _():
        copies(step)[0].wait()

    tilt = column_ref[:, 0:1].astype(i32)
    weight = column_ref[:, 1:2] / 16.0

    @pl.when(step == 0)
    def _():
        at_up, at_low = window_rows(first + planes - HALF), window_rows(first - HALF)
        row = iota((GRID, at_up.shape[1]), 0)
        order = (at_up == (row % blocks) * slots + row // blocks).astype(f32).astype(bf16)
        parts = []
        for odd in range(2):
            pieces = []
            for lane, part in ((at_low, 0), (iota((1, GRID), 1), 1)):
                plane, depth = plane_depth(lane, tilt)
                hit = (plane == first - 1) & (lane >= 0) & (jnp.bitwise_and(lane, 1) == odd)
                depth = depth if part else HALF - depth
                pieces.append(jnp.where(hit, depth, 0).astype(f32) / HALF)
            parts.append(pieces)
        mixing_low = jnp.concatenate([parts[0][0], parts[1][0]], axis=0).astype(bf16)
        mixing_own = jnp.concatenate([parts[0][1], parts[1][1]], axis=0).astype(bf16)
        weight2 = jnp.concatenate([weight, weight], axis=0)
        fill = upper_ref.shape[1] - blocks
        even = place_ref[1] % 2 == 0
        for chan in range(CHANS):
            at = slice(chan * GRID, (chan + 1) * GRID)
            near, far, middle = near_ref[chan], far_ref[chan], middle_ref[chan]
            upper = jnp.concatenate([jnp.where(even, near, far), middle], axis=0)
            upper = dot(order, upper).reshape(slots, blocks, GRID)
            if fill:
                upper = jnp.concatenate([upper, jnp.zeros((slots, fill, GRID), f32)], axis=1)
            upper_ref[:, :, at] = upper.astype(bf16)
            lower = jnp.concatenate([jnp.where(even, far, near), middle], axis=0)
            blended = dot(mixing_low, lower) + dot(mixing_own, own_ref[chan])
            blended = blended.astype(bf16).astype(f32)
            extra_ref[:, at] = interpolate(blended, weight2, TILE - 1).astype(bf16)

    lane = iota((images, planes * blocks + upper_ref.shape[1]), 1)
    block_at, plane_at = lane % blocks, lane // blocks
    plane_at = jnp.where(plane_at > planes, -1000, plane_at) + first
    low_at = jnp.where(plane_at < first + planes, plane_at, -1000)
    high_at = jnp.where(plane_at > first, plane_at - 1, -1000)
    base = (block_at * slots - HALF) * tilt
    for at in range(chunk):
        slot = step * chunk + at
        for image in range(count):
            span = slice(image * peers, (image + 1) * peers)
            for tile in range(GRID // LANES):
                part = wide_ref[tile, pl.ds(image * slots + slot, peers, stride=stride), :]
                rows_ref[at, span, tile * LANES : (tile + 1) * LANES] = part.astype(bf16)
        numerator = base + slot * tilt
        plane, depth = jnp.right_shift(numerator, 7) + HALF, jnp.bitwise_and(numerator, HALF - 1)
        mixing = jnp.where(plane == low_at, HALF - depth, jnp.where(plane == high_at, depth, 0))
        mixing = (mixing.astype(f32) * (1.0 / HALF)).astype(bf16)
        for chan in range(CHANS):
            span = slice(chan * GRID, (chan + 1) * GRID)
            right = jnp.concatenate([table_ref[slot, :, span], upper_ref[slot, :, span]], axis=0)
            part = dot(mixing, right).astype(bf16).astype(f32)
            part = interpolate(part, weight, TILE - 1).astype(bf16)
            out_ref[at, chan * images : (chan + 1) * images, :] = part
    gram_sums(chunk, images, out_ref, rows_ref, sums_ref)

    @pl.when(step == pl.num_programs(0) - 1)
    def _():
        row, lane = iota((images, LANES), 0), iota((images, LANES), 1)
        total = own_products(images, sums_ref)
        for image in range(count):
            mine = (lane == NOISE_AT) & (row == image * peers + place_ref[1])
            total = jnp.where(mine, noise_ref[image], total)
        total_ref[...] = total


def gram_sums(chunk, images, out_ref, rows_ref, sums_ref):
    for group in range(images // 16):
        start = group * 16
        slots = []
        for at in range(chunk):
            rows = [out_ref[at, chan * images + start : chan * images + start + 16, :] for chan in range(CHANS)]
            rows.append(rows_ref[at, start : start + 16, :])
            slots.append(jnp.concatenate(rows, axis=0))
        block = jnp.concatenate(slots, axis=1)
        product = lax.dot_general(block, block, (((1,), (1,)), ((), ())), preferred_element_type=f32)
        sums_ref[group] = sums_ref[group] + product


def own_products(images, sums_ref):
    parts = []
    for group in range(images // 16):
        row, lane = iota((16, LANES), 0), iota((16, LANES), 1)
        total = jnp.zeros((16, LANES), f32)
        for n, (k, l) in enumerate(PAIRS):
            block = sums_ref[group, k * 16 : (k + 1) * 16, :]
            value = jnp.sum(jnp.where(lane == row + l * 16, block, 0.0), axis=1, keepdims=True)
            total = jnp.where(lane == n, value, total)
        parts.append(total)
    return jnp.concatenate(parts, axis=0)


def solve_rows(table, noise):
    count = float(GRID * GRID)

    def gram(k, l):
        at = PAIRS.index((min(k, l), max(k, l)))
        return table[at : at + 1, :]

    factor = [[None] * COMPS for _ in range(COMPS)]
    inverse = [None] * COMPS
    for col in range(COMPS):
        for row in range(col, COMPS):
            total = gram(row + 1, col + 1) / count
            if row == col:
                total = total + noise
            for at in range(col):
                total = total - factor[row][at] * factor[col][at]
            if row == col:
                inverse[col] = 1.0 / jnp.sqrt(total)
            else:
                factor[row][col] = total * inverse[col]
    forward = []
    for row in range(COMPS):
        total = (gram(row + 1, CHANS) - gram(row + 1, 0)) / count
        for col in range(row):
            total = total - factor[row][col] * forward[col]
        forward.append(total * inverse[row])
    latent = [None] * COMPS
    for row in reversed(range(COMPS)):
        total = forward[row]
        for col in range(row + 1, COMPS):
            total = total - factor[col][row] * latent[col]
        latent[row] = total * inverse[row]
    return latent


def back_kernel(
    sizes, place_ref, part_ref, other_ref, column_ref,
    slice_ref, rows_ref, slice_extra_ref, rows_extra_ref, _,
    out_ref, latent_ref, reached_ref, reached_sem, stack_ref, row_ref, power_ref, tilt_ref, col_ref, free_ref, spill_ref, order_ref,
    depth_ref, share_at_ref, share_ref, combine_ref,
):
    planes, slots, blocks, chunk, images, steps, out_planes = sizes
    step, first = pl.program_id(0), place_ref[0]
    group = 2 if blocks % 16 else 1

    @pl.when(step == 0)
    def _():
        table = jnp.transpose(part_ref[...] + other_ref[...])
        values = jnp.transpose(column_ref[...])
        tilt, frac = values[0:1, :], values[1:2, :]
        latent = solve_rows(table, table[NOISE_AT : NOISE_AT + 1, :])
        free_ref[...] = columns(latent)
        count = latent_ref.shape[0]
        for image in range(count):
            at = image * (images // count) + place_ref[1]
            latent_ref[image : image + 1, :] = free_ref[pl.ds(at, 1), :COMPS]
        rounded = [value.astype(bf16).astype(f32) for value in latent]
        power = rounded[0] * rounded[0]
        for value in rounded[1:]:
            power = power + value * value
        rows = jnp.concatenate(rounded + [power, power], axis=0)
        row_ref[...] = jnp.concatenate([rows, rows, rows], axis=1).astype(bf16)
        power_ref[...] = jnp.concatenate([power, power], axis=1)
        tilt_ref[...] = jnp.concatenate([tilt, tilt, tilt], axis=1).astype(i32)
        col_ref[...] = columns(rounded + [power, tilt, frac])
        one = jnp.ones((1, images), f32)
        same = iota((images, images), 0) == iota((images, images), 1)
        parts = [jnp.where(same, value, 0.0) for value in [one] + rounded]
        combine_ref[...] = jnp.concatenate(parts, axis=1).astype(bf16)
        col = iota((WINDOW, GRID), 1)
        order_ref[...] = (col % blocks) * slots + col // blocks - iota((WINDOW, GRID), 0)

    def spread(total, rows, weight):
        residual = rows.astype(f32) - total
        return interpolate(residual.astype(bf16).astype(f32), weight, 1)

    weight = col_ref[:, COMPS + 2 : COMPS + 3] / 16.0

    @pl.when(step == 0)
    def _():
        latent = jnp.concatenate([col_ref[...]] * 2, axis=0)
        total = slice_extra_ref[:, :GRID].astype(f32)
        for k in range(COMPS):
            span = slice((k + 1) * GRID, (k + 2) * GRID)
            total = total + latent[:, k : k + 1] * slice_extra_ref[:, span].astype(f32)
        value = spread(total, rows_extra_ref[...], jnp.concatenate([weight, weight], axis=0))
        tilt = col_ref[:, COMPS + 1 : COMPS + 2].astype(i32)
        plane, depth = plane_depth(iota((images, GRID), 1), tilt)
        odd = jnp.bitwise_and(iota((images, GRID), 1), 1)
        for at in range(2):
            hit = (plane == first - 1) & (odd == at)
            part = jnp.sum(jnp.where(hit, depth, 0).astype(f32), axis=1, keepdims=True) / HALF
            span = slice(at * images, (at + 1) * images)
            spill_ref[span, :] = (part * value[span]).astype(bf16)
        slot_at = iota((images, LANES), 1)
        depths = jnp.zeros((images, LANES), f32)
        for block in range(blocks):
            plane, depth = plane_depth(block * slots + slot_at, tilt)
            live = (plane >= first) & (plane < first + planes)
            depths = depths + jnp.where(live, depth, 0).astype(f32)
        depth_ref[...] = depths / HALF
        shape = (GRID, 2 * images)
        low = iota(shape, 1) < images
        plane, depth = plane_depth(iota(shape, 0), tilt_ref[:, : 2 * images])
        share_at_ref[...] = jnp.where(low, plane, plane + 1)
        share_ref[...] = jnp.where(low, HALF - depth, depth).astype(f32) / HALF * power_ref[:, : 2 * images]

    @pl.when(step < steps)
    def _():
        tilt = tilt_ref[...]
        row = iota((blocks, 3 * images), 0)
        base = (row * slots - HALF) * tilt
        shape = (planes, blocks, 3 * images)
        plane_at, lane = iota(shape, 0), iota(shape, 2)
        wanted = jnp.where(lane < images, plane_at, plane_at - 1)
        wanted = jnp.where((lane < 2 * images) == (wanted < 0), -1000, wanted) + (first - HALF)
        depths = pltpu.roll(depth_ref[...], (LANES - step * chunk) % LANES, 1)
        rights, hits = [], []
        for at in range(chunk):
            slot = step * chunk + at
            value = spread(dot(combine_ref[...], slice_ref[slot]), rows_ref[at], weight)
            depth = depths[:, at : at + 1]
            odd = pl.ds(pl.multiple_of((slot % 2) * images, 16), images)
            low, high = ((1.0 - depth) * value).astype(bf16), (depth * value).astype(bf16)
            rights.append(jnp.concatenate([low, high, spill_ref[odd, :]], axis=0))
            plane = jnp.right_shift(base + slot * tilt, 7)
            hit = jnp.where(plane[None] == wanted, 1.0, 0.0)
            hits.append(hit.reshape(planes * blocks, 3 * images).astype(bf16))
        for start in range(0, chunk, group):
            pieces = [[] for _ in range(COMPS)]
            for at in range(start, start + group):
                left = jnp.concatenate([hits[at] * row_ref[k : k + 1, :] for k in range(COMPS)], axis=0)
                totals = dot(left, rights[at])
                for k in range(COMPS):
                    total = totals[k * planes * blocks : (k + 1) * planes * blocks]
                    pieces[k].append(total.reshape(planes, blocks, GRID))
            rows = pl.ds(pl.multiple_of((step * chunk + start) * blocks, 16), group * blocks)
            for k in range(COMPS):
                stack_ref[k, :, rows, :] = jnp.concatenate(pieces[k], axis=1).astype(bf16)

    def stores(plane):
        copies = []
        for n, start in enumerate(reached_starts(first + plane - HALF)):
            rows = pl.ds(pl.multiple_of(plane * GRID + start, 16), WINDOW)
            part = reached_ref.at[plane, :, pl.ds(n * WINDOW, WINDOW)]
            copies.append(pltpu.make_async_copy(part, out_ref.at[:, rows], reached_sem.at[2 * plane + n]))
        return copies

    @pl.when(step >= steps)
    def _():
        for at in range(out_planes):
            plane = (step - steps) * out_planes + at
            orders, shares = [], []
            for start in reached_starts(first + plane - HALF):
                rows = pl.ds(pl.multiple_of(start, 16), WINDOW)
                orders.append(jnp.where(order_ref[...] == start, 1.0, 0.0))
                shares.append(jnp.where(share_at_ref[rows, :] == first + plane, share_ref[rows, :], 0.0))
            order = jnp.concatenate(orders, axis=0).astype(bf16)
            share = jnp.concatenate(shares, axis=0)
            scale = 1.0 / (1.0 + jnp.sum(share, axis=1, keepdims=True))
            for k in range(COMPS):
                reached_ref[plane, k] = (dot(order, stack_ref[k, plane]) * scale).astype(bf16)
            for copy in stores(plane):
                copy.start()

    @pl.when(step == pl.num_programs(0) - 1)
    def _():
        for plane in range(planes):
            for copy in stores(plane):
                copy.wait()


def whole(shape):
    return pl.BlockSpec(shape, lambda *_: (0,) * len(shape))


def anywhere():
    return pl.BlockSpec(memory_space=pl.ANY)


def in_vmem(value):
    return pltpu.with_memory_space_constraint(value, pltpu.VMEM)


def in_hbm(value):
    return pltpu.with_memory_space_constraint(value, pltpu.HBM)


def hbm():
    return pl.BlockSpec(memory_space=pltpu.HBM)


def smem():
    return pl.BlockSpec(memory_space=pltpu.SMEM)


def local(mean_volume, components, images, tilt, shift, frac, noise_var):
    peers = lax.axis_size("slab")
    me = lax.axis_index("slab")
    planes = mean_volume.shape[0] // GRID
    slots = 2 * planes
    blocks = GRID // slots
    count = images.shape[0]
    total = peers * count
    width = CHANS * GRID
    chunk = max(1, 1024 // total)
    steps = slots // chunk
    pack_rows = count * slots + 2 * count + PARAMETERS
    place = jnp.stack([me * planes, me]).astype(i32)

    packed = pl.pallas_call(
        functools.partial(pack_kernel, (planes, slots, peers, count)),
        out_shape=jax.ShapeDtypeStruct((peers, pack_rows, GRID), bf16),
        in_specs=[smem(), smem(), smem(), whole((count * GRID, GRID))],
        out_specs=whole((peers, pack_rows, GRID)),
        scratch_shapes=[pltpu.VMEM((count * GRID, GRID), bf16)],
        grid=(1,),
        compiler_params=params(56),
        name="pack",
    )(tilt, shift, frac, images.reshape(count * GRID, GRID))
    got = lax.all_to_all(packed, "slab", split_axis=0, concat_axis=0, tiled=True)

    wide = 2 * WINDOW
    top = planes - 1
    edge_rows = (wide, wide, MIDDLE)
    near, far, middle = pl.pallas_call(
        functools.partial(edges_kernel, planes),
        out_shape=[jax.ShapeDtypeStruct((CHANS, rows, GRID), bf16) for rows in edge_rows],
        grid=(1,),
        in_specs=[
            smem(),
            pl.BlockSpec((GRID, GRID), lambda n: (0, 0)),
            pl.BlockSpec((COMPS, GRID, GRID), lambda n: (0, 0, 0)),
            pl.BlockSpec((GRID, GRID), lambda n: (top, 0)),
            pl.BlockSpec((COMPS, GRID, GRID), lambda n: (0, top, 0)),
        ],
        out_specs=[whole((CHANS, rows, GRID)) for rows in edge_rows],
        compiler_params=params(56),
        name="edges",
    )(place, mean_volume, components, mean_volume, components)
    half = peers // 2
    pairs = [(n, n + 1 if n % 2 else n - 1) for n in range(1, peers - 1) if n not in (half - 1, half)]
    middle = lax.ppermute(middle, "slab", [(half - 1, half), (half, half - 1)])
    near = lax.ppermute(near, "slab", [(n, n ^ 1) for n in range(peers)])
    far = lax.ppermute(far, "slab", pairs)

    pair = 2 if blocks % 16 else 1
    tables = planes // pair
    table, blank = pl.pallas_call(
        functools.partial(table_kernel, (planes, slots, blocks, pair)),
        out_shape=[
            pltpu.HBM((slots, planes * blocks, width), bf16),
            jax.ShapeDtypeStruct((COMPS, planes * GRID, GRID), bf16),
        ],
        grid=(tables,),
        in_specs=[smem(), anywhere(), anywhere()],
        out_specs=[
            pl.BlockSpec((slots, pair * blocks, width), lambda n: (0, n, 0)),
            anywhere(),
        ],
        scratch_shapes=[
            pltpu.VMEM((planes * GRID, GRID), bf16),
            pltpu.VMEM((COMPS, planes * GRID, GRID), bf16),
            pltpu.SemaphoreType.DMA((tables,)),
            pltpu.SemaphoreType.DMA((tables,)),
            pltpu.VMEM((GRID, GRID), bf16),
            pltpu.VMEM((COMPS, 16, GRID), bf16),
            pltpu.SemaphoreType.DMA((planes, (GRID - wide) // 16)),
        ],
        compiler_params=params(52),
        name="table",
    )(place, mean_volume, components)

    slices, rows, slices_extra, rows_extra, partial, columns_all = pl.pallas_call(
        functools.partial(extract_kernel, (planes, slots, blocks, chunk, total, peers)),
        out_shape=[
            jax.ShapeDtypeStruct((slots, CHANS * total, GRID), bf16),
            jax.ShapeDtypeStruct((slots, total, GRID), bf16),
            jax.ShapeDtypeStruct((2 * total, width), bf16),
            jax.ShapeDtypeStruct((2 * total, GRID), bf16),
            jax.ShapeDtypeStruct((total, LANES), f32),
            jax.ShapeDtypeStruct((total, LANES), f32),
        ],
        grid=(steps,),
        in_specs=[smem(), smem(), pl.BlockSpec(memory_space=pltpu.VMEM)] + [hbm()] * 6,
        out_specs=[
            pl.BlockSpec((chunk, CHANS * total, GRID), lambda n: (n, 0, 0)),
            pl.BlockSpec((chunk, total, GRID), lambda n: (n, 0, 0)),
            whole((2 * total, width)),
            whole((2 * total, GRID)),
            whole((total, LANES)),
            whole((total, LANES)),
        ],
        scratch_shapes=[
            pltpu.VMEM((CHANS, wide, GRID), bf16),
            pltpu.VMEM((CHANS, wide, GRID), bf16),
            pltpu.VMEM((CHANS, MIDDLE, GRID), bf16),
            pltpu.VMEM((CHANS, GRID, GRID), bf16),
            pltpu.VMEM((slots, planes * blocks, width), bf16),
            pltpu.SemaphoreType.DMA((5,)),
            pltpu.SemaphoreType.DMA((steps,)),
            pltpu.VMEM((GRID // LANES, peers * pack_rows, LANES), f32),
            pltpu.VMEM((slots, -(-blocks // 16) * 16, width), bf16),
            pltpu.VMEM((total // 16, LANES, LANES), f32),
        ],
        compiler_params=params(40),
        name="extract",
    )(
        place,
        noise_var,
        in_vmem(got.reshape(peers * pack_rows, GRID)),
        in_hbm(near),
        in_hbm(far),
        in_hbm(middle),
        in_hbm(mean_volume),
        in_hbm(components),
        in_hbm(table),
    )

    step = 1
    while step < peers // 2:
        partial = partial + lax.ppermute(partial, "slab", [(n, n ^ step) for n in range(peers)])
        step *= 2
    halves = partial, lax.ppermute(partial, "slab", [(n, n ^ step) for n in range(peers)])

    out_planes = min(16, planes)
    last = steps - 1
    new_components, latents = pl.pallas_call(
        functools.partial(back_kernel, (planes, slots, blocks, chunk, total, steps, out_planes)),
        out_shape=[
            jax.ShapeDtypeStruct((COMPS, planes * GRID, GRID), bf16),
            jax.ShapeDtypeStruct((count, COMPS), f32),
        ],
        grid=(steps + planes // out_planes,),
        in_specs=[
            smem(),
            whole((total, LANES)),
            whole((total, LANES)),
            whole((total, LANES)),
            pl.BlockSpec(memory_space=pltpu.VMEM),
            pl.BlockSpec((chunk, total, GRID), lambda n: (jnp.minimum(n, last), 0, 0)),
            whole((2 * total, width)),
            whole((2 * total, GRID)),
            anywhere(),
        ],
        out_specs=[
            anywhere(),
            whole((count, COMPS)),
        ],
        scratch_shapes=[
            pltpu.VMEM((planes, COMPS, 2 * WINDOW, GRID), bf16),
            pltpu.SemaphoreType.DMA((2 * planes,)),
            pltpu.VMEM((COMPS, planes, GRID, GRID), bf16),
            pltpu.VMEM((8, 3 * total), bf16),
            pltpu.VMEM((1, 2 * total), f32),
            pltpu.VMEM((1, 3 * total), i32),
            pltpu.VMEM((total, LANES), f32),
            pltpu.VMEM((total, LANES), f32),
            pltpu.VMEM((2 * total, GRID), bf16),
            pltpu.VMEM((WINDOW, GRID), i32),
            pltpu.VMEM((total, LANES), f32),
            pltpu.VMEM((GRID, 2 * total), i32),
            pltpu.VMEM((GRID, 2 * total), f32),
            pltpu.VMEM((total, CHANS * total), bf16),
        ],
        input_output_aliases={8: 0},
        compiler_params=params(29),
        name="back",
    )(place, *halves, columns_all, pltpu.with_memory_space_constraint(slices, pltpu.VMEM), rows, slices_extra, rows_extra, blank)
    return new_components, latents


def solution(mesh):
    placed = (
        P(("groups", "slab"), None),
        P(None, ("groups", "slab"), None),
        P(("groups", "slab"), None, None),
        P(("groups", "slab")),
        P(("groups", "slab")),
        P(("groups", "slab")),
        P(("groups", "slab")),
    )
    return jax.shard_map(
        local,
        mesh=mesh,
        in_specs=placed,
        out_specs=(P(None, ("groups", "slab"), None), P(("groups", "slab"), None)),
        check_vma=False,
    )
```
